128 devices in a mesh: tp: 8 (over z_hi, y), dec: 16 (over x, z_lo, core).
Axes of the slice: x: 4, y: 4, z: 4 (z_hi: 2, z_lo: 2; z = z_hi * 2 + z_lo), core: 2. Of those that a mesh axis runs over, the one named last changes fastest.
Arguments:
- queries: bfloat16 [16, 768, 8192], P('dec', None, 'tp'), may hold values from -30 to 30
- span_kv: bfloat16 [16, 768, 2048], P('dec', None, 'tp'), may hold values from -6 to 6
- page_pool: bfloat16 [1024, 128, 2048], P(('tp', 'dec')), may hold values from -6 to 6
- cache_slot: int32 [16, 128, 1], P('dec'), may hold values from 0 to 7
- cache_live: int32 [16, 128, 1], P('dec'), may hold values from 0 to 1, as said below
- span_dest: int32 [16, 6], P('dec'), may hold values from 0 to 15, as said below
Outputs:
- attn_out: bfloat16 [16, 768, 8192], P('dec', None, 'tp')
- decode_pages: bfloat16 [256, 128, 2048], P(('tp', 'dec'))
The draws below stay inside these ranges and needn't reach their ends.
Inputs may be any that keep to these rules, and one draw needn't show every extreme that they name: `cache_slot`: entries with cache_live 0 are unused. Slots may be shared by several prompts. `cache_live`: each prompt has at most 32 live entries, and some prompt exactly 32; each prompt has some decode device with all 1 of its entries live. `span_dest`: the pages of one prompt go to distinct decode columns.
All inputs are finite; a program needn't handle non-finite values.
Results may differ from the reference program's by a relative error of at most 0.0028.
Values may be sent and summed in bfloat16 or wider, within the bound.
A program may use at most 128 MiB of HBM per device.

```python
import math
import jax
import jax.numpy as jnp
from jax import lax

QH = 64
KVH = 8
HD = 128
PAGE = 128
TOK = 768
CTXP = 32
POOL = 8
CAP = 1
NEWP = 6
SLOTS = 2
N_DEC = 16
DEVICES = 128


def draw_queries(key, part):
    key = jax.random.fold_in(key, 1)
    base = jnp.clip(2.5 * jax.random.normal(key, (N_DEC, TOK, QH * HD), jnp.float32), -15.0, 15.0)
    return base.astype(jnp.bfloat16)


def draw_span_kv(key, part):
    key = jax.random.fold_in(key, 2)
    base = jnp.clip(jax.random.normal(key, (N_DEC, TOK, KVH, 2, HD), jnp.float32), -6.0, 6.0)
    return base.reshape(N_DEC, TOK, KVH * 2 * HD).astype(jnp.bfloat16)


def shuffled_slots(key):
    return jax.random.permutation(key, DEVICES * CAP).astype(jnp.int32)


def draw_cache_live(key, part):
    key = jax.random.fold_in(key, 3)
    keys = jax.random.split(key, 4)
    slot_total = DEVICES * CAP
    order = jax.vmap(shuffled_slots)(jax.random.split(keys[0], N_DEC))
    favored = jax.random.randint(keys[1], (N_DEC, 1), 0, DEVICES)
    slot_ids = jnp.arange(slot_total, dtype=jnp.int32)[None, :]
    order = jnp.where(slot_ids // CAP == favored, slot_ids % CAP - CAP, order)
    position = jnp.argsort(jnp.argsort(order, axis=1, stable=True), axis=1, stable=True)
    wanted = CTXP - jax.random.randint(keys[2], (N_DEC,), 0, CTXP // 8 + 1)
    fullest = jax.random.randint(keys[3], (), 0, N_DEC)
    wanted = jnp.where(jnp.arange(N_DEC) == fullest, CTXP, wanted)
    live_flags = (position < wanted[:, None]).astype(jnp.int32)
    return live_flags.reshape(N_DEC, DEVICES, CAP)


def column_order(key):
    return jax.random.permutation(key, N_DEC).astype(jnp.int32)


def draw_span_dest(key, part):
    key = jax.random.fold_in(key, 4)
    orders = jax.vmap(column_order)(jax.random.split(key, N_DEC))
    return orders[:, :NEWP]


def set_ends(drawn, stream_key, low, largest):
    longest = drawn.shape.index(max(drawn.shape))
    spots = []
    for shift in (0, 1):
        where = [jax.random.randint(jax.random.fold_in(stream_key, axis), (), 0, length) for axis, length in enumerate(drawn.shape)]
        where[longest] = (where[longest] + shift) % drawn.shape[longest]
        spots.append(tuple(where))
    return drawn.at[spots[0]].set(low).at[spots[1]].set(largest)


def levels(stream_key, dims, pieces, least, largest):
    factor_of = 1.0
    for dim, shards_of in pieces:
        steps = jax.random.uniform(jax.random.fold_in(jax.random.fold_in(stream_key, 6), dim), (shards_of,), jnp.float32, least / len(pieces), largest / len(pieces))
        factor_of = factor_of * jnp.repeat(jnp.exp(steps), dims[dim] // shards_of).reshape((-1,) + (1,) * (len(dims) - 1 - dim))
    return factor_of


def bell_draw(own_key, extent, width, most, pieces=(), held_as=jnp.bfloat16):
    drawn = width * jax.random.normal(own_key, extent, jnp.float32)
    if pieces:
        drawn = drawn * levels(own_key, extent, pieces, -0.22, 0.18)
    return jnp.clip(drawn, -most, most).astype(held_as)


def setup_inputs(seed: int = 0) -> dict:
    key_of = jax.random.split(jax.random.key(seed), 7)
    return {
        "queries": draw_queries(jax.random.fold_in(key_of[6], 71), 0),
        "span_kv": draw_span_kv(jax.random.fold_in(key_of[6], 71), 0),
        "page_pool": bell_draw(key_of[2], (DEVICES * POOL, PAGE, KVH * 2 * HD), 1.0, 6.0, ((0, 128),)),
        "cache_slot": set_ends(jax.random.randint(key_of[3], (N_DEC, DEVICES, CAP), 0, POOL), jax.random.fold_in(key_of[3], 1), 0, POOL - 1).astype(jnp.int32),
        "cache_live": draw_cache_live(jax.random.fold_in(key_of[6], 71), 0),
        "span_dest": draw_span_dest(jax.random.fold_in(key_of[6], 71), 0),
    }


def compact_slots(live_flags):
    flat_live = live_flags.reshape(-1).astype(jnp.int32)
    live_rank = (jnp.cumsum(flat_live) - 1).astype(jnp.int32)
    slot_ids = jnp.arange(flat_live.shape[0], dtype=jnp.int32)
    targets = jnp.arange(CTXP, dtype=jnp.int32)
    select_table = (flat_live[None, :] == 1) & (live_rank[None, :] == targets[:, None])
    live_index = lax.optimization_barrier(jnp.sum(jnp.where(select_table, slot_ids[None, :], 0), axis=1)).astype(jnp.int32)
    return (live_index, jnp.sum(flat_live).astype(jnp.int32))

def attend(query_block, kv_block, live_count, heads_query, group_size):
    span_rows = query_block.shape[0]
    total_keys = kv_block.shape[0]
    cached_keys = total_keys - span_rows
    score_scale = 1.0 / math.sqrt(HD)
    key_pos = jnp.arange(total_keys, dtype=jnp.int32)[None, :]
    query_pos = jnp.arange(span_rows, dtype=jnp.int32)[:, None]
    visible = jnp.where(key_pos < cached_keys, key_pos < live_count * PAGE, key_pos - cached_keys <= query_pos)

    def one_head(head_index):
        kv_head = head_index // group_size
        query_part = lax.dynamic_slice_in_dim(query_block, head_index * HD, HD, 1)
        key_part = lax.dynamic_slice_in_dim(kv_block, kv_head * 2 * HD, HD, 1)
        value_part = lax.dynamic_slice_in_dim(kv_block, kv_head * 2 * HD + HD, HD, 1)
        scores = lax.dot_general(query_part, key_part, (((1,), (1,)), ((), ())), preferred_element_type=jnp.float32) * score_scale
        scores = jnp.where(visible, scores, -jnp.inf)
        row_max = lax.optimization_barrier(jnp.max(scores, axis=1, keepdims=True))
        weights = jnp.exp(scores - row_max)
        weight_total = lax.optimization_barrier(jnp.sum(weights, axis=1, keepdims=True))
        mixed = jnp.dot(weights.astype(jnp.bfloat16), value_part, preferred_element_type=jnp.float32)
        return (mixed / weight_total).astype(jnp.bfloat16)
    heads_out = lax.map(one_head, jnp.arange(heads_query, dtype=jnp.int32))
    return jnp.transpose(heads_out, (1, 0, 2)).reshape(span_rows, heads_query * HD)

def reference(queries, span_kv, page_pool, cache_slot, cache_live, span_dest):
    group_size = QH // KVH
    outputs = []
    for group_index in range(N_DEC):
        live_index, live_count = compact_slots(cache_live[group_index])
        owners = (live_index // CAP).astype(jnp.int32)
        slot_values = cache_slot[group_index].reshape(-1)[live_index].astype(jnp.int32)
        cached = page_pool[owners * POOL + slot_values]
        kv_block = jnp.concatenate([cached.reshape(CTXP * PAGE, KVH * 2 * HD), span_kv[group_index]], axis=0)
        outputs.append(attend(queries[group_index], kv_block, live_count, QH, group_size))
    attn_out = jnp.stack(outputs)
    decode_pages = jnp.zeros((DEVICES * SLOTS, PAGE, KVH * 2 * HD), jnp.bfloat16)
    for group_index in range(N_DEC):
        new_pages = span_kv[group_index].reshape(NEWP, PAGE, KVH * 2 * HD)
        target_rows = ((group_index // SLOTS * N_DEC + span_dest[group_index]) * SLOTS + group_index % SLOTS).astype(jnp.int32)
        decode_pages = decode_pages.at[target_rows].set(new_pages)
    return (attn_out, decode_pages)
```

```python
import functools
import math

import jax
import jax.numpy as jnp
from jax import lax
from jax.experimental import pallas as pl
from jax.experimental.pallas import tpu as pltpu
from jax.sharding import PartitionSpec as P

HD = 128
PAGE = 128
CTXP = 32
QT = 256
KC = 512
LOG2E = 1.4426950408889634
NEG = -1e30


def compact_slots(live_flags):
    flat_live = live_flags.reshape(-1)
    live_rank = jnp.cumsum(flat_live) - 1
    slot_ids = jnp.arange(flat_live.shape[0], dtype=jnp.int32)
    targets = jnp.arange(CTXP, dtype=jnp.int32)
    select_table = (flat_live[None, :] == 1) & (live_rank[None, :] == targets[:, None])
    live_index = jnp.sum(jnp.where(select_table, slot_ids[None, :], 0), axis=1)
    return (live_index, jnp.sum(flat_live))


def attend_kernel(
    heads, span, index_ref, count_ref, q_ref, span_ref, pages_ref, out_ref, k_ref, v_ref, s_ref, mx_ref, acc_ref, sem
):
    cached = CTXP * PAGE
    tiles = span // QT
    coef = LOG2E / math.sqrt(HD)

    def page_copies(p):
        src = pages_ref.at[index_ref[p]]
        rows = pl.ds(pl.multiple_of(p * PAGE, PAGE), PAGE)
        return (
            pltpu.make_async_copy(src.at[:, pl.ds(0, HD)], k_ref.at[rows], sem.at[0, p]),
            pltpu.make_async_copy(src.at[:, pl.ds(HD, HD)], v_ref.at[rows, pl.ds(0, HD)], sem.at[1, p]),
        )

    @pl.loop(0, CTXP)
    def _(p):
        for copy in page_copies(p):
            copy.start()

    v_ref[:, HD:] = jnp.ones((cached + span, HD), jnp.bfloat16)
    k_ref[cached:, :] = span_ref[:, :HD]
    v_ref[cached:, :HD] = span_ref[:, HD:]

    @pl.loop(0, CTXP)
    def _(p):
        for copy in page_copies(p):
            copy.wait()

    live = count_ref[0]
    full = live // (KC // PAGE)
    rest = live - full * (KC // PAGE)

    def q_tile(h, i):
        return q_ref[pl.ds(i * QT, QT), pl.ds(pl.multiple_of(h * HD, HD), HD)]

    def fold(part, width):
        out = part[:, :HD]
        for c in range(1, width // HD):
            out = jnp.maximum(out, part[:, c * HD : (c + 1) * HD])
        return out

    def score(slot, q, start, width, mask=None):
        part = lax.dot_general(
            q, k_ref[pl.ds(start, width), :], (((1,), (1,)), ((), ())), preferred_element_type=jnp.float32
        )
        if mask is not None:
            part = jnp.where(mask, part, NEG)
        s_ref[slot, :, pl.ds(start, width)] = part
        mx_ref[slot] = jnp.maximum(mx_ref[slot], fold(part, width))

    def mix(slot, top, start, width):
        part = s_ref[slot, :, pl.ds(start, width)]
        weights = [
            jnp.exp2((part[:, c * HD : (c + 1) * HD] - top) * coef).astype(jnp.bfloat16) for c in range(width // HD)
        ]
        acc_ref[...] += jnp.dot(
            jnp.concatenate(weights, axis=1), v_ref[pl.ds(start, width), :], preferred_element_type=jnp.float32
        )

    def rest_mask():
        return lax.broadcasted_iota(jnp.int32, (QT, KC), 1) < rest * PAGE

    def diagonal_mask():
        return lax.broadcasted_iota(jnp.int32, (QT, QT), 1) <= lax.broadcasted_iota(jnp.int32, (QT, QT), 0)

    def step(score_of, mix_of):
        if score_of is not None:
            sh, si, ss = score_of
            q = q_tile(sh, si)
            mx_ref[ss] = jnp.full((QT, HD), NEG, jnp.float32)
        if mix_of is not None:
            mh, mi, ms = mix_of
            top = jnp.broadcast_to(jnp.max(mx_ref[ms], axis=1, keepdims=True), (QT, HD))
            acc_ref[...] = jnp.zeros_like(acc_ref)

        @pl.loop(0, full)
        def _(j):
            start = pl.multiple_of(j * KC, KC)
            if score_of is not None:
                score(ss, q, start, KC)
            if mix_of is not None:
                mix(ms, top, start, KC)

        @pl.when(rest > 0)
        def _():
            start = pl.multiple_of(full * KC, KC)
            if score_of is not None:
                score(ss, q, start, KC, rest_mask())
            if mix_of is not None:
                mix(ms, top, start, KC)

        if score_of is not None:
            for b in range(si):
                score(ss, q, cached + b * QT, QT)
            score(ss, q, cached + si * QT, QT, diagonal_mask())
        if mix_of is not None:
            mix(ms, top, cached, (mi + 1) * QT)
            acc = acc_ref[...]
            out_ref[pl.ds(mi * QT, QT), pl.ds(pl.multiple_of(mh * HD, HD), HD)] = (
                acc[:, :HD] / acc[:, HD:]
            ).astype(out_ref.dtype)

    step((0, 0, 0), None)

    @pl.loop(0, heads // 2)
    def _(hh):
        for n in range(2 * tiles):
            now = (hh * 2 + n // tiles, n % tiles, n % 2)
            m = n + 1
            later = (jnp.minimum(hh * 2 + m // tiles, heads - 1), m % tiles, m % 2)
            step(later, now)


def attend(queries, span_kv, pages, live_index, live_count):
    span, width = queries.shape
    heads = width // HD
    cached = CTXP * PAGE
    vmem = pl.BlockSpec(memory_space=pltpu.VMEM)
    smem = pl.BlockSpec(memory_space=pltpu.SMEM)
    return pl.pallas_call(
        functools.partial(attend_kernel, heads, span),
        out_shape=jax.ShapeDtypeStruct((span, width), jnp.bfloat16),
        in_specs=[smem, smem, vmem, vmem, pl.BlockSpec(memory_space=pl.ANY)],
        out_specs=vmem,
        scratch_shapes=[
            pltpu.VMEM((cached + span, HD), jnp.bfloat16),
            pltpu.VMEM((cached + span, 2 * HD), jnp.bfloat16),
            pltpu.VMEM((2, QT, cached + span), jnp.float32),
            pltpu.VMEM((2, QT, HD), jnp.float32),
            pltpu.VMEM((QT, 2 * HD), jnp.float32),
            pltpu.SemaphoreType.DMA((2, CTXP)),
        ],
        compiler_params=pltpu.CompilerParams(vmem_limit_bytes=48 * 1024 * 1024),
        cost_estimate=pl.CostEstimate(
            flops=4 * span * width * cached, bytes_accessed=8 * 1024 * 1024, transcendentals=span * heads * cached
        ),
    )(live_index, live_count, queries, span_kv, pages)


def body(queries, span_kv, page_pool, cache_slot, cache_live, span_dest):
    tp_size = lax.axis_size("tp")
    dec_size = lax.axis_size("dec")
    devices = tp_size * dec_size
    kv_width = span_kv.shape[2]
    pool_slots = page_pool.shape[0]
    pool_view = page_pool.reshape(pool_slots, PAGE, tp_size, kv_width)
    source_rows = (jnp.arange(devices, dtype=jnp.int32) // dec_size)[:, None]
    requests = cache_slot[0]
    fetched = lax.all_to_all(
        pool_view[
            lax.all_to_all(requests, ("tp", "dec"), split_axis=0, concat_axis=0, tiled=True),
            :,
            source_rows,
        ],
        ("tp", "dec"),
        split_axis=0,
        concat_axis=0,
        tiled=True,
    ).reshape(devices, PAGE, kv_width)
    new_pages = span_kv[0].reshape(-1, PAGE, kv_width)
    chosen = (span_dest[0][None, :] == jnp.arange(dec_size, dtype=jnp.int32)[:, None]).astype(
        jnp.bfloat16
    )
    outgoing = jnp.einsum(
        "dp,pkc->dkc", chosen, new_pages, preferred_element_type=jnp.float32
    ).astype(jnp.bfloat16)
    placed = lax.all_to_all(
        lax.all_to_all(outgoing, "dec", split_axis=0, concat_axis=0, tiled=True),
        "tp",
        split_axis=0,
        concat_axis=2,
        tiled=True,
    )
    live_index, live_count = compact_slots(cache_live[0])
    attn_out = attend(queries[0], span_kv[0], fetched, live_index, live_count.reshape(1))[None]
    return (attn_out, placed)


def solution(mesh):
    in_specs = (
        P("dec", None, "tp"),
        P("dec", None, "tp"),
        P(("tp", "dec"), None, None),
        P("dec", None, None),
        P("dec", None, None),
        P("dec", None),
    )
    out_specs = (P("dec", None, "tp"), P(("tp", "dec"), None, None))
    return jax.shard_map(body, mesh=mesh, in_specs=in_specs, out_specs=out_specs, check_vma=False)
```

```python
import functools
import math

import jax
import jax.numpy as jnp
from jax import lax
from jax.experimental import pallas as pl
from jax.experimental.pallas import tpu as pltpu
from jax.sharding import PartitionSpec as P

HD = 128
PAGE = 128
CTXP = 32
QT = 256
KC = 512
LOG2E = 1.4426950408889634
NEG = -1e30


def compact_slots(live_flags):
    flat_live = live_flags.reshape(-1)
    live_rank = jnp.cumsum(flat_live) - 1
    slot_ids = jnp.arange(flat_live.shape[0], dtype=jnp.int32)
    targets = jnp.arange(CTXP, dtype=jnp.int32)
    select_table = (flat_live[None, :] == 1) & (live_rank[None, :] == targets[:, None])
    live_index = jnp.sum(jnp.where(select_table, slot_ids[None, :], 0), axis=1)
    return (live_index, jnp.sum(flat_live))


MESH = pl.DeviceIdType.MESH
CAP_Y, CAP_Z, CAP_X = 17, 27, 26
LISTS = 16


def coords():
    t, d = lax.axis_index("tp"), lax.axis_index("dec")
    return t, d, t % 4, (t // 4) * 2 + (d // 2) % 2, d // 4, d % 2


def flag(cond, dtype=jnp.float32):
    return jnp.where(cond, 1.0, 0.0).astype(dtype)


def table_kernel(row_ref, tab_ref, all_ref, send_sem, recv_sem):
    t, d, y, z, x, core = coords()
    n = 16
    barrier = pltpu.get_barrier_semaphore()
    for k in range(1, n):
        pl.semaphore_signal(barrier, inc=1, device_id={"dec": (d + k) % n}, device_id_type=MESH)
    pl.semaphore_wait(barrier, n - 1)

    def copy(k, slot):
        return pltpu.make_async_remote_copy(
            src_ref=row_ref,
            dst_ref=all_ref.at[slot],
            send_sem=send_sem.at[k],
            recv_sem=recv_sem.at[slot],
            device_id={"dec": (d + k) % n},
            device_id_type=MESH,
        )

    for k in range(1, n):
        copy(k, d).start()
    all_ref[d] = row_ref[...]

    bf16, f32 = jnp.bfloat16, jnp.float32
    oi = lax.broadcasted_iota(jnp.int32, (128, 128), 0)
    oj = lax.broadcasted_iota(jnp.int32, (128, 128), 1)
    gi = lax.broadcasted_iota(jnp.int32, (16, 16), 0)
    gj = lax.broadcasted_iota(jnp.int32, (16, 16), 1)
    group_z = lambda o: o & 0x4E
    group_x = lambda o: o & 0x0C
    owner_groups = (lambda o: o >> 1, group_z, group_x, lambda o: o & 0)
    asker_groups = (lambda g: g & 0, lambda g: g & 2, lambda g: g & 14, lambda g: g)

    for k in range(1, n):
        copy(k, (d + n - k) % n).wait_recv()
    packed = jnp.concatenate([all_ref[g, 0:1, :] for g in range(n)], axis=0)
    live = packed >= 0
    slot = jnp.maximum(packed, 0)
    flat = flag(live, bf16)

    ranks, counts = [], []
    for owner, asker in zip(owner_groups, asker_groups):
        same = owner(oi) == owner(oj)
        before = jnp.dot(flat, flag(same & (oi < oj), bf16), preferred_element_type=f32)
        total = jnp.dot(flat, flag(same, bf16), preferred_element_type=f32)
        side = asker(gi) == asker(gj)
        rank = jnp.dot(flag(side, bf16), before.astype(bf16), preferred_element_type=f32)
        rank += jnp.dot(flag(side & (gj < gi), bf16), flat, preferred_element_type=f32)
        ranks.append(rank.astype(jnp.int32))
        counts.append(jnp.dot(flag(side, bf16), total.astype(bf16), preferred_element_type=f32).astype(jnp.int32))

    o = lax.broadcasted_iota(jnp.int32, (16, 128), 1)
    g = lax.broadcasted_iota(jnp.int32, (16, 128), 0)
    o_x, o_y, o_z, o_c = (o >> 2) & 3, (o >> 4) & 3, ((o >> 6) << 1) | ((o >> 1) & 1), o & 1
    zlo = z % 2
    mine = (
        live & (o_x == x) & (o_y == y) & (o_z == z),
        live & (o_x == x) & (o_z == z),
        live & (o_x == x) & (((g >> 1) & 1) == zlo),
        live & ((g >> 1) == x * 2 + zlo),
    )
    values = (
        o_c * 8 + slot,
        o_y * CAP_Y + ranks[0],
        o_z * CAP_Z + ranks[1],
        o_x * CAP_X + ranks[2],
    )
    lists = (
        (range(16),),
        [[r for r in range(16) if (r >> 1) & 1 == b] for b in range(2)],
        [[r for r in range(16) if r >> 2 == b] for b in range(4)],
        [[r for r in range(16) if r & 1 == b] for b in range(2)],
    )
    place = lax.broadcasted_iota(jnp.int32, (CTXP, 128), 0)
    lane = lax.broadcasted_iota(jnp.int32, (CTXP, 128), 1)
    table = jnp.zeros((CTXP, 128), jnp.int32)
    column = 0
    for stage in range(4):
        rank = jnp.where(mine[stage], ranks[stage], -1)
        for rows in lists[stage]:
            found = jnp.zeros((CTXP, 128), jnp.int32)
            for r in rows:
                found += jnp.where(rank[r : r + 1, :] == place, values[stage][r : r + 1, :], 0)
            found = jnp.sum(found.astype(f32), axis=1, keepdims=True).astype(jnp.int32)
            table = jnp.where(lane == column, found, table)
            column += 1
    held = jnp.sum(flag(live & (g == d)).astype(f32)).astype(jnp.int32)
    over = jnp.maximum(
        jnp.maximum(jnp.max(counts[0]) - CAP_Y, jnp.max(counts[1]) - CAP_Z), jnp.max(counts[2]) - CAP_X
    )
    for c in range(2):
        size = jnp.sum(flag(live & (g == (d // 2) * 2 + c))).astype(jnp.int32)
        table = jnp.where((lane == 7 + c) & (place >= size), table[0:1, :], table)
    table = jnp.where(lane == 9, held, table)
    table = jnp.where(lane == 10, jnp.maximum(over, 0), table)
    square = jnp.concatenate([table.astype(f32), jnp.zeros((128 - CTXP, 128), f32)], axis=0)
    tab_ref[...] = jnp.transpose(square)[:LISTS, :].astype(jnp.int32)
    for k in range(1, n):
        copy(k, d).wait_send()


def make_table(cache_slot, cache_live):
    row = jnp.where(cache_live[0, :, 0] == 1, cache_slot[0, :, 0], -1)
    row = jnp.broadcast_to(row[None, :], (8, 128))
    vmem = pl.BlockSpec(memory_space=pltpu.VMEM)
    return pl.pallas_call(
        table_kernel,
        out_shape=jax.ShapeDtypeStruct((LISTS, 128), jnp.int32),
        in_specs=[vmem],
        out_specs=vmem,
        scratch_shapes=[
            pltpu.VMEM((16, 8, 128), jnp.int32),
            pltpu.SemaphoreType.DMA((16,)),
            pltpu.SemaphoreType.DMA((16,)),
        ],
        compiler_params=pltpu.CompilerParams(collective_id=0, has_side_effects=True),
    )(row)


NCH = 4
ROWS = 32


class Exchange:
    def __init__(self, tab, pool, span, pages, kv, refs, sems):
        self.tab, self.pool, self.span, self.pages, self.kv = tab, pool, span, pages, kv
        (self.pool16, self.send_y, self.recv_y, self.send_z, self.recv_z, self.send_x, self.recv_x, self.send_c,
         self.span_pad, self.send_d) = refs
        self.sems = sems
        self.t, self.d, self.y, self.z, self.x, self.core = coords()

    def barrier(self):
        t, d = self.t, self.d
        sem = pltpu.get_barrier_semaphore()
        for device in [self.peer("c", 1)] + [self.peer(a, k) for a in "yzx" for k in (1, 2, 3)]:
            pl.semaphore_signal(sem, inc=1, device_id=device, device_id_type=MESH)

        @pl.loop(0, 16)
        def _(n):
            ot, od = n // 2, t * 2 + n % 2

            @pl.when((ot != t) | (od != d))
            def _():
                pl.semaphore_signal(sem, inc=1, device_id={"tp": ot, "dec": od}, device_id_type=MESH)

        pl.semaphore_wait(sem, 26 - jnp.where(d // 2 == t, 1, 0))

    def peer(self, axis, k):
        t, d, y, z, x, c = self.t, self.d, self.y, self.z, self.x, self.core
        if axis == "c":
            c = 1 - c
        elif axis == "y":
            y = (y + k) % 4
        elif axis == "z":
            z = (z + k) % 4
        else:
            x = (x + k) % 4
        return {"tp": (z // 2) * 4 + y, "dec": x * 4 + (z % 2) * 2 + c}

    def remote(self, src, dst, send_sem, recv_sem, device):
        return pltpu.make_async_remote_copy(
            src_ref=src, dst_ref=dst, send_sem=send_sem, recv_sem=recv_sem, device_id=device, device_id_type=MESH
        )

    def pool_own(self, half):
        rows = pl.ds(self.core * 64 + half * ROWS, ROWS)
        return pltpu.make_async_copy(
            self.pool.at[:, rows, :], self.pool16[half].at[pl.ds(self.core * 8, 8)], self.sems["own"].at[half]
        )

    def pool_pair(self, half, into):
        rows = pl.ds((1 - self.core) * 64 + half * ROWS, ROWS)
        return self.remote(
            self.pool.at[:, rows, :],
            self.pool16[half].at[pl.ds(into * 8, 8)],
            self.sems["pair_send"].at[half],
            self.sems["pair_recv"].at[half],
            self.peer("c", 1),
        )

    def start_pool(self):
        for half in range(2):
            self.pool_own(half).start()
            self.pool_pair(half, self.core).start()

    def wait_pool(self, half):
        self.pool_own(half).wait()
        self.pool_pair(half, 1 - self.core).wait_recv()

    def hop(self, axis, ch, k, source):
        send, recv, stage = {
            "y": (self.send_y, self.recv_y, 0), "z": (self.send_z, self.recv_z, 1), "x": (self.send_x, self.recv_x, 2),
        }[axis]
        units = send.shape[2]
        return self.remote(
            send.at[ch, k - 1],
            recv[ch].at[pl.ds(source * units, units)],
            self.sems["send"].at[stage, ch, k - 1],
            self.sems["recv"].at[stage, ch, k - 1],
            self.peer(axis, k),
        )

    def start_hop(self, axis, ch):
        for k in (1, 2, 3):
            self.hop(axis, ch, k, getattr(self, axis)).start()

    def wait_hop(self, axis, ch):
        me = getattr(self, axis)
        for k in (1, 2, 3):
            self.hop(axis, ch, k, (me + 4 - k) % 4).wait_recv()

    def pack_y(self, ch):
        kv, half = ch // 2, ch % 2

        @pl.loop(0, CAP_Y)
        def _(n):
            slot = self.tab[0, n]
            for k in range(4):
                to = (self.y + k) % 4
                for zhi in range(2):
                    col = pl.multiple_of((zhi * 4 + to) * 256 + kv * HD, HD)
                    block = self.pool16[half][slot, :, pl.ds(col, HD)]
                    if k == 0:
                        self.recv_y[ch][self.y * (2 * CAP_Y) + n * 2 + zhi] = block
                    else:
                        self.send_y[ch, k - 1, n * 2 + zhi] = block

        self.start_hop("y", ch)

    def pack_z(self, ch):
        self.wait_hop("y", ch)

        @pl.loop(0, CAP_Z)
        def _(n):
            for k in range(4):
                to = (self.z + k) % 4
                block = self.recv_y[ch][self.tab[1 + to % 2, n] * 2 + to // 2]
                if k == 0:
                    self.recv_z[ch][self.z * CAP_Z + n] = block
                else:
                    self.send_z[ch, k - 1, n] = block

        self.start_hop("z", ch)

    def pack_x(self, ch):
        self.wait_hop("z", ch)

        @pl.loop(0, CAP_X)
        def _(n):
            for k in range(4):
                to = (self.x + k) % 4
                block = self.recv_z[ch][self.tab[3 + to, n]]
                if k == 0:
                    self.recv_x[ch][self.x * CAP_X + n] = block
                else:
                    self.send_x[ch, k - 1, n] = block

        self.start_hop("x", ch)

    def last(self, ch, lane):
        return self.remote(
            self.send_c.at[ch],
            self.kv[ch].at[lane],
            self.sems["last_send"].at[ch],
            self.sems["last_recv"].at[ch],
            self.peer("c", 1),
        )

    def pack_c(self, ch):
        self.wait_hop("x", ch)

        @pl.loop(0, CTXP)
        def _(n):
            rows = pl.ds(pl.multiple_of(n * ROWS, ROWS), ROWS)
            self.kv[ch][self.core, rows, :] = self.recv_x[ch][self.tab[7 + self.core, n]]
            self.send_c[ch, rows, :] = self.recv_x[ch][self.tab[8 - self.core, n]]

        self.last(ch, self.core).start()

    def wait_last(self, ch):
        self.last(ch, 1 - self.core).wait_recv()

    def new_page(self, n, ot, od, half, t):
        cols = pl.ds(pl.multiple_of(t * 256, 256), 256)
        return self.remote(
            self.send_d.at[n],
            self.pages.at[half, :, cols],
            self.sems["new_send"].at[n],
            self.sems["new_recv"].at[half * 8 + t],
            {"tp": ot, "dec": od},
        )

    def own_page(self):
        cols = pl.ds(pl.multiple_of(self.t * 256, 256), 256)
        return pltpu.make_async_copy(
            self.send_d.at[self.d], self.pages.at[self.d % 2, :, cols], self.sems["new_send"].at[self.d]
        )

    def start_new(self, dest):
        self.span_pad[0:6] = self.span[...].reshape(6, PAGE, 256)
        self.span_pad[6] = jnp.zeros((PAGE, 256), jnp.bfloat16)
        ot = self.d // 2

        @pl.loop(0, 16)
        def _(n):
            od = (self.d + n) % 16
            page = jnp.int32(6)
            for p in range(6):
                page = jnp.where(dest[p] == od, p, page)
            self.send_d[od] = self.span_pad[page]
            own = (ot == self.t) & (od == self.d)

            @pl.when(own)
            def _():
                self.own_page().start()

            @pl.when(jnp.logical_not(own))
            def _():
                self.new_page(od, ot, od, self.d % 2, self.t).start()

    def wait_new(self):
        t, d = self.t, self.d

        @pl.loop(0, 16)
        def _(n):
            st, half = n // 2, n % 2
            sd = t * 2 + half
            own = (st == t) & (sd == d)

            @pl.when(own)
            def _():
                self.own_page().wait()

            @pl.when(jnp.logical_not(own))
            def _():
                self.new_page(d, st, sd, half, st).wait_recv()

        @pl.loop(0, 16)
        def _(n):
            @pl.when((d // 2 != t) | (n != d))
            def _():
                self.new_page(n, d // 2, n, d % 2, t).wait_send()

    def wait_sends(self):
        for half in range(2):
            self.pool_pair(half, self.core).wait_send()
        for ch in range(NCH):
            for axis in "yzx":
                for k in (1, 2, 3):
                    self.hop(axis, ch, k, getattr(self, axis)).wait_send()
            self.last(ch, self.core).wait_send()


def exchange_scratch():
    bf16, vmem, dma = jnp.bfloat16, pltpu.VMEM, pltpu.SemaphoreType.DMA
    unit = (ROWS, HD)
    refs = [
        [vmem((16, ROWS, 2048), bf16) for _ in range(2)],
        vmem((NCH, 3, 2 * CAP_Y) + unit, bf16),
        [vmem((8 * CAP_Y,) + unit, bf16) for _ in range(NCH)],
        vmem((NCH, 3, CAP_Z) + unit, bf16),
        [vmem((4 * CAP_Z,) + unit, bf16) for _ in range(NCH)],
        vmem((NCH, 3, CAP_X) + unit, bf16),
        [vmem((4 * CAP_X,) + unit, bf16) for _ in range(NCH)],
        vmem((NCH, CTXP * ROWS, HD), bf16),
        vmem((7, PAGE, 256), bf16),
        vmem((16, PAGE, 256), bf16),
    ]
    sems = {
        "own": dma((2,)), "pair_send": dma((2,)), "pair_recv": dma((2,)), "send": dma((3, NCH, 3)),
        "recv": dma((3, NCH, 3)), "last_send": dma((NCH,)), "last_recv": dma((NCH,)), "new_send": dma((16,)),
        "new_recv": dma((16,)),
    }
    return refs, sems


def exchange_kernel(tab, dest, span, pool, k_out, v_out, pages, kv, refs, sems):
    ex = Exchange(tab, pool, span, pages, kv, refs, sems)
    ex.barrier()
    ex.start_pool()
    ex.start_new(dest)
    ex.wait_pool(0)
    ex.pack_y(0)
    ex.wait_pool(1)
    ex.pack_y(1)
    ex.pack_z(0)
    ex.pack_y(2)
    ex.pack_x(0)
    ex.pack_z(1)
    ex.pack_y(3)
    ex.pack_c(0)
    ex.pack_x(1)
    ex.pack_z(2)
    ex.pack_c(1)
    ex.pack_x(2)
    ex.pack_z(3)
    ex.pack_c(2)
    ex.pack_x(3)
    ex.pack_c(3)
    for ch in range(NCH):
        ex.wait_last(ch)
        out = (k_out, v_out)[ch // 2]
        out[pl.ds((ch % 2) * 2048, 2048), :] = kv[ch][...].reshape(2048, HD)
    ex.wait_new()
    ex.wait_sends()


def exchange(table, dest, span, pool):
    refs, sems = exchange_scratch()
    vmem = pl.BlockSpec(memory_space=pltpu.VMEM)
    smem = pl.BlockSpec(memory_space=pltpu.SMEM)
    hbm = pl.BlockSpec(memory_space=pl.ANY)
    bf16 = jnp.bfloat16
    keys = CTXP * PAGE
    return pl.pallas_call(
        exchange_kernel,
        out_shape=[
            jax.ShapeDtypeStruct((keys, HD), bf16),
            jax.ShapeDtypeStruct((keys, HD), bf16),
            jax.ShapeDtypeStruct((2, PAGE, 2048), bf16),
        ],
        in_specs=[smem, smem, vmem, hbm],
        out_specs=[vmem, vmem, hbm],
        scratch_shapes=[[pltpu.VMEM((2, CTXP * ROWS, HD), bf16) for _ in range(NCH)], refs, sems],
        compiler_params=pltpu.CompilerParams(
            collective_id=1, has_side_effects=True, vmem_limit_bytes=56 * 1024 * 1024
        ),
    )(table, dest, span, pool)


def attend_kernel(heads, span, tab_ref, q_ref, span_ref, k_in, v_in, out_ref, k_ref, v_ref, s_ref, mx_ref, acc_ref):
    cached = CTXP * PAGE
    tiles = span // QT
    coef = LOG2E / math.sqrt(HD)

    live = tab_ref[9, 0]
    k_ref[:cached, :] = k_in[...]
    k_ref[cached:, :] = span_ref[:, :HD]
    used = lax.broadcasted_iota(jnp.int32, (CTXP * 32, HD), 0) < live * 32
    for b in range(4):
        rows = pl.ds(b * CTXP * 32, CTXP * 32)
        v_ref[rows, :HD] = jnp.where(used, v_in[rows, :], 0).astype(jnp.bfloat16)
        v_ref[rows, HD:] = jnp.where(used, 1.0, 0.0).astype(jnp.bfloat16)
    v_ref[cached:, :HD] = span_ref[:, HD:]
    v_ref[cached:, HD:] = jnp.ones((span, HD), jnp.bfloat16)

    def q_tile(h, i):
        return q_ref[pl.ds(i * QT, QT), pl.ds(pl.multiple_of(h * HD, HD), HD)]

    def fold(part, width):
        out = part[:, :HD]
        for c in range(1, width // HD):
            out = jnp.maximum(out, part[:, c * HD : (c + 1) * HD])
        return out

    def score(slot, q, start, width, mask=None):
        part = lax.dot_general(
            q, k_ref[pl.ds(start, width), :], (((1,), (1,)), ((), ())), preferred_element_type=jnp.float32
        )
        if mask is not None:
            part = jnp.where(mask, part, NEG)
        s_ref[slot, :, pl.ds(start, width)] = part
        mx_ref[slot] = jnp.maximum(mx_ref[slot], fold(part, width))

    def mix(slot, top, start, width):
        part = s_ref[slot, :, pl.ds(start, width)]
        weights = [
            jnp.exp2((part[:, c * HD : (c + 1) * HD] - top) * coef).astype(jnp.bfloat16) for c in range(width // HD)
        ]
        acc_ref[...] += jnp.dot(
            jnp.concatenate(weights, axis=1), v_ref[pl.ds(start, width), :], preferred_element_type=jnp.float32
        )

    def diagonal_mask():
        return lax.broadcasted_iota(jnp.int32, (QT, QT), 1) <= lax.broadcasted_iota(jnp.int32, (QT, QT), 0)

    def step(score_of, mix_of):
        if score_of is not None:
            sh, si, ss = score_of
            q = q_tile(sh, si)
            mx_ref[ss] = jnp.full((QT, HD), NEG, jnp.float32)
        if mix_of is not None:
            mh, mi, ms = mix_of
            top = jnp.broadcast_to(jnp.max(mx_ref[ms], axis=1, keepdims=True), (QT, HD))
            acc_ref[...] = jnp.zeros_like(acc_ref)

        @pl.loop(0, cached // KC)
        def _(j):
            start = pl.multiple_of(j * KC, KC)
            if score_of is not None:
                score(ss, q, start, KC)
            if mix_of is not None:
                mix(ms, top, start, KC)

        if score_of is not None:
            for b in range(si):
                score(ss, q, cached + b * QT, QT)
            score(ss, q, cached + si * QT, QT, diagonal_mask())
        if mix_of is not None:
            mix(ms, top, cached, (mi + 1) * QT)
            acc = acc_ref[...]
            out_ref[pl.ds(mi * QT, QT), pl.ds(pl.multiple_of(mh * HD, HD), HD)] = (
                acc[:, :HD] / acc[:, HD:]
            ).astype(out_ref.dtype)

    step((0, 0, 0), None)

    @pl.loop(0, heads // 2)
    def _(hh):
        for n in range(2 * tiles):
            now = (hh * 2 + n // tiles, n % tiles, n % 2)
            m = n + 1
            later = (jnp.minimum(hh * 2 + m // tiles, heads - 1), m % tiles, m % 2)
            step(later, now)


def attend(queries, span_kv, table, keys, values):
    span, width = queries.shape
    heads = width // HD
    cached = CTXP * PAGE
    vmem = pl.BlockSpec(memory_space=pltpu.VMEM)
    smem = pl.BlockSpec(memory_space=pltpu.SMEM)
    return pl.pallas_call(
        functools.partial(attend_kernel, heads, span),
        out_shape=jax.ShapeDtypeStruct((span, width), jnp.bfloat16),
        in_specs=[smem, vmem, vmem, vmem, vmem],
        out_specs=vmem,
        scratch_shapes=[
            pltpu.VMEM((cached + span, HD), jnp.bfloat16),
            pltpu.VMEM((cached + span, 2 * HD), jnp.bfloat16),
            pltpu.VMEM((2, QT, cached + span), jnp.float32),
            pltpu.VMEM((2, QT, HD), jnp.float32),
            pltpu.VMEM((QT, 2 * HD), jnp.float32),
        ],
        compiler_params=pltpu.CompilerParams(vmem_limit_bytes=48 * 1024 * 1024),
        cost_estimate=pl.CostEstimate(
            flops=4 * span * width * cached, bytes_accessed=8 * 1024 * 1024, transcendentals=span * heads * cached
        ),
    )(table, queries, span_kv, keys, values)


def dense_exchange(table, dest, span, pool, slots, flags):
    tp_size, dec_size = lax.axis_size("tp"), lax.axis_size("dec")
    devices = tp_size * dec_size
    width = span.shape[1]
    view = pool.reshape(pool.shape[0], PAGE, tp_size, width)
    source_rows = (jnp.arange(devices, dtype=jnp.int32) // dec_size)[:, None]
    axes = ("tp", "dec")
    asked = lax.all_to_all(slots, axes, split_axis=0, concat_axis=0, tiled=True)
    fetched = lax.all_to_all(view[asked, :, source_rows], axes, split_axis=0, concat_axis=0, tiled=True)
    live_index, live_count = compact_slots(flags)
    live_index = jnp.where(jnp.arange(CTXP) < live_count, live_index, live_index[0])
    cached = fetched.reshape(devices, PAGE, width)[live_index].reshape(CTXP, 2, 2, 32, 2, HD)
    cached = jnp.transpose(cached, (4, 2, 1, 0, 3, 5)).reshape(2, CTXP * PAGE, HD)
    new_pages = span.reshape(-1, PAGE, width)
    chosen = (dest[None, :] == jnp.arange(dec_size, dtype=jnp.int32)[:, None]).astype(jnp.bfloat16)
    outgoing = jnp.einsum("dp,pkc->dkc", chosen, new_pages, preferred_element_type=jnp.float32).astype(jnp.bfloat16)
    placed = lax.all_to_all(outgoing, "dec", split_axis=0, concat_axis=0, tiled=True)
    placed = lax.all_to_all(placed, "tp", split_axis=0, concat_axis=2, tiled=True)
    return (cached[0], cached[1], placed)


def body(queries, span_kv, page_pool, cache_slot, cache_live, span_dest):
    table = make_table(cache_slot, cache_live)
    keys, values, placed = lax.cond(
        table[10, 0] > 0,
        lambda tab, dest, span, pool, slots, flags: dense_exchange(tab, dest, span, pool, slots, flags),
        lambda tab, dest, span, pool, slots, flags: tuple(exchange(tab, dest, span, pool)),
        table, span_dest[0], span_kv[0], page_pool, cache_slot[0], cache_live[0],
    )
    attn_out = attend(queries[0], span_kv[0], table, keys, values)[None]
    return (attn_out, placed)


def solution(mesh):
    in_specs = (
        P("dec", None, "tp"),
        P("dec", None, "tp"),
        P(("tp", "dec"), None, None),
        P("dec", None, None),
        P("dec", None, None),
        P("dec", None),
    )
    out_specs = (P("dec", None, "tp"), P(("tp", "dec"), None, None))
    return jax.shard_map(body, mesh=mesh, in_specs=in_specs, out_specs=out_specs, check_vma=False)
```

```python
import functools
import math

import jax
import jax.numpy as jnp
from jax import lax
from jax.experimental import pallas as pl
from jax.experimental.pallas import tpu as pltpu
from jax.sharding import PartitionSpec as P

HD = 128
PAGE = 128
CTXP = 32
LOG2E = 1.4426950408889634
NEG = -1e30


def compact_slots(live_flags):
    flat_live = live_flags.reshape(-1)
    live_rank = jnp.cumsum(flat_live) - 1
    slot_ids = jnp.arange(flat_live.shape[0], dtype=jnp.int32)
    targets = jnp.arange(CTXP, dtype=jnp.int32)
    select_table = (flat_live[None, :] == 1) & (live_rank[None, :] == targets[:, None])
    live_index = jnp.sum(jnp.where(select_table, slot_ids[None, :], 0), axis=1)
    return (live_index, jnp.sum(flat_live))


MESH = pl.DeviceIdType.MESH
CAP_Y, CAP_Z, CAP_X = 13, 25, 26
LISTS = 16


def coords():
    t, d = lax.axis_index("tp"), lax.axis_index("dec")
    return t, d, t % 4, (t // 4) * 2 + (d // 2) % 2, d // 4, d % 2


def flag(cond, dtype=jnp.float32):
    return jnp.where(cond, 1.0, 0.0).astype(dtype)


def table_kernel(row_ref, tab_ref, all_ref, send_sem, recv_sem):
    t, d, y, z, x, core = coords()
    n = 16
    barrier = pltpu.get_barrier_semaphore()
    for k in range(1, n):
        pl.semaphore_signal(barrier, inc=1, device_id={"dec": (d + k) % n}, device_id_type=MESH)
    pl.semaphore_wait(barrier, n - 1)

    def copy(k, slot):
        return pltpu.make_async_remote_copy(
            src_ref=row_ref,
            dst_ref=all_ref.at[slot],
            send_sem=send_sem.at[k],
            recv_sem=recv_sem.at[slot],
            device_id={"dec": (d + k) % n},
            device_id_type=MESH,
        )

    for k in range(1, n):
        copy(k, d).start()
    all_ref[d] = row_ref[...]

    bf16, f32 = jnp.bfloat16, jnp.float32
    oi = lax.broadcasted_iota(jnp.int32, (128, 128), 0)
    oj = lax.broadcasted_iota(jnp.int32, (128, 128), 1)
    gi = lax.broadcasted_iota(jnp.int32, (16, 16), 0)
    gj = lax.broadcasted_iota(jnp.int32, (16, 16), 1)
    owner_groups = (lambda o: o >> 1, lambda o: o & 0x4E, lambda o: o & 0x0C, lambda o: o & 0)
    row_groups = (lambda g: g & 0, lambda g: g >> 3, lambda g: g & 14, lambda g: g)

    for k in range(1, n):
        copy(k, (d + n - k) % n).wait_recv()
    packed = jnp.concatenate([all_ref[g, 0:1, :] for g in range(n)], axis=0)
    o = lax.broadcasted_iota(jnp.int32, (16, 128), 1)
    g = lax.broadcasted_iota(jnp.int32, (16, 128), 0)
    g_zlo = (g >> 1) & 1
    asked = [
        [jnp.max(flag((packed == s) & (g_zlo == b)), axis=0, keepdims=True) for s in range(8)] for b in range(2)
    ]
    by_slot = [jnp.maximum(p, q) for p, q in zip(*asked)]
    wants = (
        jnp.concatenate(by_slot + [jnp.zeros((8, 128), f32)], axis=0).astype(bf16),
        jnp.concatenate(asked[0] + asked[1], axis=0).astype(bf16),
        flag(packed >= 0, bf16),
        flag(packed >= 0, bf16),
    )

    ranks, counts = [], []
    for want, owner, row in zip(wants, owner_groups, row_groups):
        same = owner(oi) == owner(oj)
        before = jnp.dot(want, flag(same & (oi < oj), bf16), preferred_element_type=f32)
        total = jnp.dot(want, flag(same, bf16), preferred_element_type=f32)
        side = row(gi) == row(gj)
        rank = jnp.dot(flag(side, bf16), before.astype(bf16), preferred_element_type=f32)
        rank += jnp.dot(flag(side & (gj < gi), bf16), want, preferred_element_type=f32)
        ranks.append(rank.astype(jnp.int32))
        counts.append(jnp.dot(flag(side, bf16), total.astype(bf16), preferred_element_type=f32).astype(jnp.int32))

    rank_y = jnp.concatenate([ranks[0][0:8], ranks[0][0:8]], axis=0)
    rank_z = jnp.zeros((16, 128), jnp.int32)
    for s in range(8):
        row = jnp.where(g_zlo == 1, ranks[1][8 + s : 9 + s, :], ranks[1][s : s + 1, :])
        rank_z = jnp.where(packed == s, row, rank_z)

    o_x, o_y, o_z, o_c = (o >> 2) & 3, (o >> 4) & 3, ((o >> 6) << 1) | ((o >> 1) & 1), o & 1
    zlo = z % 2
    places = (
        (o_x == x) & (o_y == y) & (o_z == z),
        (o_x == x) & (o_z == z),
        (o_x == x) & (g_zlo == zlo),
        (g >> 1) == x * 2 + zlo,
    )
    mine = [(want.astype(f32) > 0) & place for want, place in zip(wants, places)]
    values = (
        o_c * 8 + g,
        o_y * CAP_Y + rank_y,
        o_z * CAP_Z + rank_z,
        o_x * CAP_X + ranks[2],
    )
    lists = (
        (range(8),),
        (range(8), range(8, 16)),
        [[r for r in range(16) if r >> 2 == b] for b in range(4)],
        [[r for r in range(16) if r & 1 == b] for b in range(2)],
    )
    place = lax.broadcasted_iota(jnp.int32, (CTXP, 128), 0)
    lane = lax.broadcasted_iota(jnp.int32, (CTXP, 128), 1)
    table = jnp.zeros((CTXP, 128), jnp.int32)
    column = 0
    for stage in range(4):
        rank = jnp.where(mine[stage], ranks[stage], -1)
        for rows in lists[stage]:
            found = jnp.zeros((CTXP, 128), jnp.int32)
            for r in rows:
                found += jnp.where(rank[r : r + 1, :] == place, values[stage][r : r + 1, :], 0)
            found = jnp.sum(found.astype(f32), axis=1, keepdims=True).astype(jnp.int32)
            table = jnp.where(lane == column, found, table)
            column += 1
    live = packed >= 0
    held = jnp.sum(flag(live & (g == d))).astype(jnp.int32)
    over = jnp.maximum(
        jnp.maximum(jnp.max(counts[0]) - CAP_Y, jnp.max(counts[1]) - CAP_Z), jnp.max(counts[2]) - CAP_X
    )
    for c in range(2):
        size = jnp.sum(flag(live & (g == (d // 2) * 2 + c))).astype(jnp.int32)
        table = jnp.where((lane == 7 + c) & (place >= size), table[0:1, :], table)
    table = jnp.where(lane == 9, held, table)
    table = jnp.where(lane == 10, jnp.maximum(over, 0), table)
    square = jnp.concatenate([table.astype(f32), jnp.zeros((128 - CTXP, 128), f32)], axis=0)
    tab_ref[...] = jnp.transpose(square)[:LISTS, :].astype(jnp.int32)
    for k in range(1, n):
        copy(k, d).wait_send()


def make_table(cache_slot, cache_live):
    row = jnp.where(cache_live[0, :, 0] == 1, cache_slot[0, :, 0], -1)
    row = jnp.broadcast_to(row[None, :], (8, 128))
    vmem = pl.BlockSpec(memory_space=pltpu.VMEM)
    return pl.pallas_call(
        table_kernel,
        out_shape=jax.ShapeDtypeStruct((LISTS, 128), jnp.int32),
        in_specs=[vmem],
        out_specs=vmem,
        scratch_shapes=[
            pltpu.VMEM((16, 8, 128), jnp.int32),
            pltpu.SemaphoreType.DMA((16,)),
            pltpu.SemaphoreType.DMA((16,)),
        ],
        compiler_params=pltpu.CompilerParams(collective_id=0, has_side_effects=True),
    )(row)


QUARTERS = 4
NCH = 2 * QUARTERS
ROWS = 16
BLOCK = 2 * CTXP * ROWS


class Exchange:
    def __init__(self, tab, pool, span, pages, kv, refs, sems):
        self.tab, self.pool, self.span, self.pages, self.kv = tab, pool, span, pages, kv
        (self.pool16, self.send_y, self.recv_y, self.send_z, self.recv_z, self.send_x, self.recv_x, self.send_c,
         self.span_pad, self.send_d) = refs
        self.sems = sems
        self.t, self.d, self.y, self.z, self.x, self.core = coords()

    def barrier(self):
        t, d = self.t, self.d
        sem = pltpu.get_barrier_semaphore()
        for device in [self.peer("c", 1)] + [self.peer(a, k) for a in "yzx" for k in (1, 2, 3)]:
            pl.semaphore_signal(sem, inc=1, device_id=device, device_id_type=MESH)

        @pl.loop(0, 16)
        def _(n):
            ot, od = n // 2, t * 2 + n % 2

            @pl.when((ot != t) | (od != d))
            def _():
                pl.semaphore_signal(sem, inc=1, device_id={"tp": ot, "dec": od}, device_id_type=MESH)

        pl.semaphore_wait(sem, 26 - jnp.where(d // 2 == t, 1, 0))

    def peer(self, axis, k):
        t, d, y, z, x, c = self.t, self.d, self.y, self.z, self.x, self.core
        if axis == "c":
            c = 1 - c
        elif axis == "y":
            y = (y + k) % 4
        elif axis == "z":
            z = (z + k) % 4
        else:
            x = (x + k) % 4
        return {"tp": (z // 2) * 4 + y, "dec": x * 4 + (z % 2) * 2 + c}

    def remote(self, src, dst, send_sem, recv_sem, device):
        return pltpu.make_async_remote_copy(
            src_ref=src, dst_ref=dst, send_sem=send_sem, recv_sem=recv_sem, device_id=device, device_id_type=MESH
        )

    def pool_own(self, half):
        rows = pl.ds(self.core * 64 + half * ROWS, ROWS)
        return pltpu.make_async_copy(
            self.pool.at[:, rows, :], self.pool16[half].at[pl.ds(self.core * 8, 8)], self.sems["own"].at[half]
        )

    def pool_pair(self, half, into):
        rows = pl.ds((1 - self.core) * 64 + half * ROWS, ROWS)
        return self.remote(
            self.pool.at[:, rows, :],
            self.pool16[half].at[pl.ds(into * 8, 8)],
            self.sems["pair_send"].at[half],
            self.sems["pair_recv"].at[half],
            self.peer("c", 1),
        )

    def start_pool(self):
        for half in range(QUARTERS):
            self.pool_own(half).start()
            self.pool_pair(half, self.core).start()

    def wait_pool(self, half):
        self.pool_own(half).wait()
        self.pool_pair(half, 1 - self.core).wait_recv()

    def hop(self, axis, ch, k, source):
        send, recv, stage = {
            "y": (self.send_y, self.recv_y, 0), "z": (self.send_z, self.recv_z, 1), "x": (self.send_x, self.recv_x, 2),
        }[axis]
        units = send.shape[2]
        return self.remote(
            send.at[ch, k - 1],
            recv[ch].at[pl.ds(source * units, units)],
            self.sems["send"].at[stage, ch, k - 1],
            self.sems["recv"].at[stage, ch, k - 1],
            self.peer(axis, k),
        )

    def start_hop(self, axis, ch):
        for k in (1, 2, 3):
            self.hop(axis, ch, k, getattr(self, axis)).start()

    def wait_hop(self, axis, ch):
        me = getattr(self, axis)
        for k in (1, 2, 3):
            self.hop(axis, ch, k, (me + 4 - k) % 4).wait_recv()

    def pack_y(self, ch):
        half, kv = ch // 2, ch % 2

        @pl.loop(0, CAP_Y)
        def _(n):
            slot = self.tab[0, n]
            for k in range(4):
                to = (self.y + k) % 4
                for zhi in range(2):
                    col = pl.multiple_of((zhi * 4 + to) * 256 + kv * HD, HD)
                    block = self.pool16[half][slot, :, pl.ds(col, HD)]
                    if k == 0:
                        self.recv_y[ch][self.y * (2 * CAP_Y) + n * 2 + zhi] = block
                    else:
                        self.send_y[ch, k - 1, n * 2 + zhi] = block

        self.start_hop("y", ch)

    def pack_z(self, ch):
        self.wait_hop("y", ch)

        @pl.loop(0, CAP_Z)
        def _(n):
            for k in range(4):
                to = (self.z + k) % 4
                block = self.recv_y[ch][self.tab[1 + to % 2, n] * 2 + to // 2]
                if k == 0:
                    self.recv_z[ch][self.z * CAP_Z + n] = block
                else:
                    self.send_z[ch, k - 1, n] = block

        self.start_hop("z", ch)

    def pack_x(self, ch):
        self.wait_hop("z", ch)

        @pl.loop(0, CAP_X)
        def _(n):
            for k in range(4):
                to = (self.x + k) % 4
                block = self.recv_z[ch][self.tab[3 + to, n]]
                if k == 0:
                    self.recv_x[ch][self.x * CAP_X + n] = block
                else:
                    self.send_x[ch, k - 1, n] = block

        self.start_hop("x", ch)

    def last(self, ch, lane):
        return self.remote(
            self.send_c.at[ch],
            self.kv.at[ch, pl.ds(lane * CTXP * ROWS, CTXP * ROWS)],
            self.sems["last_send"].at[ch],
            self.sems["last_recv"].at[ch],
            self.peer("c", 1),
        )

    def pack_c(self, ch):
        self.wait_hop("x", ch)

        @pl.loop(0, CTXP)
        def _(n):
            rows = pl.ds(pl.multiple_of(n * ROWS, ROWS), ROWS)
            own = pl.ds(pl.multiple_of((self.core * CTXP + n) * ROWS, ROWS), ROWS)
            self.kv[ch, own, :] = self.recv_x[ch][self.tab[7 + self.core, n]]
            self.send_c[ch, rows, :] = self.recv_x[ch][self.tab[8 - self.core, n]]

        self.last(ch, self.core).start()

    def wait_last(self, ch):
        self.last(ch, 1 - self.core).wait_recv()

    def new_page(self, n, ot, od, half, t):
        cols = pl.ds(pl.multiple_of(t * 256, 256), 256)
        return self.remote(
            self.send_d.at[n],
            self.pages.at[half, :, cols],
            self.sems["new_send"].at[n],
            self.sems["new_recv"].at[half * 8 + t],
            {"tp": ot, "dec": od},
        )

    def own_page(self):
        cols = pl.ds(pl.multiple_of(self.t * 256, 256), 256)
        return pltpu.make_async_copy(
            self.send_d.at[self.d], self.pages.at[self.d % 2, :, cols], self.sems["new_send"].at[self.d]
        )

    def start_new(self, dest):
        self.span_pad[0:6] = self.span[...].reshape(6, PAGE, 256)
        self.span_pad[6] = jnp.zeros((PAGE, 256), jnp.bfloat16)
        ot = self.d // 2

        @pl.loop(0, 16)
        def _(n):
            od = (self.d + n) % 16
            page = jnp.int32(6)
            for p in range(6):
                page = jnp.where(dest[p] == od, p, page)
            self.send_d[od] = self.span_pad[page]
            own = (ot == self.t) & (od == self.d)

            @pl.when(own)
            def _():
                self.own_page().start()

            @pl.when(jnp.logical_not(own))
            def _():
                self.new_page(od, ot, od, self.d % 2, self.t).start()

    def wait_new(self):
        t, d = self.t, self.d

        @pl.loop(0, 16)
        def _(n):
            st, half = n // 2, n % 2
            sd = t * 2 + half
            own = (st == t) & (sd == d)

            @pl.when(own)
            def _():
                self.own_page().wait()

            @pl.when(jnp.logical_not(own))
            def _():
                self.new_page(d, st, sd, half, st).wait_recv()

        @pl.loop(0, 16)
        def _(n):
            @pl.when((d // 2 != t) | (n != d))
            def _():
                self.new_page(n, d // 2, n, d % 2, t).wait_send()

    def wait_sends(self):
        for half in range(QUARTERS):
            self.pool_pair(half, self.core).wait_send()
        for ch in range(NCH):
            for axis in "yzx":
                for k in (1, 2, 3):
                    self.hop(axis, ch, k, getattr(self, axis)).wait_send()
            self.last(ch, self.core).wait_send()


def exchange_scratch():
    bf16, vmem, dma = jnp.bfloat16, pltpu.VMEM, pltpu.SemaphoreType.DMA
    unit = (ROWS, HD)
    refs = [
        [vmem((16, ROWS, 2048), bf16) for _ in range(QUARTERS)],
        vmem((NCH, 3, 2 * CAP_Y) + unit, bf16),
        [vmem((8 * CAP_Y,) + unit, bf16) for _ in range(NCH)],
        vmem((NCH, 3, CAP_Z) + unit, bf16),
        [vmem((4 * CAP_Z,) + unit, bf16) for _ in range(NCH)],
        vmem((NCH, 3, CAP_X) + unit, bf16),
        [vmem((4 * CAP_X,) + unit, bf16) for _ in range(NCH)],
        vmem((NCH, CTXP * ROWS, HD), bf16),
        vmem((7, PAGE, 256), bf16),
        vmem((16, PAGE, 256), bf16),
    ]
    sems = {
        "own": dma((QUARTERS,)), "pair_send": dma((QUARTERS,)), "pair_recv": dma((QUARTERS,)), "send": dma((3, NCH, 3)),
        "recv": dma((3, NCH, 3)), "last_send": dma((NCH,)), "last_recv": dma((NCH,)), "new_send": dma((16,)),
        "new_recv": dma((16,)),
    }
    return refs, sems


class Attention:
    def __init__(self, q, out, s, mx, m, acc):
        self.q, self.out, self.s, self.mx, self.m, self.acc = q, out, s, mx, m, acc
        self.span = q.shape[0]
        self.heads = q.shape[1] // HD
        self.coef = LOG2E / math.sqrt(HD)

    def columns(self, n):
        return pl.ds(pl.multiple_of(n * HD, HD), HD)

    def score(self, n, slot, k, mask=None):
        q = self.q[:, self.columns(n)]
        width = k.shape[0]
        step = min(512, width)
        top = None
        for start in range(0, width, step):
            size = min(step, width - start)
            part = lax.dot_general(
                q, k[start : start + size], (((1,), (1,)), ((), ())), preferred_element_type=jnp.float32
            )
            if mask is not None:
                part = jnp.where(mask[:, start : start + size], part, NEG)
            self.s[slot][:, start : start + size] = part
            for c in range(0, size, HD):
                piece = part[:, c : c + HD]
                top = piece if top is None else jnp.maximum(top, piece)
        self.mx[slot][...] = top

    def mix(self, n, slot, v, first):
        top = jnp.broadcast_to(jnp.max(self.mx[slot][...], axis=1, keepdims=True), (self.span, HD))
        if not first:
            old = self.m[n]
            top = jnp.maximum(old, top)
            fade = jnp.exp2((old - top) * self.coef)
        self.m[n] = top
        weights = [
            jnp.exp2((self.s[slot][:, c : c + HD] - top) * self.coef).astype(jnp.bfloat16)
            for c in range(0, v.shape[0], HD)
        ]
        mixed = jnp.dot(jnp.concatenate(weights, axis=1), v, preferred_element_type=jnp.float32)
        if not first:
            mixed += self.acc[n] * jnp.concatenate([fade, fade], axis=1)
        self.acc[n] = mixed

    def two_heads(self, pair, k, v, first=False, mask=None):
        n = pair * 2
        self.score(n + 1, 1, k, mask)
        self.mix(n, 0, v, first)
        self.score(jnp.minimum(n + 2, self.heads - 1), 0, k, mask)
        self.mix(n + 1, 1, v, first)

    def causal(self):
        shape = (self.span, self.span)
        return lax.broadcasted_iota(jnp.int32, shape, 1) <= lax.broadcasted_iota(jnp.int32, shape, 0)

    def finish(self):
        @pl.loop(0, self.heads)
        def _(n):
            acc = self.acc[n]
            self.out[:, self.columns(n)] = (acc[:, :HD] / acc[:, HD:]).astype(self.out.dtype)


def attention_scratch(span, width):
    heads = width // HD
    wide = max(BLOCK, span)
    f32 = jnp.float32
    return [
        [pltpu.VMEM((span, wide), f32) for _ in range(2)],
        [pltpu.VMEM((span, HD), f32) for _ in range(2)],
        pltpu.VMEM((heads, span, HD), f32),
        pltpu.VMEM((heads, span, 2 * HD), f32),
    ]


def value_block(values, live):
    row = lax.broadcasted_iota(jnp.int32, (BLOCK, HD), 0) % (CTXP * ROWS)
    used = row < live * ROWS
    return jnp.where(used, values, 0).astype(jnp.bfloat16), jnp.where(used, 1.0, 0.0).astype(jnp.bfloat16)


def span_values(span_ref, v_span):
    v_span[:, :HD] = span_ref[:, HD:]
    v_span[:, HD:] = jnp.ones((v_span.shape[0], HD), jnp.bfloat16)


def fused_kernel(tab, dest, q, span, pool, out, pages, kv, v_span, v_block, attn, refs, sems):
    ex = Exchange(tab, pool, span, pages, kv, refs, sems)
    at = Attention(q, out, *attn)
    pairs = at.heads // 2
    first_block = 8

    ex.barrier()
    ex.start_pool()
    span_values(span, v_span)
    at.score(0, 0, span[:, :HD], at.causal())

    @pl.loop(0, first_block + QUARTERS * pairs)
    def _(step):
        for i in range(NCH + 3):

            @pl.when(step == 2 * i)
            def _(i=i):
                if i == 0:
                    ex.wait_pool(0)
                    ex.pack_y(0)
                if 0 <= i - 3 < NCH:
                    ex.pack_c(i - 3)
                if 0 <= i - 2 < NCH:
                    ex.pack_x(i - 2)
                if 0 <= i - 1 < NCH:
                    ex.pack_z(i - 1)
                if i + 1 < NCH:
                    if i % 2 == 1:
                        ex.wait_pool((i + 1) // 2)
                    ex.pack_y(i + 1)
                if i == NCH:
                    ex.start_new(dest)

        @pl.when(step < pairs)
        def _():
            at.two_heads(step, span[:, :HD], v_span[...], True, at.causal())

        for b in range(QUARTERS):

            @pl.when(step == first_block + b * pairs)
            def _(b=b):
                ex.wait_last(2 * b)
                ex.wait_last(2 * b + 1)
                values, ones = value_block(kv[2 * b + 1], tab[9, 0])
                v_block[:, :HD] = values
                v_block[:, HD:] = ones
                at.score(0, 0, kv[2 * b])

        @pl.when(step >= first_block)
        def _():
            e = step - first_block
            at.two_heads(e % pairs, kv[(e // pairs) * 2], v_block[...])

    at.finish()
    ex.wait_new()
    ex.wait_sends()


def fused(table, dest, queries, span, pool):
    refs, sems = exchange_scratch()
    vmem = pl.BlockSpec(memory_space=pltpu.VMEM)
    smem = pl.BlockSpec(memory_space=pltpu.SMEM)
    hbm = pl.BlockSpec(memory_space=pl.ANY)
    bf16 = jnp.bfloat16
    rows, width = queries.shape
    return pl.pallas_call(
        fused_kernel,
        out_shape=[jax.ShapeDtypeStruct((rows, width), bf16), jax.ShapeDtypeStruct((2, PAGE, 2048), bf16)],
        in_specs=[smem, smem, vmem, vmem, hbm],
        out_specs=[vmem, hbm],
        scratch_shapes=[
            pltpu.VMEM((NCH, BLOCK, HD), bf16),
            pltpu.VMEM((rows, 2 * HD), bf16),
            pltpu.VMEM((BLOCK, 2 * HD), bf16),
            attention_scratch(rows, width),
            refs,
            sems,
        ],
        compiler_params=pltpu.CompilerParams(
            collective_id=1, has_side_effects=True, vmem_limit_bytes=62 * 1024 * 1024
        ),
    )(table, dest, queries, span, pool)


def attend_kernel(tab, q, span, kv, out, v_span, v_block, attn):
    at = Attention(q, out, *attn)
    pairs = at.heads // 2
    span_values(span, v_span)
    at.score(0, 0, span[:, :HD], at.causal())

    @pl.loop(0, pairs)
    def _(pair):
        at.two_heads(pair, span[:, :HD], v_span[...], True, at.causal())

    @pl.loop(0, QUARTERS)
    def _(b):
        values, ones = value_block(kv[2 * b + 1], tab[9, 0])
        v_block[:, :HD] = values
        v_block[:, HD:] = ones
        at.score(0, 0, kv[2 * b])

        @pl.loop(0, pairs)
        def _(pair):
            at.two_heads(pair, kv[2 * b], v_block[...])

    at.finish()


def attend(table, queries, span, kv):
    rows, width = queries.shape
    vmem = pl.BlockSpec(memory_space=pltpu.VMEM)
    smem = pl.BlockSpec(memory_space=pltpu.SMEM)
    return pl.pallas_call(
        attend_kernel,
        out_shape=jax.ShapeDtypeStruct((rows, width), jnp.bfloat16),
        in_specs=[smem, vmem, vmem, vmem],
        out_specs=vmem,
        scratch_shapes=[
            pltpu.VMEM((rows, 2 * HD), jnp.bfloat16),
            pltpu.VMEM((BLOCK, 2 * HD), jnp.bfloat16),
            attention_scratch(rows, width),
        ],
        compiler_params=pltpu.CompilerParams(vmem_limit_bytes=48 * 1024 * 1024),
    )(table, queries, span, kv)


def dense(table, dest, queries, span, pool, slots, flags):
    tp_size, dec_size = lax.axis_size("tp"), lax.axis_size("dec")
    devices = tp_size * dec_size
    width = span.shape[1]
    view = pool.reshape(pool.shape[0], PAGE, tp_size, width)
    source_rows = (jnp.arange(devices, dtype=jnp.int32) // dec_size)[:, None]
    axes = ("tp", "dec")
    asked = lax.all_to_all(slots, axes, split_axis=0, concat_axis=0, tiled=True)
    fetched = lax.all_to_all(view[asked, :, source_rows], axes, split_axis=0, concat_axis=0, tiled=True)
    live_index, live_count = compact_slots(flags)
    live_index = jnp.where(jnp.arange(CTXP) < live_count, live_index, live_index[0])
    cached = fetched.reshape(devices, PAGE, width)[live_index]
    cached = cached.reshape(CTXP, 2, QUARTERS, ROWS, 2, HD)
    cached = jnp.transpose(cached, (2, 4, 1, 0, 3, 5)).reshape(NCH, BLOCK, HD)
    new_pages = span.reshape(-1, PAGE, width)
    chosen = (dest[None, :] == jnp.arange(dec_size, dtype=jnp.int32)[:, None]).astype(jnp.bfloat16)
    outgoing = jnp.einsum("dp,pkc->dkc", chosen, new_pages, preferred_element_type=jnp.float32).astype(jnp.bfloat16)
    placed = lax.all_to_all(outgoing, "dec", split_axis=0, concat_axis=0, tiled=True)
    placed = lax.all_to_all(placed, "tp", split_axis=0, concat_axis=2, tiled=True)
    return (attend(table, queries, span, cached), placed)


def body(queries, span_kv, page_pool, cache_slot, cache_live, span_dest):
    table = make_table(cache_slot, cache_live)
    attn_out, placed = lax.cond(
        table[10, 0] > 0,
        lambda *a: dense(*a),
        lambda tab, dest, q, span, pool, slots, flags: tuple(fused(tab, dest, q, span, pool)),
        table, span_dest[0], queries[0], span_kv[0], page_pool, cache_slot[0], cache_live[0],
    )
    return (attn_out[None], placed)


def solution(mesh):
    in_specs = (
        P("dec", None, "tp"),
        P("dec", None, "tp"),
        P(("tp", "dec"), None, None),
        P("dec", None, None),
        P("dec", None, None),
        P("dec", None),
    )
    out_specs = (P("dec", None, "tp"), P(("tp", "dec"), None, None))
    return jax.shard_map(body, mesh=mesh, in_specs=in_specs, out_specs=out_specs, check_vma=False)
```

```python
import functools
import math

import jax
import jax.numpy as jnp
from jax import lax
from jax.experimental import pallas as pl
from jax.experimental.pallas import tpu as pltpu
from jax.sharding import PartitionSpec as P

HD = 128
PAGE = 128
CTXP = 32
LOG2E = 1.4426950408889634
NEG = -1e30


def compact_slots(live_flags):
    flat_live = live_flags.reshape(-1)
    live_rank = jnp.cumsum(flat_live) - 1
    slot_ids = jnp.arange(flat_live.shape[0], dtype=jnp.int32)
    targets = jnp.arange(CTXP, dtype=jnp.int32)
    select_table = (flat_live[None, :] == 1) & (live_rank[None, :] == targets[:, None])
    live_index = jnp.sum(jnp.where(select_table, slot_ids[None, :], 0), axis=1)
    return (live_index, jnp.sum(flat_live))


MESH = pl.DeviceIdType.MESH
CAP_Y, CAP_Z, CAP_X = 13, 25, 26
LISTS = 16


def coords():
    t, d = lax.axis_index("tp"), lax.axis_index("dec")
    return t, d, t % 4, (t // 4) * 2 + (d // 2) % 2, d // 4, d % 2


def flag(cond, dtype=jnp.float32):
    return jnp.where(cond, 1.0, 0.0).astype(dtype)


def table_kernel(row_ref, tab_ref, all_ref, send_sem, recv_sem):
    t, d, y, z, x, core = coords()
    n = 16
    barrier = pltpu.get_barrier_semaphore()
    for k in range(1, n):
        pl.semaphore_signal(barrier, inc=1, device_id={"dec": (d + k) % n}, device_id_type=MESH)
    pl.semaphore_wait(barrier, n - 1)

    def copy(k, slot):
        return pltpu.make_async_remote_copy(
            src_ref=row_ref,
            dst_ref=all_ref.at[slot],
            send_sem=send_sem.at[k],
            recv_sem=recv_sem.at[slot],
            device_id={"dec": (d + k) % n},
            device_id_type=MESH,
        )

    for k in range(1, n):
        copy(k, d).start()
    all_ref[d] = row_ref[...]

    bf16, f32 = jnp.bfloat16, jnp.float32
    oi = lax.broadcasted_iota(jnp.int32, (128, 128), 0)
    oj = lax.broadcasted_iota(jnp.int32, (128, 128), 1)
    gi = lax.broadcasted_iota(jnp.int32, (16, 16), 0)
    gj = lax.broadcasted_iota(jnp.int32, (16, 16), 1)
    owner_groups = (lambda o: o >> 1, lambda o: o & 0x4E, lambda o: o & 0x0C, lambda o: o & 0)
    row_groups = (lambda g: g & 0, lambda g: g >> 3, lambda g: g & 14, lambda g: g)

    for k in range(1, n):
        copy(k, (d + n - k) % n).wait_recv()
    packed = jnp.concatenate([all_ref[g, 0:1, :] for g in range(n)], axis=0)
    o = lax.broadcasted_iota(jnp.int32, (16, 128), 1)
    g = lax.broadcasted_iota(jnp.int32, (16, 128), 0)
    g_zlo = (g >> 1) & 1
    asked = [
        [jnp.max(flag((packed == s) & (g_zlo == b)), axis=0, keepdims=True) for s in range(8)] for b in range(2)
    ]
    by_slot = [jnp.maximum(p, q) for p, q in zip(*asked)]
    wants = (
        jnp.concatenate(by_slot + [jnp.zeros((8, 128), f32)], axis=0).astype(bf16),
        jnp.concatenate(asked[0] + asked[1], axis=0).astype(bf16),
        flag(packed >= 0, bf16),
        flag(packed >= 0, bf16),
    )

    ranks, counts = [], []
    for want, owner, row in zip(wants, owner_groups, row_groups):
        same = owner(oi) == owner(oj)
        before = jnp.dot(want, flag(same & (oi < oj), bf16), preferred_element_type=f32)
        total = jnp.dot(want, flag(same, bf16), preferred_element_type=f32)
        side = row(gi) == row(gj)
        rank = jnp.dot(flag(side, bf16), before.astype(bf16), preferred_element_type=f32)
        rank += jnp.dot(flag(side & (gj < gi), bf16), want, preferred_element_type=f32)
        ranks.append(rank.astype(jnp.int32))
        counts.append(jnp.dot(flag(side, bf16), total.astype(bf16), preferred_element_type=f32).astype(jnp.int32))

    rank_y = jnp.concatenate([ranks[0][0:8], ranks[0][0:8]], axis=0)
    rank_z = jnp.zeros((16, 128), jnp.int32)
    for s in range(8):
        row = jnp.where(g_zlo == 1, ranks[1][8 + s : 9 + s, :], ranks[1][s : s + 1, :])
        rank_z = jnp.where(packed == s, row, rank_z)

    o_x, o_y, o_z, o_c = (o >> 2) & 3, (o >> 4) & 3, ((o >> 6) << 1) | ((o >> 1) & 1), o & 1
    zlo = z % 2
    places = (
        (o_x == x) & (o_y == y) & (o_z == z),
        (o_x == x) & (o_z == z),
        (o_x == x) & (g_zlo == zlo),
        (g >> 1) == x * 2 + zlo,
    )
    mine = [(want.astype(f32) > 0) & place for want, place in zip(wants, places)]
    values = (
        o_c * 8 + g,
        o_y * CAP_Y + rank_y,
        o_z * CAP_Z + rank_z,
        o_x * CAP_X + ranks[2],
    )
    lists = (
        (range(8),),
        (range(8), range(8, 16)),
        [[r for r in range(16) if r >> 2 == b] for b in range(4)],
        [[r for r in range(16) if r & 1 == b] for b in range(2)],
    )
    place = lax.broadcasted_iota(jnp.int32, (CTXP, 128), 0)
    lane = lax.broadcasted_iota(jnp.int32, (CTXP, 128), 1)
    table = jnp.zeros((CTXP, 128), jnp.int32)
    column = 0
    for stage in range(4):
        rank = jnp.where(mine[stage], ranks[stage], -1)
        for rows in lists[stage]:
            found = jnp.zeros((CTXP, 128), jnp.int32)
            for r in rows:
                found += jnp.where(rank[r : r + 1, :] == place, values[stage][r : r + 1, :], 0)
            found = jnp.sum(found.astype(f32), axis=1, keepdims=True).astype(jnp.int32)
            table = jnp.where(lane == column, found, table)
            column += 1
    live = packed >= 0
    held = jnp.sum(flag(live & (g == d))).astype(jnp.int32)
    over = jnp.maximum(
        jnp.maximum(jnp.max(counts[0]) - CAP_Y, jnp.max(counts[1]) - CAP_Z), jnp.max(counts[2]) - CAP_X
    )
    for c in range(2):
        size = jnp.sum(flag(live & (g == (d // 2) * 2 + c))).astype(jnp.int32)
        table = jnp.where((lane == 7 + c) & (place >= size), table[0:1, :], table)
    table = jnp.where(lane == 9, held, table)
    table = jnp.where(lane == 10, jnp.maximum(over, 0), table)
    square = jnp.concatenate([table.astype(f32), jnp.zeros((128 - CTXP, 128), f32)], axis=0)
    tab_ref[...] = jnp.transpose(square)[:LISTS, :].astype(jnp.int32)
    for k in range(1, n):
        copy(k, d).wait_send()


def make_table(cache_slot, cache_live):
    row = jnp.where(cache_live[0, :, 0] == 1, cache_slot[0, :, 0], -1)
    row = jnp.broadcast_to(row[None, :], (8, 128))
    vmem = pl.BlockSpec(memory_space=pltpu.VMEM)
    return pl.pallas_call(
        table_kernel,
        out_shape=jax.ShapeDtypeStruct((LISTS, 128), jnp.int32),
        in_specs=[vmem],
        out_specs=vmem,
        scratch_shapes=[
            pltpu.VMEM((16, 8, 128), jnp.int32),
            pltpu.SemaphoreType.DMA((16,)),
            pltpu.SemaphoreType.DMA((16,)),
        ],
        compiler_params=pltpu.CompilerParams(collective_id=0, has_side_effects=True),
    )(row)


QUARTERS = 4
NCH = 2 * QUARTERS
ROWS = 16
BLOCK = 2 * CTXP * ROWS


class Exchange:
    def __init__(self, tab, pool, span, pages, kv, refs, sems):
        self.tab, self.pool, self.span, self.pages, self.kv = tab, pool, span, pages, kv
        (self.pool16, self.send_y, self.recv_y, self.send_z, self.recv_z, self.send_x, self.recv_x, self.send_c,
         self.span_pad, self.send_n, self.recv_n) = refs
        self.sems = sems
        self.t, self.d, self.y, self.z, self.x, self.core = coords()

    def barrier(self):
        t, d = self.t, self.d
        sem = pltpu.get_barrier_semaphore()
        for device in [self.peer("c", 1)] + [self.peer(a, k) for a in "yzx" for k in (1, 2, 3)]:
            pl.semaphore_signal(sem, inc=1, device_id=device, device_id_type=MESH)

        zlo = self.z % 2

        @pl.loop(0, 16)
        def _(n):
            device = {"tp": n // 2, "dec": self.x * 4 + (t % 2) * 2 + n % 2}

            @pl.when((n // 2 != t) | (device["dec"] != d))
            def _():
                pl.semaphore_signal(sem, inc=1, device_id=device, device_id_type=MESH)

        pl.semaphore_wait(sem, 26 - jnp.where(t % 2 == zlo, 1, 0))

    def peer(self, axis, k):
        t, d, y, z, x, c = self.t, self.d, self.y, self.z, self.x, self.core
        if axis == "c":
            c = 1 - c
        elif axis == "y":
            y = (y + k) % 4
        elif axis == "z":
            z = (z + k) % 4
        else:
            x = (x + k) % 4
        return {"tp": (z // 2) * 4 + y, "dec": x * 4 + (z % 2) * 2 + c}

    def remote(self, src, dst, send_sem, recv_sem, device):
        return pltpu.make_async_remote_copy(
            src_ref=src, dst_ref=dst, send_sem=send_sem, recv_sem=recv_sem, device_id=device, device_id_type=MESH
        )

    def pool_own(self, half):
        rows = pl.ds(self.core * 64 + half * ROWS, ROWS)
        return pltpu.make_async_copy(
            self.pool.at[:, rows, :], self.pool16[half].at[pl.ds(self.core * 8, 8)], self.sems["own"].at[half]
        )

    def pool_pair(self, half, into):
        rows = pl.ds((1 - self.core) * 64 + half * ROWS, ROWS)
        return self.remote(
            self.pool.at[:, rows, :],
            self.pool16[half].at[pl.ds(into * 8, 8)],
            self.sems["pair_send"].at[half],
            self.sems["pair_recv"].at[half],
            self.peer("c", 1),
        )

    def start_pool(self):
        for half in range(QUARTERS):
            self.pool_pair(half, self.core).start()

    def wait_pool(self, half):
        self.pool_own(half).wait()
        self.pool_pair(half, 1 - self.core).wait_recv()

    def hop(self, axis, ch, k, source):
        send, recv, stage = {
            "y": (self.send_y, self.recv_y, 0), "z": (self.send_z, self.recv_z, 1), "x": (self.send_x, self.recv_x, 2),
        }[axis]
        units = send.shape[2]
        return self.remote(
            send.at[ch, k - 1],
            recv[ch].at[pl.ds(source * units, units)],
            self.sems["send"].at[stage, ch, k - 1],
            self.sems["recv"].at[stage, ch, k - 1],
            self.peer(axis, k),
        )

    def start_hop(self, axis, ch):
        for k in (1, 2, 3):
            self.hop(axis, ch, k, getattr(self, axis)).start()

    def wait_hop(self, axis, ch):
        me = getattr(self, axis)
        for k in (1, 2, 3):
            self.hop(axis, ch, k, (me + 4 - k) % 4).wait_recv()

    def pack_y(self, ch):
        half, kv = ch // 2, ch % 2

        @pl.loop(0, CAP_Y, unroll=True)
        def _(n):
            slot = self.tab[0, n]
            for k in range(4):
                to = (self.y + k) % 4
                for zhi in range(2):
                    col = pl.multiple_of((zhi * 4 + to) * 256 + kv * HD, HD)
                    block = self.pool16[half][slot, :, pl.ds(col, HD)]
                    if k == 0:
                        self.recv_y[ch][self.y * (2 * CAP_Y) + n * 2 + zhi] = block
                    else:
                        self.send_y[ch, k - 1, n * 2 + zhi] = block

        self.start_hop("y", ch)

    def pack_z(self, ch):
        self.wait_hop("y", ch)

        @pl.loop(0, CAP_Z, unroll=True)
        def _(n):
            for k in range(4):
                to = (self.z + k) % 4
                block = self.recv_y[ch][self.tab[1 + to % 2, n] * 2 + to // 2]
                if k == 0:
                    self.recv_z[ch][self.z * CAP_Z + n] = block
                else:
                    self.send_z[ch, k - 1, n] = block

        self.start_hop("z", ch)

    def pack_x(self, ch):
        self.wait_hop("z", ch)

        @pl.loop(0, CAP_X, unroll=True)
        def _(n):
            for k in range(4):
                to = (self.x + k) % 4
                block = self.recv_z[ch][self.tab[3 + to, n]]
                if k == 0:
                    self.recv_x[ch][self.x * CAP_X + n] = block
                else:
                    self.send_x[ch, k - 1, n] = block

        self.start_hop("x", ch)

    def last(self, ch, lane):
        return self.remote(
            self.send_c.at[ch],
            self.kv.at[ch, pl.ds(lane * CTXP * ROWS, CTXP * ROWS)],
            self.sems["last_send"].at[ch],
            self.sems["last_recv"].at[ch],
            self.peer("c", 1),
        )

    def pack_c(self, ch):
        self.wait_hop("x", ch)

        @pl.loop(0, CTXP, unroll=True)
        def _(n):
            rows = pl.ds(pl.multiple_of(n * ROWS, ROWS), ROWS)
            own = pl.ds(pl.multiple_of((self.core * CTXP + n) * ROWS, ROWS), ROWS)
            self.kv[ch, own, :] = self.recv_x[ch][self.tab[7 + self.core, n]]
            self.send_c[ch, rows, :] = self.recv_x[ch][self.tab[8 - self.core, n]]

        self.last(ch, self.core).start()

    def wait_last(self, ch):
        self.last(ch, 1 - self.core).wait_recv()

    def new_hop(self, k, source):
        return self.remote(
            self.send_n.at[k - 1],
            self.recv_n.at[source],
            self.sems["new_send"].at[k - 1],
            self.sems["new_recv"].at[k - 1],
            self.peer("x", k),
        )

    def start_new(self, dest):
        self.span_pad[0:6] = self.span[...].reshape(6, PAGE, 256)
        self.span_pad[6] = jnp.zeros((PAGE, 256), jnp.bfloat16)
        for k in range(4):
            for j in range(4):
                column = ((self.x + k) % 4) * 4 + j
                page = jnp.int32(6)
                for p in range(6):
                    page = jnp.where(dest[p] == column, p, page)
                if k == 0:
                    self.recv_n[self.x, j] = self.span_pad[page]
                else:
                    self.send_n[k - 1, j] = self.span_pad[page]
        for k in (1, 2, 3):
            self.new_hop(k, self.x).start()

    def new_page(self, n, owner_t, owner_d, core, t):
        cols = pl.ds(pl.multiple_of(t * 256, 256), 256)
        return self.remote(
            self.recv_n.at[n // 4, n % 4],
            self.pages.at[core, :, cols],
            self.sems["page_send"].at[n],
            self.sems["page_recv"].at[core * 8 + t],
            {"tp": owner_t, "dec": owner_d},
        )

    def own_page(self, n):
        cols = pl.ds(pl.multiple_of(self.t * 256, 256), 256)
        return pltpu.make_async_copy(
            self.recv_n.at[n // 4, n % 4], self.pages.at[self.core, :, cols], self.sems["page_send"].at[n]
        )

    def each_page(self, mine, other):
        @pl.loop(0, 16)
        def _(n):
            owner_t, owner_d = (n // 4) * 2 + self.z % 2, self.x * 4 + n % 4
            own = (owner_t == self.t) & (owner_d == self.d)

            @pl.when(own)
            def _():
                mine(self.own_page(n))

            @pl.when(jnp.logical_not(own))
            def _():
                other(self.new_page(n, owner_t, owner_d, self.core, self.t))

    def forward_new(self):
        for k in (1, 2, 3):
            self.new_hop(k, (self.x + 4 - k) % 4).wait_recv()
        self.each_page(lambda copy: copy.start(), lambda copy: copy.start())

    def wait_new(self):
        self.each_page(lambda copy: copy.wait(), lambda copy: copy.wait_send())
        block = (self.t // 2) * 4 + self.d % 4

        @pl.loop(0, 16)
        def _(n):
            sender_t, core = n // 2, n % 2
            sender_d = self.x * 4 + (self.t % 2) * 2 + core

            @pl.when((sender_t != self.t) | (sender_d != self.d))
            def _():
                self.new_page(block, sender_t, sender_d, core, sender_t).wait_recv()

        for k in (1, 2, 3):
            self.new_hop(k, self.x).wait_send()

    def wait_sends(self):
        for half in range(QUARTERS):
            self.pool_pair(half, self.core).wait_send()
        for ch in range(NCH):
            for axis in "yzx":
                for k in (1, 2, 3):
                    self.hop(axis, ch, k, getattr(self, axis)).wait_send()
            self.last(ch, self.core).wait_send()


def exchange_scratch():
    bf16, vmem, dma = jnp.bfloat16, pltpu.VMEM, pltpu.SemaphoreType.DMA
    unit = (ROWS, HD)
    refs = [
        [vmem((16, ROWS, 2048), bf16) for _ in range(QUARTERS)],
        vmem((NCH, 3, 2 * CAP_Y) + unit, bf16),
        [vmem((8 * CAP_Y,) + unit, bf16) for _ in range(NCH)],
        vmem((NCH, 3, CAP_Z) + unit, bf16),
        [vmem((4 * CAP_Z,) + unit, bf16) for _ in range(NCH)],
        vmem((NCH, 3, CAP_X) + unit, bf16),
        [vmem((4 * CAP_X,) + unit, bf16) for _ in range(NCH)],
        vmem((NCH, CTXP * ROWS, HD), bf16),
        vmem((7, PAGE, 256), bf16),
        vmem((3, 4, PAGE, 256), bf16),
        vmem((4, 4, PAGE, 256), bf16),
    ]
    sems = {
        "own": dma((QUARTERS,)), "pair_send": dma((QUARTERS,)), "pair_recv": dma((QUARTERS,)), "send": dma((3, NCH, 3)),
        "recv": dma((3, NCH, 3)), "last_send": dma((NCH,)), "last_recv": dma((NCH,)), "new_send": dma((3,)),
        "new_recv": dma((3,)), "page_send": dma((16,)), "page_recv": dma((16,)),
    }
    return refs, sems


class Attention:
    def __init__(self, q, out, s, mx, m, acc):
        self.q, self.out, self.s, self.mx, self.m, self.acc = q, out, s, mx, m, acc
        self.span = q.shape[0]
        self.heads = q.shape[1] // HD
        self.coef = LOG2E / math.sqrt(HD)

    def columns(self, n):
        return pl.ds(pl.multiple_of(n * HD, HD), HD)

    def score(self, n, slot, k, mask=None):
        q = self.q[:, self.columns(n)]
        width = k.shape[0]
        step = min(512, width)
        top = None
        for start in range(0, width, step):
            size = min(step, width - start)
            part = lax.dot_general(
                q, k[start : start + size], (((1,), (1,)), ((), ())), preferred_element_type=jnp.float32
            )
            if mask is not None:
                part = jnp.where(mask[:, start : start + size], part, NEG)
            self.s[slot][:, start : start + size] = part
            for c in range(0, size, HD):
                piece = part[:, c : c + HD]
                top = piece if top is None else jnp.maximum(top, piece)
        self.mx[slot][...] = top

    def mix(self, n, slot, v, first):
        top = jnp.broadcast_to(jnp.max(self.mx[slot][...], axis=1, keepdims=True), (self.span, HD))
        if not first:
            old = self.m[n]
            top = jnp.maximum(old, top)
            fade = jnp.exp2((old - top) * self.coef)
        self.m[n] = top
        weights = [
            jnp.exp2((self.s[slot][:, c : c + HD] - top) * self.coef).astype(jnp.bfloat16)
            for c in range(0, v.shape[0], HD)
        ]
        mixed = jnp.dot(jnp.concatenate(weights, axis=1), v, preferred_element_type=jnp.float32)
        if not first:
            mixed += self.acc[n] * jnp.concatenate([fade, fade], axis=1)
        self.acc[n] = mixed

    def two_heads(self, pair, k, v, first=False, mask=None):
        n = pair * 2
        self.score(n + 1, 1, k, mask)
        self.mix(n, 0, v, first)
        self.score(jnp.minimum(n + 2, self.heads - 1), 0, k, mask)
        self.mix(n + 1, 1, v, first)

    def causal(self):
        shape = (self.span, self.span)
        return lax.broadcasted_iota(jnp.int32, shape, 1) <= lax.broadcasted_iota(jnp.int32, shape, 0)

    def finish(self):
        @pl.loop(0, self.heads)
        def _(n):
            acc = self.acc[n]
            self.out[:, self.columns(n)] = (acc[:, :HD] / acc[:, HD:]).astype(self.out.dtype)


def attention_scratch(span, width):
    heads = width // HD
    wide = max(BLOCK, span)
    f32 = jnp.float32
    return [
        [pltpu.VMEM((span, wide), f32) for _ in range(2)],
        [pltpu.VMEM((span, HD), f32) for _ in range(2)],
        pltpu.VMEM((heads, span, HD), f32),
        pltpu.VMEM((heads, span, 2 * HD), f32),
    ]


def value_block(values, live):
    row = lax.broadcasted_iota(jnp.int32, (BLOCK, HD), 0) % (CTXP * ROWS)
    used = row < live * ROWS
    return jnp.where(used, values, 0).astype(jnp.bfloat16), jnp.where(used, 1.0, 0.0).astype(jnp.bfloat16)


def span_values(span_ref, v_span):
    v_span[:, :HD] = span_ref[:, HD:]
    v_span[:, HD:] = jnp.ones((v_span.shape[0], HD), jnp.bfloat16)


FORWARD = 10


def fused_kernel(tab, dest, q, span, pool, out, pages, kv, v_span, v_block, attn, refs, sems):
    ex = Exchange(tab, pool, span, pages, kv, refs, sems)
    at = Attention(q, out, *attn)
    pairs = at.heads // 2
    first_block = 10

    for quarter in range(QUARTERS):
        ex.pool_own(quarter).start()
    ex.barrier()
    ex.start_pool()
    ex.wait_pool(0)
    ex.pack_y(0)
    ex.pack_y(1)
    ex.start_new(dest)
    span_values(span, v_span)
    at.score(0, 0, span[:, :HD], at.causal())

    @pl.loop(0, first_block + QUARTERS * pairs)
    def _(step):
        for i in range(1, NCH + 3):

            @pl.when(step == 2 * i)
            def _(i=i):
                if i - 1 < NCH:
                    ex.pack_z(i - 1)
                if i + 1 < NCH:
                    if i % 2 == 1:
                        ex.wait_pool((i + 1) // 2)
                    ex.pack_y(i + 1)
                if i == FORWARD:
                    ex.forward_new()

            @pl.when(step == 2 * i + 1)
            def _(i=i):
                if 0 <= i - 2 < NCH:
                    ex.pack_x(i - 2)
                if 0 <= i - 3 < NCH:
                    ex.pack_c(i - 3)

        @pl.when(step < pairs)
        def _():
            at.two_heads(step, span[:, :HD], v_span[...], True, at.causal())

        for b in range(QUARTERS):

            @pl.when(step == first_block + b * pairs)
            def _(b=b):
                ex.wait_last(2 * b)
                ex.wait_last(2 * b + 1)
                values, ones = value_block(kv[2 * b + 1], tab[9, 0])
                v_block[:, :HD] = values
                v_block[:, HD:] = ones
                at.score(0, 0, kv[2 * b])

        @pl.when(step >= first_block)
        def _():
            e = step - first_block
            at.two_heads(e % pairs, kv[(e // pairs) * 2], v_block[...])

    at.finish()
    ex.wait_new()
    ex.wait_sends()


def fused(table, dest, queries, span, pool):
    refs, sems = exchange_scratch()
    vmem = pl.BlockSpec(memory_space=pltpu.VMEM)
    smem = pl.BlockSpec(memory_space=pltpu.SMEM)
    hbm = pl.BlockSpec(memory_space=pl.ANY)
    bf16 = jnp.bfloat16
    rows, width = queries.shape
    return pl.pallas_call(
        fused_kernel,
        out_shape=[jax.ShapeDtypeStruct((rows, width), bf16), jax.ShapeDtypeStruct((2, PAGE, 2048), bf16)],
        in_specs=[smem, smem, vmem, vmem, hbm],
        out_specs=[vmem, hbm],
        scratch_shapes=[
            pltpu.VMEM((NCH, BLOCK, HD), bf16),
            pltpu.VMEM((rows, 2 * HD), bf16),
            pltpu.VMEM((BLOCK, 2 * HD), bf16),
            attention_scratch(rows, width),
            refs,
            sems,
        ],
        compiler_params=pltpu.CompilerParams(
            collective_id=1, has_side_effects=True, vmem_limit_bytes=62 * 1024 * 1024
        ),
    )(table, dest, queries, span, pool)


def attend_kernel(tab, q, span, kv, out, v_span, v_block, attn):
    at = Attention(q, out, *attn)
    pairs = at.heads // 2
    span_values(span, v_span)
    at.score(0, 0, span[:, :HD], at.causal())

    @pl.loop(0, pairs)
    def _(pair):
        at.two_heads(pair, span[:, :HD], v_span[...], True, at.causal())

    @pl.loop(0, QUARTERS)
    def _(b):
        values, ones = value_block(kv[2 * b + 1], tab[9, 0])
        v_block[:, :HD] = values
        v_block[:, HD:] = ones
        at.score(0, 0, kv[2 * b])

        @pl.loop(0, pairs)
        def _(pair):
            at.two_heads(pair, kv[2 * b], v_block[...])

    at.finish()


def attend(table, queries, span, kv):
    rows, width = queries.shape
    vmem = pl.BlockSpec(memory_space=pltpu.VMEM)
    smem = pl.BlockSpec(memory_space=pltpu.SMEM)
    return pl.pallas_call(
        attend_kernel,
        out_shape=jax.ShapeDtypeStruct((rows, width), jnp.bfloat16),
        in_specs=[smem, vmem, vmem, vmem],
        out_specs=vmem,
        scratch_shapes=[
            pltpu.VMEM((rows, 2 * HD), jnp.bfloat16),
            pltpu.VMEM((BLOCK, 2 * HD), jnp.bfloat16),
            attention_scratch(rows, width),
        ],
        compiler_params=pltpu.CompilerParams(vmem_limit_bytes=48 * 1024 * 1024),
    )(table, queries, span, kv)


def dense(table, dest, queries, span, pool, slots, flags):
    tp_size, dec_size = lax.axis_size("tp"), lax.axis_size("dec")
    devices = tp_size * dec_size
    width = span.shape[1]
    view = pool.reshape(pool.shape[0], PAGE, tp_size, width)
    source_rows = (jnp.arange(devices, dtype=jnp.int32) // dec_size)[:, None]
    axes = ("tp", "dec")
    asked = lax.all_to_all(slots, axes, split_axis=0, concat_axis=0, tiled=True)
    fetched = lax.all_to_all(view[asked, :, source_rows], axes, split_axis=0, concat_axis=0, tiled=True)
    live_index, live_count = compact_slots(flags)
    live_index = jnp.where(jnp.arange(CTXP) < live_count, live_index, live_index[0])
    cached = fetched.reshape(devices, PAGE, width)[live_index]
    cached = cached.reshape(CTXP, 2, QUARTERS, ROWS, 2, HD)
    cached = jnp.transpose(cached, (2, 4, 1, 0, 3, 5)).reshape(NCH, BLOCK, HD)
    new_pages = span.reshape(-1, PAGE, width)
    chosen = (dest[None, :] == jnp.arange(dec_size, dtype=jnp.int32)[:, None]).astype(jnp.bfloat16)
    outgoing = jnp.einsum("dp,pkc->dkc", chosen, new_pages, preferred_element_type=jnp.float32).astype(jnp.bfloat16)
    placed = lax.all_to_all(outgoing, "dec", split_axis=0, concat_axis=0, tiled=True)
    placed = lax.all_to_all(placed, "tp", split_axis=0, concat_axis=2, tiled=True)
    return (attend(table, queries, span, cached), placed)


def body(queries, span_kv, page_pool, cache_slot, cache_live, span_dest):
    table = make_table(cache_slot, cache_live)
    attn_out, placed = lax.cond(
        table[10, 0] > 0,
        lambda *a: dense(*a),
        lambda tab, dest, q, span, pool, slots, flags: tuple(fused(tab, dest, q, span, pool)),
        table, span_dest[0], queries[0], span_kv[0], page_pool, cache_slot[0], cache_live[0],
    )
    return (attn_out[None], placed)


def solution(mesh):
    in_specs = (
        P("dec", None, "tp"),
        P("dec", None, "tp"),
        P(("tp", "dec"), None, None),
        P("dec", None, None),
        P("dec", None, None),
        P("dec", None),
    )
    out_specs = (P("dec", None, "tp"), P(("tp", "dec"), None, None))
    return jax.shard_map(body, mesh=mesh, in_specs=in_specs, out_specs=out_specs, check_vma=False)
```

```python
import functools
import math

import jax
import jax.numpy as jnp
from jax import lax
from jax.experimental import pallas as pl
from jax.experimental.pallas import tpu as pltpu
from jax.sharding import PartitionSpec as P

HD = 128
PAGE = 128
CTXP = 32
LOG2E = 1.4426950408889634
NEG = -1e30


def compact_slots(live_flags):
    flat_live = live_flags.reshape(-1)
    live_rank = jnp.cumsum(flat_live) - 1
    slot_ids = jnp.arange(flat_live.shape[0], dtype=jnp.int32)
    targets = jnp.arange(CTXP, dtype=jnp.int32)
    select_table = (flat_live[None, :] == 1) & (live_rank[None, :] == targets[:, None])
    live_index = jnp.sum(jnp.where(select_table, slot_ids[None, :], 0), axis=1)
    return (live_index, jnp.sum(flat_live))


MESH = pl.DeviceIdType.MESH
CAP_Y, CAP_Z, CAP_X = 13, 25, 26
LISTS = 16


def coords():
    t, d = lax.axis_index("tp"), lax.axis_index("dec")
    return t, d, t % 4, (t // 4) * 2 + (d // 2) % 2, d // 4, d % 2


def flag(cond, dtype=jnp.float32):
    return jnp.where(cond, 1.0, 0.0).astype(dtype)


def table_kernel(row_ref, tab_ref, all_ref, send_sem, recv_sem):
    t, d, y, z, x, core = coords()
    n = 16
    barrier = pltpu.get_barrier_semaphore()
    for k in range(1, n):
        pl.semaphore_signal(barrier, inc=1, device_id={"dec": (d + k) % n}, device_id_type=MESH)
    pl.semaphore_wait(barrier, n - 1)

    def copy(k, slot):
        return pltpu.make_async_remote_copy(
            src_ref=row_ref,
            dst_ref=all_ref.at[slot],
            send_sem=send_sem.at[k],
            recv_sem=recv_sem.at[slot],
            device_id={"dec": (d + k) % n},
            device_id_type=MESH,
        )

    for k in range(1, n):
        copy(k, d).start()
    all_ref[d] = row_ref[...]

    bf16, f32 = jnp.bfloat16, jnp.float32
    oi = lax.broadcasted_iota(jnp.int32, (128, 128), 0)
    oj = lax.broadcasted_iota(jnp.int32, (128, 128), 1)
    gi = lax.broadcasted_iota(jnp.int32, (16, 16), 0)
    gj = lax.broadcasted_iota(jnp.int32, (16, 16), 1)
    owner_groups = (lambda o: o >> 1, lambda o: o & 0x4E, lambda o: o & 0x0C, lambda o: o & 0)
    row_groups = (lambda g: g & 0, lambda g: g >> 3, lambda g: g & 14, lambda g: g)

    for k in range(1, n):
        copy(k, (d + n - k) % n).wait_recv()
    packed = jnp.concatenate([all_ref[g, 0:1, :] for g in range(n)], axis=0)
    o = lax.broadcasted_iota(jnp.int32, (16, 128), 1)
    g = lax.broadcasted_iota(jnp.int32, (16, 128), 0)
    g_zlo = (g >> 1) & 1
    asked = [
        [jnp.max(flag((packed == s) & (g_zlo == b)), axis=0, keepdims=True) for s in range(8)] for b in range(2)
    ]
    by_slot = [jnp.maximum(p, q) for p, q in zip(*asked)]
    wants = (
        jnp.concatenate(by_slot + [jnp.zeros((8, 128), f32)], axis=0).astype(bf16),
        jnp.concatenate(asked[0] + asked[1], axis=0).astype(bf16),
        flag(packed >= 0, bf16),
        flag(packed >= 0, bf16),
    )

    ranks, counts = [], []
    for want, owner, row in zip(wants, owner_groups, row_groups):
        same = owner(oi) == owner(oj)
        before = jnp.dot(want, flag(same & (oi < oj), bf16), preferred_element_type=f32)
        total = jnp.dot(want, flag(same, bf16), preferred_element_type=f32)
        side = row(gi) == row(gj)
        rank = jnp.dot(flag(side, bf16), before.astype(bf16), preferred_element_type=f32)
        rank += jnp.dot(flag(side & (gj < gi), bf16), want, preferred_element_type=f32)
        ranks.append(rank.astype(jnp.int32))
        counts.append(jnp.dot(flag(side, bf16), total.astype(bf16), preferred_element_type=f32).astype(jnp.int32))

    rank_y = jnp.concatenate([ranks[0][0:8], ranks[0][0:8]], axis=0)
    rank_z = jnp.zeros((16, 128), jnp.int32)
    for s in range(8):
        row = jnp.where(g_zlo == 1, ranks[1][8 + s : 9 + s, :], ranks[1][s : s + 1, :])
        rank_z = jnp.where(packed == s, row, rank_z)

    o_x, o_y, o_z, o_c = (o >> 2) & 3, (o >> 4) & 3, ((o >> 6) << 1) | ((o >> 1) & 1), o & 1
    zlo = z % 2
    places = (
        (o_x == x) & (o_y == y) & (o_z == z),
        (o_x == x) & (o_z == z),
        (o_x == x) & (g_zlo == zlo),
        (g >> 1) == x * 2 + zlo,
    )
    mine = [(want.astype(f32) > 0) & place for want, place in zip(wants, places)]
    values = (
        o_c * 8 + g,
        o_y * CAP_Y + rank_y,
        o_z * CAP_Z + rank_z,
        o_x * CAP_X + ranks[2],
    )
    lists = (
        (range(8),),
        (range(8), range(8, 16)),
        [[r for r in range(16) if r >> 2 == b] for b in range(4)],
        [[r for r in range(16) if r & 1 == b] for b in range(2)],
    )
    place = lax.broadcasted_iota(jnp.int32, (CTXP, 128), 0)
    lane = lax.broadcasted_iota(jnp.int32, (CTXP, 128), 1)
    table = jnp.zeros((CTXP, 128), jnp.int32)
    column = 0
    for stage in range(4):
        rank = jnp.where(mine[stage], ranks[stage], -1)
        for rows in lists[stage]:
            found = jnp.zeros((CTXP, 128), jnp.int32)
            for r in rows:
                found += jnp.where(rank[r : r + 1, :] == place, values[stage][r : r + 1, :], 0)
            found = jnp.sum(found.astype(f32), axis=1, keepdims=True).astype(jnp.int32)
            table = jnp.where(lane == column, found, table)
            column += 1
    live = packed >= 0
    held = jnp.sum(flag(live & (g == d))).astype(jnp.int32)
    over = jnp.maximum(
        jnp.maximum(jnp.max(counts[0]) - CAP_Y, jnp.max(counts[1]) - CAP_Z), jnp.max(counts[2]) - CAP_X
    )
    for c in range(2):
        size = jnp.sum(flag(live & (g == (d // 2) * 2 + c))).astype(jnp.int32)
        table = jnp.where((lane == 7 + c) & (place >= size), table[0:1, :], table)
    table = jnp.where(lane == 9, held, table)
    table = jnp.where(lane == 10, jnp.maximum(over, 0), table)
    square = jnp.concatenate([table.astype(f32), jnp.zeros((128 - CTXP, 128), f32)], axis=0)
    tab_ref[...] = jnp.transpose(square)[:LISTS, :].astype(jnp.int32)
    for k in range(1, n):
        copy(k, d).wait_send()


def make_table(cache_slot, cache_live):
    row = jnp.where(cache_live[0, :, 0] == 1, cache_slot[0, :, 0], -1)
    row = jnp.broadcast_to(row[None, :], (8, 128))
    vmem = pl.BlockSpec(memory_space=pltpu.VMEM)
    return pl.pallas_call(
        table_kernel,
        out_shape=jax.ShapeDtypeStruct((LISTS, 128), jnp.int32),
        in_specs=[vmem],
        out_specs=vmem,
        scratch_shapes=[
            pltpu.VMEM((16, 8, 128), jnp.int32),
            pltpu.SemaphoreType.DMA((16,)),
            pltpu.SemaphoreType.DMA((16,)),
        ],
        compiler_params=pltpu.CompilerParams(collective_id=0, has_side_effects=True),
    )(row)


QUARTERS = 4
NCH = 2 * QUARTERS
ROWS = 16
BLOCK = 2 * CTXP * ROWS


class Exchange:
    def __init__(self, tab, pool, span, pages, kv, refs, sems):
        self.tab, self.pool, self.span, self.pages, self.kv = tab, pool, span, pages, kv
        (self.pool16, self.send_y, self.recv_y, self.send_z, self.recv_z, self.send_x, self.recv_x, self.send_c,
         self.span_pad, self.send_n, self.recv_n) = refs
        self.sems = sems
        self.t, self.d, self.y, self.z, self.x, self.core = coords()

    def barrier(self):
        t, d = self.t, self.d
        sem = pltpu.get_barrier_semaphore()
        for device in [self.peer("c", 1)] + [self.peer(a, k) for a in "yzx" for k in (1, 2, 3)]:
            pl.semaphore_signal(sem, inc=1, device_id=device, device_id_type=MESH)

        zlo = self.z % 2

        @pl.loop(0, 16)
        def _(n):
            device = {"tp": n // 2, "dec": self.x * 4 + (t % 2) * 2 + n % 2}

            @pl.when((n // 2 != t) | (device["dec"] != d))
            def _():
                pl.semaphore_signal(sem, inc=1, device_id=device, device_id_type=MESH)

        pl.semaphore_wait(sem, 26 - jnp.where(t % 2 == zlo, 1, 0))

    def peer(self, axis, k):
        t, d, y, z, x, c = self.t, self.d, self.y, self.z, self.x, self.core
        if axis == "c":
            c = 1 - c
        elif axis == "y":
            y = (y + k) % 4
        elif axis == "z":
            z = (z + k) % 4
        else:
            x = (x + k) % 4
        return {"tp": (z // 2) * 4 + y, "dec": x * 4 + (z % 2) * 2 + c}

    def remote(self, src, dst, send_sem, recv_sem, device):
        return pltpu.make_async_remote_copy(
            src_ref=src, dst_ref=dst, send_sem=send_sem, recv_sem=recv_sem, device_id=device, device_id_type=MESH
        )

    def pool_own(self, half):
        rows = pl.ds(self.core * 64 + half * ROWS, ROWS)
        return pltpu.make_async_copy(
            self.pool.at[:, rows, :], self.pool16[half].at[pl.ds(self.core * 8, 8)], self.sems["own"].at[half]
        )

    def pool_pair(self, half, into):
        rows = pl.ds((1 - self.core) * 64 + half * ROWS, ROWS)
        return self.remote(
            self.pool.at[:, rows, :],
            self.pool16[half].at[pl.ds(into * 8, 8)],
            self.sems["pair_send"].at[half],
            self.sems["pair_recv"].at[half],
            self.peer("c", 1),
        )

    def start_pool(self):
        for half in range(QUARTERS):
            self.pool_pair(half, self.core).start()

    def wait_pool(self, half):
        self.pool_own(half).wait()
        self.pool_pair(half, 1 - self.core).wait_recv()

    def hop(self, axis, ch, k, source):
        send, recv, stage = {
            "y": (self.send_y, self.recv_y, 0), "z": (self.send_z, self.recv_z, 1), "x": (self.send_x, self.recv_x, 2),
        }[axis]
        units = send.shape[2]
        return self.remote(
            send.at[ch, k - 1],
            recv[ch].at[pl.ds(source * units, units)],
            self.sems["send"].at[stage, ch, k - 1],
            self.sems["recv"].at[stage, ch, k - 1],
            self.peer(axis, k),
        )

    def start_hop(self, axis, ch):
        for k in (1, 2, 3):
            self.hop(axis, ch, k, getattr(self, axis)).start()

    def wait_hop(self, axis, ch):
        me = getattr(self, axis)
        for k in (1, 2, 3):
            self.hop(axis, ch, k, (me + 4 - k) % 4).wait_recv()

    def pack_y(self, ch):
        half, kv = ch // 2, ch % 2

        @pl.loop(0, CAP_Y, unroll=True)
        def _(n):
            slot = self.tab[0, n]
            for k in range(4):
                to = (self.y + k) % 4
                for zhi in range(2):
                    col = pl.multiple_of((zhi * 4 + to) * 256 + kv * HD, HD)
                    block = self.pool16[half][slot, :, pl.ds(col, HD)]
                    if k == 0:
                        self.recv_y[ch][self.y * (2 * CAP_Y) + n * 2 + zhi] = block
                    else:
                        self.send_y[ch, k - 1, n * 2 + zhi] = block

        self.start_hop("y", ch)

    def pack_z(self, ch):
        self.wait_hop("y", ch)

        @pl.loop(0, CAP_Z, unroll=True)
        def _(n):
            for k in range(4):
                to = (self.z + k) % 4
                block = self.recv_y[ch][self.tab[1 + to % 2, n] * 2 + to // 2]
                if k == 0:
                    self.recv_z[ch][self.z * CAP_Z + n] = block
                else:
                    self.send_z[ch, k - 1, n] = block

        self.start_hop("z", ch)

    def pack_x(self, ch):
        self.wait_hop("z", ch)

        @pl.loop(0, CAP_X, unroll=True)
        def _(n):
            for k in range(4):
                to = (self.x + k) % 4
                block = self.recv_z[ch][self.tab[3 + to, n]]
                if k == 0:
                    self.recv_x[ch][self.x * CAP_X + n] = block
                else:
                    self.send_x[ch, k - 1, n] = block

        self.start_hop("x", ch)

    def last(self, ch, lane):
        return self.remote(
            self.send_c.at[ch],
            self.kv.at[ch, pl.ds(lane * CTXP * ROWS, CTXP * ROWS)],
            self.sems["last_send"].at[ch],
            self.sems["last_recv"].at[ch],
            self.peer("c", 1),
        )

    def pack_c(self, ch):
        self.wait_hop("x", ch)

        @pl.loop(0, CTXP, unroll=True)
        def _(n):
            rows = pl.ds(pl.multiple_of(n * ROWS, ROWS), ROWS)
            own = pl.ds(pl.multiple_of((self.core * CTXP + n) * ROWS, ROWS), ROWS)
            self.kv[ch, own, :] = self.recv_x[ch][self.tab[7 + self.core, n]]
            self.send_c[ch, rows, :] = self.recv_x[ch][self.tab[8 - self.core, n]]

        self.last(ch, self.core).start()

    def wait_last(self, ch):
        self.last(ch, 1 - self.core).wait_recv()

    def new_hop(self, k, source):
        return self.remote(
            self.send_n.at[k - 1],
            self.recv_n.at[source],
            self.sems["new_send"].at[k - 1],
            self.sems["new_recv"].at[k - 1],
            self.peer("x", k),
        )

    def start_new(self, dest):
        self.span_pad[0:6] = self.span[...].reshape(6, PAGE, 256)
        self.span_pad[6] = jnp.zeros((PAGE, 256), jnp.bfloat16)
        for k in range(4):
            for j in range(4):
                column = ((self.x + k) % 4) * 4 + j
                page = jnp.int32(6)
                for p in range(6):
                    page = jnp.where(dest[p] == column, p, page)
                if k == 0:
                    self.recv_n[self.x, j] = self.span_pad[page]
                else:
                    self.send_n[k - 1, j] = self.span_pad[page]
        for k in (1, 2, 3):
            self.new_hop(k, self.x).start()

    def new_page(self, n, owner_t, owner_d, core, t):
        cols = pl.ds(pl.multiple_of(t * 256, 256), 256)
        return self.remote(
            self.recv_n.at[n // 4, n % 4],
            self.pages.at[core, :, cols],
            self.sems["page_send"].at[n],
            self.sems["page_recv"].at[core * 8 + t],
            {"tp": owner_t, "dec": owner_d},
        )

    def own_page(self, n):
        cols = pl.ds(pl.multiple_of(self.t * 256, 256), 256)
        return pltpu.make_async_copy(
            self.recv_n.at[n // 4, n % 4], self.pages.at[self.core, :, cols], self.sems["page_send"].at[n]
        )

    def each_page(self, mine, other):
        @pl.loop(0, 16)
        def _(n):
            owner_t, owner_d = (n // 4) * 2 + self.z % 2, self.x * 4 + n % 4
            own = (owner_t == self.t) & (owner_d == self.d)

            @pl.when(own)
            def _():
                mine(self.own_page(n))

            @pl.when(jnp.logical_not(own))
            def _():
                other(self.new_page(n, owner_t, owner_d, self.core, self.t))

    def forward_new(self):
        for k in (1, 2, 3):
            self.new_hop(k, (self.x + 4 - k) % 4).wait_recv()
        self.each_page(lambda copy: copy.start(), lambda copy: copy.start())

    def wait_new(self):
        self.each_page(lambda copy: copy.wait(), lambda copy: copy.wait_send())
        block = (self.t // 2) * 4 + self.d % 4

        @pl.loop(0, 16)
        def _(n):
            sender_t, core = n // 2, n % 2
            sender_d = self.x * 4 + (self.t % 2) * 2 + core

            @pl.when((sender_t != self.t) | (sender_d != self.d))
            def _():
                self.new_page(block, sender_t, sender_d, core, sender_t).wait_recv()

        for k in (1, 2, 3):
            self.new_hop(k, self.x).wait_send()

    def wait_sends(self):
        for half in range(QUARTERS):
            self.pool_pair(half, self.core).wait_send()
        for ch in range(NCH):
            for axis in "yzx":
                for k in (1, 2, 3):
                    self.hop(axis, ch, k, getattr(self, axis)).wait_send()
            self.last(ch, self.core).wait_send()


def exchange_scratch():
    bf16, vmem, dma = jnp.bfloat16, pltpu.VMEM, pltpu.SemaphoreType.DMA
    unit = (ROWS, HD)
    refs = [
        [vmem((16, ROWS, 2048), bf16) for _ in range(QUARTERS)],
        vmem((NCH, 3, 2 * CAP_Y) + unit, bf16),
        [vmem((8 * CAP_Y,) + unit, bf16) for _ in range(NCH)],
        vmem((NCH, 3, CAP_Z) + unit, bf16),
        [vmem((4 * CAP_Z,) + unit, bf16) for _ in range(NCH)],
        vmem((NCH, 3, CAP_X) + unit, bf16),
        [vmem((4 * CAP_X,) + unit, bf16) for _ in range(NCH)],
        vmem((NCH, CTXP * ROWS, HD), bf16),
        vmem((7, PAGE, 256), bf16),
        vmem((3, 4, PAGE, 256), bf16),
        vmem((4, 4, PAGE, 256), bf16),
    ]
    sems = {
        "own": dma((QUARTERS,)), "pair_send": dma((QUARTERS,)), "pair_recv": dma((QUARTERS,)), "send": dma((3, NCH, 3)),
        "recv": dma((3, NCH, 3)), "last_send": dma((NCH,)), "last_recv": dma((NCH,)), "new_send": dma((3,)),
        "new_recv": dma((3,)), "page_send": dma((16,)), "page_recv": dma((16,)),
    }
    return refs, sems


ONES = 16


class Attention:
    def __init__(self, q, s, mx, m, acc):
        self.q, self.s, self.mx, self.m, self.acc = q, s, mx, m, acc
        self.span = q.shape[0]
        self.heads = q.shape[1] // HD
        self.coef = LOG2E / math.sqrt(HD)

    def columns(self, n):
        return pl.ds(pl.multiple_of(n * HD, HD), HD)

    def product(self, k, q):
        return lax.dot_general(k, q, (((1,), (1,)), ((), ())), preferred_element_type=jnp.float32)

    def fold(self, part):
        return jnp.max(part.reshape(part.shape[0] // 8, 8, part.shape[1]), axis=0)

    def weights(self, part, top):
        return jnp.exp2((part - top) * self.coef).astype(jnp.bfloat16)

    def score(self, n, slot, k):
        q = self.q[:, self.columns(n)]
        top = None
        for start in range(0, BLOCK, KEYS):
            part = self.product(k[start : start + KEYS], q)
            self.s[slot][start : start + KEYS, :] = part
            piece = self.fold(part)
            top = piece if top is None else jnp.maximum(top, piece)
        self.mx[slot][...] = top

    def mix(self, n, slot, vt):
        top = jnp.max(self.mx[slot][...], axis=0, keepdims=True)
        old = self.m[n, 0:1, :]
        top = jnp.maximum(old, top)
        fade = jnp.exp2((old - top) * self.coef)
        self.m[n] = jnp.broadcast_to(top, (8, self.span))
        weights = [self.weights(self.s[slot][start : start + KEYS, :], top) for start in range(0, BLOCK, KEYS)]
        mixed = jnp.dot(vt[...], jnp.concatenate(weights, axis=0), preferred_element_type=jnp.float32)
        self.acc[n] = self.acc[n] * fade + mixed

    def score_span(self, n, slot, k):
        q = self.q[:, self.columns(n)]
        shape = (KEYS, KEYS)
        diagonal = lax.broadcasted_iota(jnp.int32, shape, 0) <= lax.broadcasted_iota(jnp.int32, shape, 1)
        top = None
        for start in range(0, self.span, KEYS):
            part = self.product(k[start : start + KEYS], q[start:])
            edge = jnp.where(diagonal, part[:, :KEYS], NEG)
            part = edge if start + KEYS == self.span else jnp.concatenate([edge, part[:, KEYS:]], axis=1)
            self.s[slot][start : start + KEYS, start:] = part
            piece = self.fold(part)
            if start:
                piece = jnp.concatenate([top[:, :start], jnp.maximum(top[:, start:], piece)], axis=1)
            top = piece
        self.mx[slot][...] = top

    def mix_span(self, n, slot, vt):
        top = jnp.max(self.mx[slot][...], axis=0, keepdims=True)
        self.m[n] = jnp.broadcast_to(top, (8, self.span))
        for start in range(0, self.span, KEYS):
            weights = self.weights(self.s[slot][start : start + KEYS, start:], top[:, start:])
            mixed = jnp.dot(vt[:, start : start + KEYS], weights, preferred_element_type=jnp.float32)
            if start:
                self.acc[n, :, start:] += mixed
            else:
                self.acc[n] = mixed

    def two_heads(self, pair, score, mix, k, v):
        n = pair * 2
        score(n + 1, 1, k)
        mix(n, 0, v)
        score(jnp.minimum(n + 2, self.heads - 1), 0, k)
        mix(n + 1, 1, v)

    def result(self, n):
        acc = self.acc[n]
        return jnp.transpose((acc[:HD] / acc[HD : HD + 1]).astype(jnp.bfloat16))


KEYS = 256


def attention_scratch(span, width):
    heads = width // HD
    f32 = jnp.float32
    return [
        [pltpu.VMEM((BLOCK, span), f32) for _ in range(2)],
        [pltpu.VMEM((8, span), f32) for _ in range(2)],
        pltpu.VMEM((heads, 8, span), f32),
        pltpu.VMEM((heads, HD + ONES, span), f32),
    ]


def span_values(span_ref, v_span):
    v_span[:HD, :] = jnp.transpose(span_ref[:, HD:])
    v_span[HD:, :] = jnp.ones((ONES, v_span.shape[1]), jnp.bfloat16)


def block_values(values, live, v_block):
    key = lax.broadcasted_iota(jnp.int32, (HD, BLOCK), 1) % (CTXP * ROWS)
    used = key < live * ROWS
    v_block[:HD, :] = jnp.where(used, jnp.transpose(values), 0).astype(jnp.bfloat16)
    v_block[HD:, :] = jnp.where(used[:ONES], 1.0, 0.0).astype(jnp.bfloat16)


FORWARD = 9


def fused_kernel(tab, dest, q, span, pool, out, pages, kv, v_span, v_block, done, done_sem, attn, refs, sems):
    ex = Exchange(tab, pool, span, pages, kv, refs, sems)
    at = Attention(q, *attn)
    pairs = at.heads // 2
    first_block = 10

    for quarter in range(QUARTERS):
        ex.pool_own(quarter).start()
    ex.barrier()
    ex.start_pool()
    ex.wait_pool(0)
    ex.pack_y(0)
    ex.pack_y(1)
    ex.start_new(dest)
    span_values(span, v_span)
    at.score_span(0, 0, span[:, :HD])

    def write_out(pair):
        cols = pl.ds(pl.multiple_of(pair * 2 * HD, 2 * HD), 2 * HD)
        return pltpu.make_async_copy(done.at[:, cols], out.at[:, cols], done_sem.at[pair])

    @pl.loop(0, first_block + QUARTERS * pairs)
    def _(step):
        for i in range(1, NCH + 3):

            @pl.when(step == 2 * i)
            def _(i=i):
                if i - 1 < NCH:
                    ex.pack_z(i - 1)
                if i + 1 < NCH:
                    if i % 2 == 1:
                        ex.wait_pool((i + 1) // 2)
                    ex.pack_y(i + 1)
                if i == FORWARD:
                    ex.forward_new()

            @pl.when(step == 2 * i + 1)
            def _(i=i):
                if 0 <= i - 2 < NCH:
                    ex.pack_x(i - 2)
                if 0 <= i - 3 < NCH:
                    ex.pack_c(i - 3)

        @pl.when(step < pairs)
        def _():
            at.two_heads(step, at.score_span, at.mix_span, span[:, :HD], v_span)

        for b in range(QUARTERS):

            @pl.when(step == first_block + b * pairs)
            def _(b=b):
                ex.wait_last(2 * b)
                ex.wait_last(2 * b + 1)
                block_values(kv[2 * b + 1], tab[9, 0], v_block)
                at.score(0, 0, kv[2 * b])

        @pl.when(step >= first_block)
        def _():
            e = step - first_block
            at.two_heads(e % pairs, at.score, at.mix, kv[(e // pairs) * 2], v_block)

        @pl.when(step >= first_block + (QUARTERS - 1) * pairs)
        def _():
            pair = (step - first_block) % pairs
            for n in range(2):
                done[:, at.columns(pair * 2 + n)] = at.result(pair * 2 + n)
            write_out(pair).start()

    for pair in range(pairs):
        write_out(pair).wait()
    ex.wait_new()
    ex.wait_sends()


VMEM_MIB = 56


def fused(table, dest, queries, span, pool):
    refs, sems = exchange_scratch()
    vmem = pl.BlockSpec(memory_space=pltpu.VMEM)
    smem = pl.BlockSpec(memory_space=pltpu.SMEM)
    hbm = pl.BlockSpec(memory_space=pl.ANY)
    bf16 = jnp.bfloat16
    rows, width = queries.shape
    return pl.pallas_call(
        fused_kernel,
        out_shape=[jax.ShapeDtypeStruct((rows, width), bf16), jax.ShapeDtypeStruct((2, PAGE, 2048), bf16)],
        in_specs=[smem, smem, vmem, vmem, hbm],
        out_specs=[hbm, hbm],
        scratch_shapes=[
            pltpu.VMEM((NCH, BLOCK, HD), bf16),
            pltpu.VMEM((HD + ONES, rows), bf16),
            pltpu.VMEM((HD + ONES, BLOCK), bf16),
            pltpu.VMEM((rows, width), bf16),
            pltpu.SemaphoreType.DMA((width // HD // 2,)),
            attention_scratch(rows, width),
            refs,
            sems,
        ],
        compiler_params=pltpu.CompilerParams(
            collective_id=1, has_side_effects=True, vmem_limit_bytes=VMEM_MIB * 1024 * 1024
        ),
    )(table, dest, queries, span, pool)


def attend_kernel(tab, q, span, kv, out, v_span, v_block, attn):
    at = Attention(q, *attn)
    pairs = at.heads // 2
    span_values(span, v_span)
    at.score_span(0, 0, span[:, :HD])

    @pl.loop(0, pairs)
    def _(pair):
        at.two_heads(pair, at.score_span, at.mix_span, span[:, :HD], v_span)

    @pl.loop(0, QUARTERS)
    def _(b):
        block_values(kv[2 * b + 1], tab[9, 0], v_block)
        at.score(0, 0, kv[2 * b])

        @pl.loop(0, pairs)
        def _(pair):
            at.two_heads(pair, at.score, at.mix, kv[2 * b], v_block)

    @pl.loop(0, at.heads)
    def _(n):
        out[:, at.columns(n)] = at.result(n)


def attend(table, queries, span, kv):
    rows, width = queries.shape
    vmem = pl.BlockSpec(memory_space=pltpu.VMEM)
    smem = pl.BlockSpec(memory_space=pltpu.SMEM)
    return pl.pallas_call(
        attend_kernel,
        out_shape=jax.ShapeDtypeStruct((rows, width), jnp.bfloat16),
        in_specs=[smem, vmem, vmem, vmem],
        out_specs=vmem,
        scratch_shapes=[
            pltpu.VMEM((HD + ONES, rows), jnp.bfloat16),
            pltpu.VMEM((HD + ONES, BLOCK), jnp.bfloat16),
            attention_scratch(rows, width),
        ],
        compiler_params=pltpu.CompilerParams(vmem_limit_bytes=48 * 1024 * 1024),
    )(table, queries, span, kv)


def dense(table, dest, queries, span, pool, slots, flags):
    tp_size, dec_size = lax.axis_size("tp"), lax.axis_size("dec")
    devices = tp_size * dec_size
    width = span.shape[1]
    view = pool.reshape(pool.shape[0], PAGE, tp_size, width)
    source_rows = (jnp.arange(devices, dtype=jnp.int32) // dec_size)[:, None]
    axes = ("tp", "dec")
    asked = lax.all_to_all(slots, axes, split_axis=0, concat_axis=0, tiled=True)
    fetched = lax.all_to_all(view[asked, :, source_rows], axes, split_axis=0, concat_axis=0, tiled=True)
    live_index, live_count = compact_slots(flags)
    live_index = jnp.where(jnp.arange(CTXP) < live_count, live_index, live_index[0])
    cached = fetched.reshape(devices, PAGE, width)[live_index]
    cached = cached.reshape(CTXP, 2, QUARTERS, ROWS, 2, HD)
    cached = jnp.transpose(cached, (2, 4, 1, 0, 3, 5)).reshape(NCH, BLOCK, HD)
    new_pages = span.reshape(-1, PAGE, width)
    chosen = (dest[None, :] == jnp.arange(dec_size, dtype=jnp.int32)[:, None]).astype(jnp.bfloat16)
    outgoing = jnp.einsum("dp,pkc->dkc", chosen, new_pages, preferred_element_type=jnp.float32).astype(jnp.bfloat16)
    placed = lax.all_to_all(outgoing, "dec", split_axis=0, concat_axis=0, tiled=True)
    placed = lax.all_to_all(placed, "tp", split_axis=0, concat_axis=2, tiled=True)
    return (attend(table, queries, span, cached), placed)


def body(queries, span_kv, page_pool, cache_slot, cache_live, span_dest):
    table = make_table(cache_slot, cache_live)
    attn_out, placed = lax.cond(
        table[10, 0] > 0,
        lambda *a: dense(*a),
        lambda tab, dest, q, span, pool, slots, flags: tuple(fused(tab, dest, q, span, pool)),
        table, span_dest[0], queries[0], span_kv[0], page_pool, cache_slot[0], cache_live[0],
    )
    return (attn_out[None], placed)


def solution(mesh):
    in_specs = (
        P("dec", None, "tp"),
        P("dec", None, "tp"),
        P(("tp", "dec"), None, None),
        P("dec", None, None),
        P("dec", None, None),
        P("dec", None),
    )
    out_specs = (P("dec", None, "tp"), P(("tp", "dec"), None, None))
    return jax.shard_map(body, mesh=mesh, in_specs=in_specs, out_specs=out_specs, check_vma=False)
```

```python
import functools
import math

import jax
import jax.numpy as jnp
from jax import lax
from jax.experimental import pallas as pl
from jax.experimental.pallas import tpu as pltpu
from jax.sharding import PartitionSpec as P

HD = 128
PAGE = 128
CTXP = 32
LOG2E = 1.4426950408889634
NEG = -1e30


def compact_slots(live_flags):
    flat_live = live_flags.reshape(-1)
    live_rank = jnp.cumsum(flat_live) - 1
    slot_ids = jnp.arange(flat_live.shape[0], dtype=jnp.int32)
    targets = jnp.arange(CTXP, dtype=jnp.int32)
    select_table = (flat_live[None, :] == 1) & (live_rank[None, :] == targets[:, None])
    live_index = jnp.sum(jnp.where(select_table, slot_ids[None, :], 0), axis=1)
    return (live_index, jnp.sum(flat_live))


MESH = pl.DeviceIdType.MESH
CAP_Y, CAP_Z, CAP_X = 13, 25, 26


def coords():
    t, d = lax.axis_index("tp"), lax.axis_index("dec")
    return t, d, t % 4, (t // 4) * 2 + (d // 2) % 2, d // 4, d % 2


def flag(cond, dtype=jnp.float32):
    return jnp.where(cond, 1.0, 0.0).astype(dtype)


def route(packed):
    t, d, y, z, x, core = coords()
    bf16, f32 = jnp.bfloat16, jnp.float32
    oi = lax.broadcasted_iota(jnp.int32, (128, 128), 0)
    oj = lax.broadcasted_iota(jnp.int32, (128, 128), 1)
    gi = lax.broadcasted_iota(jnp.int32, (16, 16), 0)
    gj = lax.broadcasted_iota(jnp.int32, (16, 16), 1)
    owner_groups = (lambda o: o >> 1, lambda o: o & 0x4E, lambda o: o & 0x0C, lambda o: o & 0)
    row_groups = (lambda g: g & 0, lambda g: g >> 3, lambda g: g & 14, lambda g: g)

    o = lax.broadcasted_iota(jnp.int32, (16, 128), 1)
    g = lax.broadcasted_iota(jnp.int32, (16, 128), 0)
    g_zlo = (g >> 1) & 1
    asked = [
        [jnp.max(flag((packed == s) & (g_zlo == b)), axis=0, keepdims=True) for s in range(8)] for b in range(2)
    ]
    by_slot = [jnp.maximum(p, q) for p, q in zip(*asked)]
    wants = (
        jnp.concatenate(by_slot + [jnp.zeros((8, 128), f32)], axis=0).astype(bf16),
        jnp.concatenate(asked[0] + asked[1], axis=0).astype(bf16),
        flag(packed >= 0, bf16),
        flag(packed >= 0, bf16),
    )

    ranks, counts = [], []
    for want, owner, row in zip(wants, owner_groups, row_groups):
        same = owner(oi) == owner(oj)
        before = jnp.dot(want, flag(same & (oi < oj), bf16), preferred_element_type=f32)
        total = jnp.dot(want, flag(same, bf16), preferred_element_type=f32)
        side = row(gi) == row(gj)
        rank = jnp.dot(flag(side, bf16), before.astype(bf16), preferred_element_type=f32)
        rank += jnp.dot(flag(side & (gj < gi), bf16), want, preferred_element_type=f32)
        ranks.append(rank.astype(jnp.int32))
        counts.append(jnp.dot(flag(side, bf16), total.astype(bf16), preferred_element_type=f32).astype(jnp.int32))

    rank_y = jnp.concatenate([ranks[0][0:8], ranks[0][0:8]], axis=0)
    rank_z = jnp.zeros((16, 128), jnp.int32)
    for s in range(8):
        row = jnp.where(g_zlo == 1, ranks[1][8 + s : 9 + s, :], ranks[1][s : s + 1, :])
        rank_z = jnp.where(packed == s, row, rank_z)

    o_x, o_y, o_z, o_c = (o >> 2) & 3, (o >> 4) & 3, ((o >> 6) << 1) | ((o >> 1) & 1), o & 1
    zlo = z % 2
    places = (
        (o_x == x) & (o_y == y) & (o_z == z),
        (o_x == x) & (o_z == z),
        (o_x == x) & (g_zlo == zlo),
        (g >> 1) == x * 2 + zlo,
    )
    mine = [(want.astype(f32) > 0) & place for want, place in zip(wants, places)]
    values = (
        o_c * 8 + g,
        o_y * CAP_Y + jnp.minimum(rank_y, CAP_Y - 1),
        o_z * CAP_Z + jnp.minimum(rank_z, CAP_Z - 1),
        o_x * CAP_X + jnp.minimum(ranks[2], CAP_X - 1),
    )
    lists = (
        (range(8),),
        (range(8), range(8, 16)),
        [[r for r in range(16) if r >> 2 == b] for b in range(4)],
        [[r for r in range(16) if r & 1 == b] for b in range(2)],
    )
    place = lax.broadcasted_iota(jnp.int32, (CTXP, 128), 0)
    lane = lax.broadcasted_iota(jnp.int32, (CTXP, 128), 1)
    table = jnp.zeros((CTXP, 128), jnp.int32)
    column = 0
    for stage in range(4):
        rank = jnp.where(mine[stage], ranks[stage], -1)
        for rows in lists[stage]:
            found = jnp.zeros((CTXP, 128), jnp.int32)
            for r in rows:
                found += jnp.where(rank[r : r + 1, :] == place, values[stage][r : r + 1, :], 0)
            found = jnp.sum(found.astype(f32), axis=1, keepdims=True).astype(jnp.int32)
            table = jnp.where(lane == column, found, table)
            column += 1
    live = packed >= 0
    held = jnp.sum(flag(live & (g == d))).astype(jnp.int32)
    over = jnp.maximum(
        jnp.maximum(jnp.max(counts[0]) - CAP_Y, jnp.max(counts[1]) - CAP_Z), jnp.max(counts[2]) - CAP_X
    )
    for c in range(2):
        size = jnp.sum(flag(live & (g == (d // 2) * 2 + c))).astype(jnp.int32)
        table = jnp.where((lane == 7 + c) & (place >= size), table[0:1, :], table)
    table = jnp.where(lane == 9, held, table)
    return table, over


QUARTERS = 4
NCH = 2 * QUARTERS
ROWS = 16
BLOCK = 2 * CTXP * ROWS


class Exchange:
    def __init__(self, tab, pool, span, pages, kv, refs, sems):
        self.tab, self.pool, self.span, self.pages, self.kv = tab, pool, span, pages, kv
        (self.pool16, self.send_y, self.recv_y, self.send_z, self.recv_z, self.send_x, self.recv_x, self.send_c,
         self.span_pad, self.send_n, self.recv_n, self.row, self.rows) = refs
        self.sems = sems
        self.t, self.d, self.y, self.z, self.x, self.core = coords()

    def barrier(self):
        t, d = self.t, self.d
        sem = pltpu.get_barrier_semaphore()
        for device in [self.peer("c", 1)] + [self.peer(a, k) for a in "yzx" for k in (1, 2, 3)]:
            pl.semaphore_signal(sem, inc=1, device_id=device, device_id_type=MESH)

        for k in range(1, 16):
            pl.semaphore_signal(sem, inc=1, device_id={"dec": (d + k) % 16}, device_id_type=MESH)
        zlo = self.z % 2

        @pl.loop(0, 16)
        def _(n):
            device = {"tp": n // 2, "dec": self.x * 4 + (t % 2) * 2 + n % 2}

            @pl.when((n // 2 != t) | (device["dec"] != d))
            def _():
                pl.semaphore_signal(sem, inc=1, device_id=device, device_id_type=MESH)

        pl.semaphore_wait(sem, 41 - jnp.where(t % 2 == zlo, 1, 0))

    def entry(self, place, column, size):
        return jnp.minimum(jnp.maximum(self.tab[place, column], 0), size - 1)

    def peer(self, axis, k):
        t, d, y, z, x, c = self.t, self.d, self.y, self.z, self.x, self.core
        if axis == "c":
            c = 1 - c
        elif axis == "y":
            y = (y + k) % 4
        elif axis == "z":
            z = (z + k) % 4
        else:
            x = (x + k) % 4
        return {"tp": (z // 2) * 4 + y, "dec": x * 4 + (z % 2) * 2 + c}

    def remote(self, src, dst, send_sem, recv_sem, device):
        return pltpu.make_async_remote_copy(
            src_ref=src, dst_ref=dst, send_sem=send_sem, recv_sem=recv_sem, device_id=device, device_id_type=MESH
        )

    def row_copy(self, k, slot):
        return self.remote(
            self.row,
            self.rows.at[slot],
            self.sems["row_send"].at[k],
            self.sems["row_recv"].at[slot],
            {"dec": (self.d + k) % 16},
        )

    def start_rows(self):
        for k in range(1, 16):
            self.row_copy(k, self.d).start()
        self.rows[self.d] = self.row[...]

    def wait_rows(self):
        for k in range(1, 16):
            self.row_copy(k, (self.d + 16 - k) % 16).wait_recv()
        return jnp.concatenate([self.rows[g, 0:1, :] for g in range(16)], axis=0)

    def pool_own(self, half):
        rows = pl.ds(self.core * 64 + half * ROWS, ROWS)
        return pltpu.make_async_copy(
            self.pool.at[:, rows, :], self.pool16[half].at[pl.ds(self.core * 8, 8)], self.sems["own"].at[half]
        )

    def pool_pair(self, half, into):
        rows = pl.ds((1 - self.core) * 64 + half * ROWS, ROWS)
        return self.remote(
            self.pool.at[:, rows, :],
            self.pool16[half].at[pl.ds(into * 8, 8)],
            self.sems["pair_send"].at[half],
            self.sems["pair_recv"].at[half],
            self.peer("c", 1),
        )

    def start_pool(self):
        for half in range(QUARTERS):
            self.pool_pair(half, self.core).start()

    def wait_pool(self, half):
        self.pool_own(half).wait()
        self.pool_pair(half, 1 - self.core).wait_recv()

    def hop(self, axis, ch, k, source):
        send, recv, stage = {
            "y": (self.send_y, self.recv_y, 0), "z": (self.send_z, self.recv_z, 1), "x": (self.send_x, self.recv_x, 2),
        }[axis]
        units = send.shape[2]
        return self.remote(
            send.at[ch, k - 1],
            recv[ch].at[pl.ds(source * units, units)],
            self.sems["send"].at[stage, ch, k - 1],
            self.sems["recv"].at[stage, ch, k - 1],
            self.peer(axis, k),
        )

    def start_hop(self, axis, ch):
        for k in (1, 2, 3):
            self.hop(axis, ch, k, getattr(self, axis)).start()

    def wait_hop(self, axis, ch):
        me = getattr(self, axis)
        for k in (1, 2, 3):
            self.hop(axis, ch, k, (me + 4 - k) % 4).wait_recv()

    def pack_y(self, ch):
        half, kv = ch // 2, ch % 2

        @pl.loop(0, CAP_Y, unroll=True)
        def _(n):
            slot = self.entry(n, 0, 16)
            for k in range(4):
                to = (self.y + k) % 4
                for zhi in range(2):
                    col = pl.multiple_of((zhi * 4 + to) * 256 + kv * HD, HD)
                    block = self.pool16[half][slot, :, pl.ds(col, HD)]
                    if k == 0:
                        self.recv_y[ch][self.y * (2 * CAP_Y) + n * 2 + zhi] = block
                    else:
                        self.send_y[ch, k - 1, n * 2 + zhi] = block

        self.start_hop("y", ch)

    def pack_z(self, ch):
        self.wait_hop("y", ch)

        @pl.loop(0, CAP_Z, unroll=True)
        def _(n):
            for k in range(4):
                to = (self.z + k) % 4
                block = self.recv_y[ch][self.entry(n, 1 + to % 2, 4 * CAP_Y) * 2 + to // 2]
                if k == 0:
                    self.recv_z[ch][self.z * CAP_Z + n] = block
                else:
                    self.send_z[ch, k - 1, n] = block

        self.start_hop("z", ch)

    def pack_x(self, ch):
        self.wait_hop("z", ch)

        @pl.loop(0, CAP_X, unroll=True)
        def _(n):
            for k in range(4):
                to = (self.x + k) % 4
                block = self.recv_z[ch][self.entry(n, 3 + to, 4 * CAP_Z)]
                if k == 0:
                    self.recv_x[ch][self.x * CAP_X + n] = block
                else:
                    self.send_x[ch, k - 1, n] = block

        self.start_hop("x", ch)

    def last(self, ch, lane):
        return self.remote(
            self.send_c.at[ch],
            self.kv.at[ch, pl.ds(lane * CTXP * ROWS, CTXP * ROWS)],
            self.sems["last_send"].at[ch],
            self.sems["last_recv"].at[ch],
            self.peer("c", 1),
        )

    def pack_c(self, ch):
        self.wait_hop("x", ch)

        @pl.loop(0, CTXP, unroll=True)
        def _(n):
            rows = pl.ds(pl.multiple_of(n * ROWS, ROWS), ROWS)
            own = pl.ds(pl.multiple_of((self.core * CTXP + n) * ROWS, ROWS), ROWS)
            self.kv[ch, own, :] = self.recv_x[ch][self.entry(n, 7 + self.core, 4 * CAP_X)]
            self.send_c[ch, rows, :] = self.recv_x[ch][self.entry(n, 8 - self.core, 4 * CAP_X)]

        self.last(ch, self.core).start()

    def wait_last(self, ch):
        self.last(ch, 1 - self.core).wait_recv()

    def new_hop(self, k, source):
        return self.remote(
            self.send_n.at[k - 1],
            self.recv_n.at[source],
            self.sems["new_send"].at[k - 1],
            self.sems["new_recv"].at[k - 1],
            self.peer("x", k),
        )

    def start_new(self, dest):
        self.span_pad[0:6] = self.span[...].reshape(6, PAGE, 256)
        self.span_pad[6] = jnp.zeros((PAGE, 256), jnp.bfloat16)
        for k in range(4):
            for j in range(4):
                column = ((self.x + k) % 4) * 4 + j
                page = jnp.int32(6)
                for p in range(6):
                    page = jnp.where(dest[p] == column, p, page)
                if k == 0:
                    self.recv_n[self.x, j] = self.span_pad[page]
                else:
                    self.send_n[k - 1, j] = self.span_pad[page]
        for k in (1, 2, 3):
            self.new_hop(k, self.x).start()

    def new_page(self, n, owner_t, owner_d, core, t):
        cols = pl.ds(pl.multiple_of(t * 256, 256), 256)
        return self.remote(
            self.recv_n.at[n // 4, n % 4],
            self.pages.at[core, :, cols],
            self.sems["page_send"].at[n],
            self.sems["page_recv"].at[core * 8 + t],
            {"tp": owner_t, "dec": owner_d},
        )

    def own_page(self, n):
        cols = pl.ds(pl.multiple_of(self.t * 256, 256), 256)
        return pltpu.make_async_copy(
            self.recv_n.at[n // 4, n % 4], self.pages.at[self.core, :, cols], self.sems["page_send"].at[n]
        )

    def each_page(self, mine, other):
        @pl.loop(0, 16)
        def _(n):
            owner_t, owner_d = (n // 4) * 2 + self.z % 2, self.x * 4 + n % 4
            own = (owner_t == self.t) & (owner_d == self.d)

            @pl.when(own)
            def _():
                mine(self.own_page(n))

            @pl.when(jnp.logical_not(own))
            def _():
                other(self.new_page(n, owner_t, owner_d, self.core, self.t))

    def forward_new(self):
        for k in (1, 2, 3):
            self.new_hop(k, (self.x + 4 - k) % 4).wait_recv()
        self.each_page(lambda copy: copy.start(), lambda copy: copy.start())

    def wait_new(self):
        self.each_page(lambda copy: copy.wait(), lambda copy: copy.wait_send())
        block = (self.t // 2) * 4 + self.d % 4

        @pl.loop(0, 16)
        def _(n):
            sender_t, core = n // 2, n % 2
            sender_d = self.x * 4 + (self.t % 2) * 2 + core

            @pl.when((sender_t != self.t) | (sender_d != self.d))
            def _():
                self.new_page(block, sender_t, sender_d, core, sender_t).wait_recv()

        for k in (1, 2, 3):
            self.new_hop(k, self.x).wait_send()

    def wait_sends(self):
        for k in range(1, 16):
            self.row_copy(k, self.d).wait_send()
        for half in range(QUARTERS):
            self.pool_pair(half, self.core).wait_send()
        for ch in range(NCH):
            for axis in "yzx":
                for k in (1, 2, 3):
                    self.hop(axis, ch, k, getattr(self, axis)).wait_send()
            self.last(ch, self.core).wait_send()


def exchange_scratch():
    bf16, vmem, dma = jnp.bfloat16, pltpu.VMEM, pltpu.SemaphoreType.DMA
    unit = (ROWS, HD)
    refs = [
        [vmem((16, ROWS, 2048), bf16) for _ in range(QUARTERS)],
        vmem((NCH, 3, 2 * CAP_Y) + unit, bf16),
        [vmem((8 * CAP_Y,) + unit, bf16) for _ in range(NCH)],
        vmem((NCH, 3, CAP_Z) + unit, bf16),
        [vmem((4 * CAP_Z,) + unit, bf16) for _ in range(NCH)],
        vmem((NCH, 3, CAP_X) + unit, bf16),
        [vmem((4 * CAP_X,) + unit, bf16) for _ in range(NCH)],
        vmem((NCH, CTXP * ROWS, HD), bf16),
        vmem((7, PAGE, 256), bf16),
        vmem((3, 4, PAGE, 256), bf16),
        vmem((4, 4, PAGE, 256), bf16),
        vmem((8, 128), jnp.int32),
        vmem((16, 8, 128), jnp.int32),
    ]
    sems = {
        "own": dma((QUARTERS,)), "pair_send": dma((QUARTERS,)), "pair_recv": dma((QUARTERS,)), "send": dma((3, NCH, 3)),
        "recv": dma((3, NCH, 3)), "last_send": dma((NCH,)), "last_recv": dma((NCH,)), "new_send": dma((3,)),
        "new_recv": dma((3,)), "page_send": dma((16,)), "page_recv": dma((16,)),
        "row_send": dma((16,)), "row_recv": dma((16,)), "table": dma((1,)),
    }
    return refs, sems


ONES = 16


class Attention:
    def __init__(self, q, s, mx, m, acc):
        self.q, self.s, self.mx, self.m, self.acc = q, s, mx, m, acc
        self.span = q.shape[0]
        self.heads = q.shape[1] // HD
        self.coef = LOG2E / math.sqrt(HD)

    def columns(self, n):
        return pl.ds(pl.multiple_of(n * HD, HD), HD)

    def product(self, k, q):
        return lax.dot_general(k, q, (((1,), (1,)), ((), ())), preferred_element_type=jnp.float32)

    def fold(self, part):
        return jnp.max(part.reshape(part.shape[0] // 8, 8, part.shape[1]), axis=0)

    def weights(self, part, top):
        return jnp.exp2((part - top) * self.coef).astype(jnp.bfloat16)

    def score(self, n, slot, k):
        q = self.q[:, self.columns(n)]
        top = None
        for start in range(0, BLOCK, KEYS):
            part = self.product(k[start : start + KEYS], q)
            self.s[slot][start : start + KEYS, :] = part
            piece = self.fold(part)
            top = piece if top is None else jnp.maximum(top, piece)
        self.mx[slot][...] = top

    def mix(self, n, slot, vt):
        top = jnp.max(self.mx[slot][...], axis=0, keepdims=True)
        old = self.m[n, 0:1, :]
        top = jnp.maximum(old, top)
        fade = jnp.exp2((old - top) * self.coef)
        self.m[n] = jnp.broadcast_to(top, (8, self.span))
        weights = [self.weights(self.s[slot][start : start + KEYS, :], top) for start in range(0, BLOCK, KEYS)]
        mixed = jnp.dot(vt[...], jnp.concatenate(weights, axis=0), preferred_element_type=jnp.float32)
        self.acc[n] = self.acc[n] * fade + mixed

    def score_span(self, n, slot, k):
        q = self.q[:, self.columns(n)]
        shape = (KEYS, KEYS)
        diagonal = lax.broadcasted_iota(jnp.int32, shape, 0) <= lax.broadcasted_iota(jnp.int32, shape, 1)
        top = None
        for start in range(0, self.span, KEYS):
            part = self.product(k[start : start + KEYS], q[start:])
            edge = jnp.where(diagonal, part[:, :KEYS], NEG)
            part = edge if start + KEYS == self.span else jnp.concatenate([edge, part[:, KEYS:]], axis=1)
            self.s[slot][start : start + KEYS, start:] = part
            piece = self.fold(part)
            if start:
                piece = jnp.concatenate([top[:, :start], jnp.maximum(top[:, start:], piece)], axis=1)
            top = piece
        self.mx[slot][...] = top

    def mix_span(self, n, slot, vt):
        top = jnp.max(self.mx[slot][...], axis=0, keepdims=True)
        self.m[n] = jnp.broadcast_to(top, (8, self.span))
        for start in range(0, self.span, KEYS):
            weights = self.weights(self.s[slot][start : start + KEYS, start:], top[:, start:])
            mixed = jnp.dot(vt[:, start : start + KEYS], weights, preferred_element_type=jnp.float32)
            if start:
                self.acc[n, :, start:] += mixed
            else:
                self.acc[n] = mixed

    def two_heads(self, pair, score, mix, k, v):
        n = pair * 2
        score(n + 1, 1, k)
        mix(n, 0, v)
        score(jnp.minimum(n + 2, self.heads - 1), 0, k)
        mix(n + 1, 1, v)

    def result(self, n):
        acc = self.acc[n]
        return jnp.transpose((acc[:HD] / acc[HD : HD + 1]).astype(jnp.bfloat16))


KEYS = 256


def attention_scratch(span, width):
    heads = width // HD
    f32 = jnp.float32
    return [
        [pltpu.VMEM((BLOCK, span), f32) for _ in range(2)],
        [pltpu.VMEM((8, span), f32) for _ in range(2)],
        pltpu.VMEM((heads, 8, span), f32),
        pltpu.VMEM((heads, HD + ONES, span), f32),
    ]


def span_values(span_ref, v_span):
    v_span[:HD, :] = jnp.transpose(span_ref[:, HD:])
    v_span[HD:, :] = jnp.ones((ONES, v_span.shape[1]), jnp.bfloat16)


def block_values(values, live, v_block):
    key = lax.broadcasted_iota(jnp.int32, (HD, BLOCK), 1) % (CTXP * ROWS)
    used = key < live * ROWS
    v_block[:HD, :] = jnp.where(used, jnp.transpose(values), 0).astype(jnp.bfloat16)
    v_block[HD:, :] = jnp.where(used[:ONES], 1.0, 0.0).astype(jnp.bfloat16)


FORWARD = 9


def fused_kernel(
    dest, slots, flags, q, span, pool, out, pages, over, kv, v_span, v_block, done, done_sem, tab, tab_made, attn, refs, sems
):
    ex = Exchange(tab, pool, span, pages, kv, refs, sems)
    at = Attention(q, *attn)
    pairs = at.heads // 2
    first_block = 10

    for quarter in range(QUARTERS):
        ex.pool_own(quarter).start()
    ex.row[...] = jnp.broadcast_to(jnp.where(flags[...] == 1, slots[...], -1), ex.row.shape)
    ex.barrier()
    ex.start_rows()
    ex.start_pool()
    ex.start_new(dest)
    span_values(span, v_span)
    at.score_span(0, 0, span[:, :HD])
    table, most = route(ex.wait_rows())
    over[0] = jnp.maximum(most, 0)
    tab_made[...] = table
    to_scalars = pltpu.make_async_copy(tab_made, tab, sems["table"].at[0])
    to_scalars.start()
    to_scalars.wait()
    ex.wait_pool(0)
    ex.pack_y(0)
    ex.pack_y(1)

    def write_out(pair):
        cols = pl.ds(pl.multiple_of(pair * 2 * HD, 2 * HD), 2 * HD)
        return pltpu.make_async_copy(done.at[:, cols], out.at[:, cols], done_sem.at[pair])

    @pl.loop(0, first_block + QUARTERS * pairs)
    def _(step):
        for i in range(1, NCH + 3):

            @pl.when(step == 2 * i)
            def _(i=i):
                if i - 1 < NCH:
                    ex.pack_z(i - 1)
                if i + 1 < NCH:
                    if i % 2 == 1:
                        ex.wait_pool((i + 1) // 2)
                    ex.pack_y(i + 1)
                if i == FORWARD:
                    ex.forward_new()

            @pl.when(step == 2 * i + 1)
            def _(i=i):
                if 0 <= i - 2 < NCH:
                    ex.pack_x(i - 2)
                if 0 <= i - 3 < NCH:
                    ex.pack_c(i - 3)

        @pl.when(step < pairs)
        def _():
            at.two_heads(step, at.score_span, at.mix_span, span[:, :HD], v_span)

        for b in range(QUARTERS):

            @pl.when(step == first_block + b * pairs)
            def _(b=b):
                ex.wait_last(2 * b)
                ex.wait_last(2 * b + 1)
                block_values(kv[2 * b + 1], tab[0, 9], v_block)
                at.score(0, 0, kv[2 * b])

        @pl.when(step >= first_block)
        def _():
            e = step - first_block
            at.two_heads(e % pairs, at.score, at.mix, kv[(e // pairs) * 2], v_block)

        @pl.when(step >= first_block + (QUARTERS - 1) * pairs)
        def _():
            pair = (step - first_block) % pairs
            for n in range(2):
                done[:, at.columns(pair * 2 + n)] = at.result(pair * 2 + n)
            write_out(pair).start()

    for pair in range(pairs):
        write_out(pair).wait()
    ex.wait_new()
    ex.wait_sends()


VMEM_MIB = 56


def fused(dest, slots, flags, queries, span, pool):
    refs, sems = exchange_scratch()
    vmem = pl.BlockSpec(memory_space=pltpu.VMEM)
    smem = pl.BlockSpec(memory_space=pltpu.SMEM)
    hbm = pl.BlockSpec(memory_space=pl.ANY)
    bf16 = jnp.bfloat16
    rows, width = queries.shape
    return pl.pallas_call(
        fused_kernel,
        out_shape=[
            jax.ShapeDtypeStruct((rows, width), bf16),
            jax.ShapeDtypeStruct((2, PAGE, 2048), bf16),
            jax.ShapeDtypeStruct((1,), jnp.int32),
        ],
        in_specs=[smem, vmem, vmem, vmem, vmem, hbm],
        out_specs=[hbm, hbm, smem],
        scratch_shapes=[
            pltpu.VMEM((NCH, BLOCK, HD), bf16),
            pltpu.VMEM((HD + ONES, rows), bf16),
            pltpu.VMEM((HD + ONES, BLOCK), bf16),
            pltpu.VMEM((rows, width), bf16),
            pltpu.SemaphoreType.DMA((width // HD // 2,)),
            pltpu.SMEM((CTXP, 128), jnp.int32),
            pltpu.VMEM((CTXP, 128), jnp.int32),
            attention_scratch(rows, width),
            refs,
            sems,
        ],
        compiler_params=pltpu.CompilerParams(
            collective_id=1, has_side_effects=True, vmem_limit_bytes=VMEM_MIB * 1024 * 1024
        ),
    )(dest, slots, flags, queries, span, pool)


def attend_kernel(live, q, span, kv, out, v_span, v_block, attn):
    at = Attention(q, *attn)
    pairs = at.heads // 2
    span_values(span, v_span)
    at.score_span(0, 0, span[:, :HD])

    @pl.loop(0, pairs)
    def _(pair):
        at.two_heads(pair, at.score_span, at.mix_span, span[:, :HD], v_span)

    @pl.loop(0, QUARTERS)
    def _(b):
        block_values(kv[2 * b + 1], live[0], v_block)
        at.score(0, 0, kv[2 * b])

        @pl.loop(0, pairs)
        def _(pair):
            at.two_heads(pair, at.score, at.mix, kv[2 * b], v_block)

    @pl.loop(0, at.heads)
    def _(n):
        out[:, at.columns(n)] = at.result(n)


def attend(live, queries, span, kv):
    rows, width = queries.shape
    vmem = pl.BlockSpec(memory_space=pltpu.VMEM)
    smem = pl.BlockSpec(memory_space=pltpu.SMEM)
    return pl.pallas_call(
        attend_kernel,
        out_shape=jax.ShapeDtypeStruct((rows, width), jnp.bfloat16),
        in_specs=[smem, vmem, vmem, vmem],
        out_specs=vmem,
        scratch_shapes=[
            pltpu.VMEM((HD + ONES, rows), jnp.bfloat16),
            pltpu.VMEM((HD + ONES, BLOCK), jnp.bfloat16),
            attention_scratch(rows, width),
        ],
        compiler_params=pltpu.CompilerParams(vmem_limit_bytes=48 * 1024 * 1024),
    )(live, queries, span, kv)


def dense(dest, queries, span, pool, slots, flags):
    tp_size, dec_size = lax.axis_size("tp"), lax.axis_size("dec")
    devices = tp_size * dec_size
    width = span.shape[1]
    view = pool.reshape(pool.shape[0], PAGE, tp_size, width)
    source_rows = (jnp.arange(devices, dtype=jnp.int32) // dec_size)[:, None]
    axes = ("tp", "dec")
    asked = lax.all_to_all(slots, axes, split_axis=0, concat_axis=0, tiled=True)
    fetched = lax.all_to_all(view[asked, :, source_rows], axes, split_axis=0, concat_axis=0, tiled=True)
    live_index, live_count = compact_slots(flags)
    live_index = jnp.where(jnp.arange(CTXP) < live_count, live_index, live_index[0])
    cached = fetched.reshape(devices, PAGE, width)[live_index]
    cached = cached.reshape(CTXP, 2, QUARTERS, ROWS, 2, HD)
    cached = jnp.transpose(cached, (2, 4, 1, 0, 3, 5)).reshape(NCH, BLOCK, HD)
    new_pages = span.reshape(-1, PAGE, width)
    chosen = (dest[None, :] == jnp.arange(dec_size, dtype=jnp.int32)[:, None]).astype(jnp.bfloat16)
    outgoing = jnp.einsum("dp,pkc->dkc", chosen, new_pages, preferred_element_type=jnp.float32).astype(jnp.bfloat16)
    placed = lax.all_to_all(outgoing, "dec", split_axis=0, concat_axis=0, tiled=True)
    placed = lax.all_to_all(placed, "tp", split_axis=0, concat_axis=2, tiled=True)
    return (attend(live_count.reshape(1), queries, span, cached), placed)


def body(queries, span_kv, page_pool, cache_slot, cache_live, span_dest):
    dest, q, span = span_dest[0], queries[0], span_kv[0]
    attn_out, placed, over = fused(dest, cache_slot.reshape(1, -1), cache_live.reshape(1, -1), q, span, page_pool)
    attn_out, placed = lax.cond(
        over[0] > 0,
        lambda attn, pages, *a: dense(*a),
        lambda attn, pages, *a: (attn, pages),
        attn_out, placed, dest, q, span, page_pool, cache_slot[0], cache_live[0],
    )
    return (attn_out[None], placed)


def solution(mesh):
    in_specs = (
        P("dec", None, "tp"),
        P("dec", None, "tp"),
        P(("tp", "dec"), None, None),
        P("dec", None, None),
        P("dec", None, None),
        P("dec", None),
    )
    out_specs = (P("dec", None, "tp"), P(("tp", "dec"), None, None))
    return jax.shard_map(body, mesh=mesh, in_specs=in_specs, out_specs=out_specs, check_vma=False)
```

```python
import functools
import math

import jax
import jax.numpy as jnp
from jax import lax
from jax.experimental import pallas as pl
from jax.experimental.pallas import tpu as pltpu
from jax.sharding import PartitionSpec as P

HD = 128
PAGE = 128
CTXP = 32
LOG2E = 1.4426950408889634
NEG = -1e30


def compact_slots(live_flags):
    flat_live = live_flags.reshape(-1)
    live_rank = jnp.cumsum(flat_live) - 1
    slot_ids = jnp.arange(flat_live.shape[0], dtype=jnp.int32)
    targets = jnp.arange(CTXP, dtype=jnp.int32)
    select_table = (flat_live[None, :] == 1) & (live_rank[None, :] == targets[:, None])
    live_index = jnp.sum(jnp.where(select_table, slot_ids[None, :], 0), axis=1)
    return (live_index, jnp.sum(flat_live))


MESH = pl.DeviceIdType.MESH
CAP_Y, CAP_Z, CAP_X = 13, 25, 26


def coords():
    t, d = lax.axis_index("tp"), lax.axis_index("dec")
    return t, d, t % 4, (t // 4) * 2 + (d // 2) % 2, d // 4, d % 2


def flag(cond, dtype=jnp.float32):
    return jnp.where(cond, 1.0, 0.0).astype(dtype)


def route(packed):
    t, d, y, z, x, core = coords()
    bf16, f32 = jnp.bfloat16, jnp.float32
    oi = lax.broadcasted_iota(jnp.int32, (128, 128), 0)
    oj = lax.broadcasted_iota(jnp.int32, (128, 128), 1)
    gi = lax.broadcasted_iota(jnp.int32, (16, 16), 0)
    gj = lax.broadcasted_iota(jnp.int32, (16, 16), 1)
    owner_groups = (lambda o: o >> 1, lambda o: o & 0x4E, lambda o: o & 0x0C, lambda o: o & 0)
    row_groups = (lambda g: g & 0, lambda g: g >> 3, lambda g: g & 14, lambda g: g)

    o = lax.broadcasted_iota(jnp.int32, (16, 128), 1)
    g = lax.broadcasted_iota(jnp.int32, (16, 128), 0)
    g_zlo = (g >> 1) & 1
    asked = [
        [jnp.max(flag((packed == s) & (g_zlo == b)), axis=0, keepdims=True) for s in range(8)] for b in range(2)
    ]
    by_slot = [jnp.maximum(p, q) for p, q in zip(*asked)]
    wants = (
        jnp.concatenate(by_slot + [jnp.zeros((8, 128), f32)], axis=0).astype(bf16),
        jnp.concatenate(asked[0] + asked[1], axis=0).astype(bf16),
        flag(packed >= 0, bf16),
        flag(packed >= 0, bf16),
    )

    ranks, counts = [], []
    for want, owner, row in zip(wants, owner_groups, row_groups):
        same = owner(oi) == owner(oj)
        before = jnp.dot(want, flag(same & (oi < oj), bf16), preferred_element_type=f32)
        total = jnp.dot(want, flag(same, bf16), preferred_element_type=f32)
        side = row(gi) == row(gj)
        rank = jnp.dot(flag(side, bf16), before.astype(bf16), preferred_element_type=f32)
        rank += jnp.dot(flag(side & (gj < gi), bf16), want, preferred_element_type=f32)
        ranks.append(rank.astype(jnp.int32))
        counts.append(jnp.dot(flag(side, bf16), total.astype(bf16), preferred_element_type=f32).astype(jnp.int32))

    rank_y = jnp.concatenate([ranks[0][0:8], ranks[0][0:8]], axis=0)
    rank_z = jnp.zeros((16, 128), jnp.int32)
    for s in range(8):
        row = jnp.where(g_zlo == 1, ranks[1][8 + s : 9 + s, :], ranks[1][s : s + 1, :])
        rank_z = jnp.where(packed == s, row, rank_z)

    o_x, o_y, o_z, o_c = (o >> 2) & 3, (o >> 4) & 3, ((o >> 6) << 1) | ((o >> 1) & 1), o & 1
    zlo = z % 2
    places = (
        (o_x == x) & (o_y == y) & (o_z == z),
        (o_x == x) & (o_z == z),
        (o_x == x) & (g_zlo == zlo),
        (g >> 1) == x * 2 + zlo,
    )
    mine = [(want.astype(f32) > 0) & place for want, place in zip(wants, places)]
    values = (
        o_c * 8 + g,
        o_y * CAP_Y + jnp.minimum(rank_y, CAP_Y - 1),
        o_z * CAP_Z + jnp.minimum(rank_z, CAP_Z - 1),
        o_x * CAP_X + jnp.minimum(ranks[2], CAP_X - 1),
    )
    lists = (
        (range(8),),
        (range(8), range(8, 16)),
        [[r for r in range(16) if r >> 2 == b] for b in range(4)],
        [[r for r in range(16) if r & 1 == b] for b in range(2)],
    )
    place = lax.broadcasted_iota(jnp.int32, (CTXP, 128), 0)
    lane = lax.broadcasted_iota(jnp.int32, (CTXP, 128), 1)
    table = jnp.zeros((CTXP, 128), jnp.int32)
    column = 0
    for stage in range(4):
        rank = jnp.where(mine[stage], ranks[stage], -1)
        for rows in lists[stage]:
            found = jnp.zeros((CTXP, 128), jnp.int32)
            for r in rows:
                found += jnp.where(rank[r : r + 1, :] == place, values[stage][r : r + 1, :], 0)
            found = jnp.sum(found.astype(f32), axis=1, keepdims=True).astype(jnp.int32)
            table = jnp.where(lane == column, found, table)
            column += 1
    live = packed >= 0
    held = jnp.sum(flag(live & (g == d))).astype(jnp.int32)
    over = jnp.maximum(
        jnp.maximum(jnp.max(counts[0]) - CAP_Y, jnp.max(counts[1]) - CAP_Z), jnp.max(counts[2]) - CAP_X
    )
    for c in range(2):
        size = jnp.sum(flag(live & (g == (d // 2) * 2 + c))).astype(jnp.int32)
        table = jnp.where((lane == 7 + c) & (place >= size), table[0:1, :], table)
    table = jnp.where(lane == 9, held, table)
    sizes = jnp.where(lane < 1, 16, jnp.where(lane < 3, 4 * CAP_Y, jnp.where(lane < 7, 4 * CAP_Z, 4 * CAP_X)))
    return jnp.minimum(jnp.maximum(table, 0), sizes - 1), over


QUARTERS = 4
NCH = 2 * QUARTERS
ROWS = 16
BLOCK = 2 * CTXP * ROWS


class Exchange:
    def __init__(self, tab, pool, span, pages, kv, refs, sems):
        self.tab, self.pool, self.span, self.pages, self.kv = tab, pool, span, pages, kv
        (self.pool16, self.send_y, self.recv_y, self.send_z, self.recv_z, self.send_x, self.recv_x, self.send_c,
         self.span_pad, self.send_n, self.recv_n, self.row, self.rows) = refs
        self.sems = sems
        self.t, self.d, self.y, self.z, self.x, self.core = coords()

    def barrier(self):
        t, d = self.t, self.d
        sem = pltpu.get_barrier_semaphore()
        for device in [self.peer("c", 1)] + [self.peer(a, k) for a in "yzx" for k in (1, 2, 3)]:
            pl.semaphore_signal(sem, inc=1, device_id=device, device_id_type=MESH)

        for k in range(1, 16):
            pl.semaphore_signal(sem, inc=1, device_id={"dec": (d + k) % 16}, device_id_type=MESH)
        zlo = self.z % 2

        @pl.loop(0, 16)
        def _(n):
            device = {"tp": n // 2, "dec": self.x * 4 + (t % 2) * 2 + n % 2}

            @pl.when((n // 2 != t) | (device["dec"] != d))
            def _():
                pl.semaphore_signal(sem, inc=1, device_id=device, device_id_type=MESH)

        pl.semaphore_wait(sem, 41 - jnp.where(t % 2 == zlo, 1, 0))

    def entry(self, place, column):
        return self.tab[place, column]

    def peer(self, axis, k):
        t, d, y, z, x, c = self.t, self.d, self.y, self.z, self.x, self.core
        if axis == "c":
            c = 1 - c
        elif axis == "y":
            y = (y + k) % 4
        elif axis == "z":
            z = (z + k) % 4
        else:
            x = (x + k) % 4
        return {"tp": (z // 2) * 4 + y, "dec": x * 4 + (z % 2) * 2 + c}

    def remote(self, src, dst, send_sem, recv_sem, device):
        return pltpu.make_async_remote_copy(
            src_ref=src, dst_ref=dst, send_sem=send_sem, recv_sem=recv_sem, device_id=device, device_id_type=MESH
        )

    def row_copy(self, k, slot):
        return self.remote(
            self.row,
            self.rows.at[slot],
            self.sems["row_send"].at[k],
            self.sems["row_recv"].at[slot],
            {"dec": (self.d + k) % 16},
        )

    def start_rows(self):
        for k in range(1, 16):
            self.row_copy(k, self.d).start()
        self.rows[self.d] = self.row[...]

    def wait_rows(self):
        for k in range(1, 16):
            self.row_copy(k, (self.d + 16 - k) % 16).wait_recv()
        return jnp.concatenate([self.rows[g, 0:1, :] for g in range(16)], axis=0)

    def pool_own(self, half):
        rows = pl.ds(self.core * 64 + half * ROWS, ROWS)
        return pltpu.make_async_copy(
            self.pool.at[:, rows, :], self.pool16[half].at[pl.ds(self.core * 8, 8)], self.sems["own"].at[half]
        )

    def pool_pair(self, half, into):
        rows = pl.ds((1 - self.core) * 64 + half * ROWS, ROWS)
        return self.remote(
            self.pool.at[:, rows, :],
            self.pool16[half].at[pl.ds(into * 8, 8)],
            self.sems["pair_send"].at[half],
            self.sems["pair_recv"].at[half],
            self.peer("c", 1),
        )

    def start_pool(self):
        for half in range(QUARTERS):
            self.pool_pair(half, self.core).start()

    def wait_pool(self, half):
        self.pool_own(half).wait()
        self.pool_pair(half, 1 - self.core).wait_recv()

    def hop(self, axis, ch, k, source):
        send, recv, stage = {
            "y": (self.send_y, self.recv_y, 0), "z": (self.send_z, self.recv_z, 1), "x": (self.send_x, self.recv_x, 2),
        }[axis]
        units = send.shape[2]
        return self.remote(
            send.at[ch, k - 1],
            recv[ch].at[pl.ds(source * units, units)],
            self.sems["send"].at[stage, ch, k - 1],
            self.sems["recv"].at[stage, ch, k - 1],
            self.peer(axis, k),
        )

    def start_hop(self, axis, ch):
        for k in (1, 2, 3):
            self.hop(axis, ch, k, getattr(self, axis)).start()

    def wait_hop(self, axis, ch):
        me = getattr(self, axis)
        for k in (1, 2, 3):
            self.hop(axis, ch, k, (me + 4 - k) % 4).wait_recv()

    def pack_y(self, ch):
        half, kv = ch // 2, ch % 2

        @pl.loop(0, CAP_Y, unroll=True)
        def _(n):
            slot = self.entry(n, 0)
            for k in range(4):
                to = (self.y + k) % 4
                for zhi in range(2):
                    col = pl.multiple_of((zhi * 4 + to) * 256 + kv * HD, HD)
                    block = self.pool16[half][slot, :, pl.ds(col, HD)]
                    if k == 0:
                        self.recv_y[ch][self.y * (2 * CAP_Y) + n * 2 + zhi] = block
                    else:
                        self.send_y[ch, k - 1, n * 2 + zhi] = block

        self.start_hop("y", ch)

    def pack_z(self, ch):
        self.wait_hop("y", ch)

        @pl.loop(0, CAP_Z, unroll=True)
        def _(n):
            for k in range(4):
                to = (self.z + k) % 4
                block = self.recv_y[ch][self.entry(n, 1 + to % 2) * 2 + to // 2]
                if k == 0:
                    self.recv_z[ch][self.z * CAP_Z + n] = block
                else:
                    self.send_z[ch, k - 1, n] = block

        self.start_hop("z", ch)

    def pack_x(self, ch):
        self.wait_hop("z", ch)

        @pl.loop(0, CAP_X, unroll=True)
        def _(n):
            for k in range(4):
                to = (self.x + k) % 4
                block = self.recv_z[ch][self.entry(n, 3 + to)]
                if k == 0:
                    self.recv_x[ch][self.x * CAP_X + n] = block
                else:
                    self.send_x[ch, k - 1, n] = block

        self.start_hop("x", ch)

    def last(self, ch, lane):
        return self.remote(
            self.send_c.at[ch],
            self.kv.at[ch, pl.ds(lane * CTXP * ROWS, CTXP * ROWS)],
            self.sems["last_send"].at[ch],
            self.sems["last_recv"].at[ch],
            self.peer("c", 1),
        )

    def pack_c(self, ch):
        self.wait_hop("x", ch)

        @pl.loop(0, CTXP, unroll=True)
        def _(n):
            rows = pl.ds(pl.multiple_of(n * ROWS, ROWS), ROWS)
            own = pl.ds(pl.multiple_of((self.core * CTXP + n) * ROWS, ROWS), ROWS)
            self.kv[ch, own, :] = self.recv_x[ch][self.entry(n, 7 + self.core)]
            self.send_c[ch, rows, :] = self.recv_x[ch][self.entry(n, 8 - self.core)]

        self.last(ch, self.core).start()

    def wait_last(self, ch):
        self.last(ch, 1 - self.core).wait_recv()

    def new_hop(self, k, source):
        return self.remote(
            self.send_n.at[k - 1],
            self.recv_n.at[source],
            self.sems["new_send"].at[k - 1],
            self.sems["new_recv"].at[k - 1],
            self.peer("x", k),
        )

    def start_new(self, dest):
        self.span_pad[0:6] = self.span[...].reshape(6, PAGE, 256)
        self.span_pad[6] = jnp.zeros((PAGE, 256), jnp.bfloat16)
        for k in range(4):
            for j in range(4):
                column = ((self.x + k) % 4) * 4 + j
                page = jnp.int32(6)
                for p in range(6):
                    page = jnp.where(dest[p] == column, p, page)
                if k == 0:
                    self.recv_n[self.x, j] = self.span_pad[page]
                else:
                    self.send_n[k - 1, j] = self.span_pad[page]
        for k in (1, 2, 3):
            self.new_hop(k, self.x).start()

    def new_page(self, n, owner_t, owner_d, core, t):
        cols = pl.ds(pl.multiple_of(t * 256, 256), 256)
        return self.remote(
            self.recv_n.at[n // 4, n % 4],
            self.pages.at[core, :, cols],
            self.sems["page_send"].at[n],
            self.sems["page_recv"].at[core * 8 + t],
            {"tp": owner_t, "dec": owner_d},
        )

    def own_page(self, n):
        cols = pl.ds(pl.multiple_of(self.t * 256, 256), 256)
        return pltpu.make_async_copy(
            self.recv_n.at[n // 4, n % 4], self.pages.at[self.core, :, cols], self.sems["page_send"].at[n]
        )

    def each_page(self, mine, other):
        @pl.loop(0, 16)
        def _(n):
            owner_t, owner_d = (n // 4) * 2 + self.z % 2, self.x * 4 + n % 4
            own = (owner_t == self.t) & (owner_d == self.d)

            @pl.when(own)
            def _():
                mine(self.own_page(n))

            @pl.when(jnp.logical_not(own))
            def _():
                other(self.new_page(n, owner_t, owner_d, self.core, self.t))

    def forward_new(self):
        for k in (1, 2, 3):
            self.new_hop(k, (self.x + 4 - k) % 4).wait_recv()
        self.each_page(lambda copy: copy.start(), lambda copy: copy.start())

    def wait_new(self):
        self.each_page(lambda copy: copy.wait(), lambda copy: copy.wait_send())
        block = (self.t // 2) * 4 + self.d % 4

        @pl.loop(0, 16)
        def _(n):
            sender_t, core = n // 2, n % 2
            sender_d = self.x * 4 + (self.t % 2) * 2 + core

            @pl.when((sender_t != self.t) | (sender_d != self.d))
            def _():
                self.new_page(block, sender_t, sender_d, core, sender_t).wait_recv()

        for k in (1, 2, 3):
            self.new_hop(k, self.x).wait_send()

    def wait_sends(self):
        for k in range(1, 16):
            self.row_copy(k, self.d).wait_send()
        for half in range(QUARTERS):
            self.pool_pair(half, self.core).wait_send()
        for ch in range(NCH):
            for axis in "yzx":
                for k in (1, 2, 3):
                    self.hop(axis, ch, k, getattr(self, axis)).wait_send()
            self.last(ch, self.core).wait_send()


def exchange_scratch():
    bf16, vmem, dma = jnp.bfloat16, pltpu.VMEM, pltpu.SemaphoreType.DMA
    unit = (ROWS, HD)
    refs = [
        [vmem((16, ROWS, 2048), bf16) for _ in range(QUARTERS)],
        vmem((NCH, 3, 2 * CAP_Y) + unit, bf16),
        [vmem((8 * CAP_Y,) + unit, bf16) for _ in range(NCH)],
        vmem((NCH, 3, CAP_Z) + unit, bf16),
        [vmem((4 * CAP_Z,) + unit, bf16) for _ in range(NCH)],
        vmem((NCH, 3, CAP_X) + unit, bf16),
        [vmem((4 * CAP_X,) + unit, bf16) for _ in range(NCH)],
        vmem((NCH, CTXP * ROWS, HD), bf16),
        vmem((7, PAGE, 256), bf16),
        vmem((3, 4, PAGE, 256), bf16),
        vmem((4, 4, PAGE, 256), bf16),
        vmem((8, 128), jnp.int32),
        vmem((16, 8, 128), jnp.int32),
    ]
    sems = {
        "own": dma((QUARTERS,)), "pair_send": dma((QUARTERS,)), "pair_recv": dma((QUARTERS,)), "send": dma((3, NCH, 3)),
        "recv": dma((3, NCH, 3)), "last_send": dma((NCH,)), "last_recv": dma((NCH,)), "new_send": dma((3,)),
        "new_recv": dma((3,)), "page_send": dma((16,)), "page_recv": dma((16,)),
        "row_send": dma((16,)), "row_recv": dma((16,)), "table": dma((1,)),
    }
    return refs, sems


ONES = 16


class Attention:
    def __init__(self, q, s, mx, m, acc):
        self.q, self.s, self.mx, self.m, self.acc = q, s, mx, m, acc
        self.span = q.shape[0]
        self.heads = q.shape[1] // HD
        self.coef = LOG2E / math.sqrt(HD)

    def columns(self, n):
        return pl.ds(pl.multiple_of(n * HD, HD), HD)

    def product(self, k, q):
        return lax.dot_general(k, q, (((1,), (1,)), ((), ())), preferred_element_type=jnp.float32)

    def fold(self, part):
        return jnp.max(part.reshape(part.shape[0] // 8, 8, part.shape[1]), axis=0)

    def weights(self, part, top):
        return jnp.exp2((part - top) * self.coef).astype(jnp.bfloat16)

    def score(self, n, slot, k):
        q = self.q[:, self.columns(n)]
        top = None
        for start in range(0, BLOCK, KEYS):
            part = self.product(k[start : start + KEYS], q)
            self.s[slot][start : start + KEYS, :] = part
            piece = self.fold(part)
            top = piece if top is None else jnp.maximum(top, piece)
        self.mx[slot][...] = top

    def mix(self, n, slot, vt):
        top = jnp.max(self.mx[slot][...], axis=0, keepdims=True)
        old = self.m[n, 0:1, :]
        top = jnp.maximum(old, top)
        fade = jnp.exp2((old - top) * self.coef)
        self.m[n] = jnp.broadcast_to(top, (8, self.span))
        weights = [self.weights(self.s[slot][start : start + KEYS, :], top) for start in range(0, BLOCK, KEYS)]
        mixed = jnp.dot(vt[...], jnp.concatenate(weights, axis=0), preferred_element_type=jnp.float32)
        self.acc[n] = self.acc[n] * fade + mixed

    def score_span(self, n, slot, k):
        q = self.q[:, self.columns(n)]
        shape = (KEYS, KEYS)
        diagonal = lax.broadcasted_iota(jnp.int32, shape, 0) <= lax.broadcasted_iota(jnp.int32, shape, 1)
        top = None
        for start in range(0, self.span, KEYS):
            part = self.product(k[start : start + KEYS], q[start:])
            edge = jnp.where(diagonal, part[:, :KEYS], NEG)
            part = edge if start + KEYS == self.span else jnp.concatenate([edge, part[:, KEYS:]], axis=1)
            self.s[slot][start : start + KEYS, start:] = part
            piece = self.fold(part)
            if start:
                piece = jnp.concatenate([top[:, :start], jnp.maximum(top[:, start:], piece)], axis=1)
            top = piece
        self.mx[slot][...] = top

    def mix_span(self, n, slot, vt):
        top = jnp.max(self.mx[slot][...], axis=0, keepdims=True)
        self.m[n] = jnp.broadcast_to(top, (8, self.span))
        for start in range(0, self.span, KEYS):
            weights = self.weights(self.s[slot][start : start + KEYS, start:], top[:, start:])
            mixed = jnp.dot(vt[:, start : start + KEYS], weights, preferred_element_type=jnp.float32)
            if start:
                self.acc[n, :, start:] += mixed
            else:
                self.acc[n] = mixed

    def two_heads(self, pair, score, mix, k, v):
        n = pair * 2
        score(n + 1, 1, k)
        mix(n, 0, v)
        score(jnp.minimum(n + 2, self.heads - 1), 0, k)
        mix(n + 1, 1, v)

    def result(self, n):
        acc = self.acc[n]
        return jnp.transpose((acc[:HD] / acc[HD : HD + 1]).astype(jnp.bfloat16))


KEYS = 256


def attention_scratch(span, width):
    heads = width // HD
    f32 = jnp.float32
    return [
        [pltpu.VMEM((BLOCK, span), f32) for _ in range(2)],
        [pltpu.VMEM((8, span), f32) for _ in range(2)],
        pltpu.VMEM((heads, 8, span), f32),
        pltpu.VMEM((heads, HD + ONES, span), f32),
    ]


def span_values(span_ref, v_span):
    v_span[:HD, :] = jnp.transpose(span_ref[:, HD:])
    v_span[HD:, :] = jnp.ones((ONES, v_span.shape[1]), jnp.bfloat16)


def block_values(values, live, v_block):
    key = lax.broadcasted_iota(jnp.int32, (HD, BLOCK), 1) % (CTXP * ROWS)
    used = key < live * ROWS
    v_block[:HD, :] = jnp.where(used, jnp.transpose(values), 0).astype(jnp.bfloat16)
    v_block[HD:, :] = jnp.where(used[:ONES], 1.0, 0.0).astype(jnp.bfloat16)


FORWARD = 9


def fused_kernel(
    dest, slots, flags, q, span, pool, out, pages, over, kv, v_span, v_block, done, done_sem, tab, tab_made, attn, refs, sems
):
    ex = Exchange(tab, pool, span, pages, kv, refs, sems)
    at = Attention(q, *attn)
    pairs = at.heads // 2
    first_block = 10

    for quarter in range(QUARTERS):
        ex.pool_own(quarter).start()
    ex.row[...] = jnp.broadcast_to(jnp.where(flags[...] == 1, slots[...], -1), ex.row.shape)
    ex.barrier()
    ex.start_rows()
    ex.start_pool()
    ex.start_new(dest)
    span_values(span, v_span)
    at.score_span(0, 0, span[:, :HD])
    table, most = route(ex.wait_rows())
    over[0] = jnp.maximum(most, 0)
    tab_made[...] = table
    to_scalars = pltpu.make_async_copy(tab_made, tab, sems["table"].at[0])
    to_scalars.start()
    to_scalars.wait()
    ex.wait_pool(0)
    ex.pack_y(0)
    ex.pack_y(1)

    def write_out(pair):
        cols = pl.ds(pl.multiple_of(pair * 2 * HD, 2 * HD), 2 * HD)
        return pltpu.make_async_copy(done.at[:, cols], out.at[:, cols], done_sem.at[pair])

    @pl.loop(0, first_block + QUARTERS * pairs)
    def _(step):
        for i in range(1, NCH + 3):

            @pl.when(step == 2 * i)
            def _(i=i):
                if i - 1 < NCH:
                    ex.pack_z(i - 1)
                if i + 1 < NCH:
                    if i % 2 == 1:
                        ex.wait_pool((i + 1) // 2)
                    ex.pack_y(i + 1)
                if i == FORWARD:
                    ex.forward_new()

            @pl.when(step == 2 * i + 1)
            def _(i=i):
                if 0 <= i - 2 < NCH:
                    ex.pack_x(i - 2)
                if 0 <= i - 3 < NCH:
                    ex.pack_c(i - 3)

        @pl.when(step < pairs)
        def _():
            at.two_heads(step, at.score_span, at.mix_span, span[:, :HD], v_span)

        for b in range(QUARTERS):

            @pl.when(step == first_block + b * pairs)
            def _(b=b):
                ex.wait_last(2 * b)
                ex.wait_last(2 * b + 1)
                block_values(kv[2 * b + 1], tab[0, 9], v_block)
                at.score(0, 0, kv[2 * b])

        @pl.when(step >= first_block)
        def _():
            e = step - first_block
            at.two_heads(e % pairs, at.score, at.mix, kv[(e // pairs) * 2], v_block)

        @pl.when(step >= first_block + (QUARTERS - 1) * pairs)
        def _():
            pair = (step - first_block) % pairs
            for n in range(2):
                done[:, at.columns(pair * 2 + n)] = at.result(pair * 2 + n)
            write_out(pair).start()

    for pair in range(pairs):
        write_out(pair).wait()
    ex.wait_new()
    ex.wait_sends()


VMEM_MIB = 56


def fused(dest, slots, flags, queries, span, pool):
    refs, sems = exchange_scratch()
    vmem = pl.BlockSpec(memory_space=pltpu.VMEM)
    smem = pl.BlockSpec(memory_space=pltpu.SMEM)
    hbm = pl.BlockSpec(memory_space=pl.ANY)
    bf16 = jnp.bfloat16
    rows, width = queries.shape
    return pl.pallas_call(
        fused_kernel,
        out_shape=[
            jax.ShapeDtypeStruct((rows, width), bf16),
            jax.ShapeDtypeStruct((2, PAGE, 2048), bf16),
            jax.ShapeDtypeStruct((1,), jnp.int32),
        ],
        in_specs=[smem, vmem, vmem, vmem, vmem, hbm],
        out_specs=[hbm, hbm, smem],
        scratch_shapes=[
            pltpu.VMEM((NCH, BLOCK, HD), bf16),
            pltpu.VMEM((HD + ONES, rows), bf16),
            pltpu.VMEM((HD + ONES, BLOCK), bf16),
            pltpu.VMEM((rows, width), bf16),
            pltpu.SemaphoreType.DMA((width // HD // 2,)),
            pltpu.SMEM((CTXP, 128), jnp.int32),
            pltpu.VMEM((CTXP, 128), jnp.int32),
            attention_scratch(rows, width),
            refs,
            sems,
        ],
        compiler_params=pltpu.CompilerParams(
            collective_id=1, has_side_effects=True, vmem_limit_bytes=VMEM_MIB * 1024 * 1024
        ),
    )(dest, slots, flags, queries, span, pool)


def attend_kernel(live, q, span, kv, out, v_span, v_block, attn):
    at = Attention(q, *attn)
    pairs = at.heads // 2
    span_values(span, v_span)
    at.score_span(0, 0, span[:, :HD])

    @pl.loop(0, pairs)
    def _(pair):
        at.two_heads(pair, at.score_span, at.mix_span, span[:, :HD], v_span)

    @pl.loop(0, QUARTERS)
    def _(b):
        block_values(kv[2 * b + 1], live[0], v_block)
        at.score(0, 0, kv[2 * b])

        @pl.loop(0, pairs)
        def _(pair):
            at.two_heads(pair, at.score, at.mix, kv[2 * b], v_block)

    @pl.loop(0, at.heads)
    def _(n):
        out[:, at.columns(n)] = at.result(n)


def attend(live, queries, span, kv):
    rows, width = queries.shape
    vmem = pl.BlockSpec(memory_space=pltpu.VMEM)
    smem = pl.BlockSpec(memory_space=pltpu.SMEM)
    return pl.pallas_call(
        attend_kernel,
        out_shape=jax.ShapeDtypeStruct((rows, width), jnp.bfloat16),
        in_specs=[smem, vmem, vmem, vmem],
        out_specs=vmem,
        scratch_shapes=[
            pltpu.VMEM((HD + ONES, rows), jnp.bfloat16),
            pltpu.VMEM((HD + ONES, BLOCK), jnp.bfloat16),
            attention_scratch(rows, width),
        ],
        compiler_params=pltpu.CompilerParams(vmem_limit_bytes=48 * 1024 * 1024),
    )(live, queries, span, kv)


def dense(dest, queries, span, pool, slots, flags):
    tp_size, dec_size = lax.axis_size("tp"), lax.axis_size("dec")
    devices = tp_size * dec_size
    width = span.shape[1]
    view = pool.reshape(pool.shape[0], PAGE, tp_size, width)
    source_rows = (jnp.arange(devices, dtype=jnp.int32) // dec_size)[:, None]
    axes = ("tp", "dec")
    asked = lax.all_to_all(slots, axes, split_axis=0, concat_axis=0, tiled=True)
    fetched = lax.all_to_all(view[asked, :, source_rows], axes, split_axis=0, concat_axis=0, tiled=True)
    live_index, live_count = compact_slots(flags)
    live_index = jnp.where(jnp.arange(CTXP) < live_count, live_index, live_index[0])
    cached = fetched.reshape(devices, PAGE, width)[live_index]
    cached = cached.reshape(CTXP, 2, QUARTERS, ROWS, 2, HD)
    cached = jnp.transpose(cached, (2, 4, 1, 0, 3, 5)).reshape(NCH, BLOCK, HD)
    new_pages = span.reshape(-1, PAGE, width)
    chosen = (dest[None, :] == jnp.arange(dec_size, dtype=jnp.int32)[:, None]).astype(jnp.bfloat16)
    outgoing = jnp.einsum("dp,pkc->dkc", chosen, new_pages, preferred_element_type=jnp.float32).astype(jnp.bfloat16)
    placed = lax.all_to_all(outgoing, "dec", split_axis=0, concat_axis=0, tiled=True)
    placed = lax.all_to_all(placed, "tp", split_axis=0, concat_axis=2, tiled=True)
    return (attend(live_count.reshape(1), queries, span, cached), placed)


def body(queries, span_kv, page_pool, cache_slot, cache_live, span_dest):
    dest, q, span = span_dest[0], queries[0], span_kv[0]
    attn_out, placed, over = fused(dest, cache_slot.reshape(1, -1), cache_live.reshape(1, -1), q, span, page_pool)
    attn_out, placed = lax.cond(
        over[0] > 0,
        lambda attn, pages, *a: dense(*a),
        lambda attn, pages, *a: (attn, pages),
        attn_out, placed, dest, q, span, page_pool, cache_slot[0], cache_live[0],
    )
    return (attn_out[None], placed)


def solution(mesh):
    in_specs = (
        P("dec", None, "tp"),
        P("dec", None, "tp"),
        P(("tp", "dec"), None, None),
        P("dec", None, None),
        P("dec", None, None),
        P("dec", None),
    )
    out_specs = (P("dec", None, "tp"), P(("tp", "dec"), None, None))
    return jax.shard_map(body, mesh=mesh, in_specs=in_specs, out_specs=out_specs, check_vma=False)
```

```python
import functools
import math

import jax
import jax.numpy as jnp
from jax import lax
from jax.experimental import pallas as pl
from jax.experimental.pallas import tpu as pltpu
from jax.sharding import PartitionSpec as P

HD = 128
PAGE = 128
CTXP = 32
LOG2E = 1.4426950408889634
NEG = -1e30


def compact_slots(live_flags):
    flat_live = live_flags.reshape(-1)
    live_rank = jnp.cumsum(flat_live) - 1
    slot_ids = jnp.arange(flat_live.shape[0], dtype=jnp.int32)
    targets = jnp.arange(CTXP, dtype=jnp.int32)
    select_table = (flat_live[None, :] == 1) & (live_rank[None, :] == targets[:, None])
    live_index = jnp.sum(jnp.where(select_table, slot_ids[None, :], 0), axis=1)
    return (live_index, jnp.sum(flat_live))


MESH = pl.DeviceIdType.MESH
CAP_Y, CAP_Z, CAP_X = 13, 25, 26


def coords():
    t, d = lax.axis_index("tp"), lax.axis_index("dec")
    return t, d, t % 4, (t // 4) * 2 + (d // 2) % 2, d // 4, d % 2


def flag(cond, dtype=jnp.float32):
    return jnp.where(cond, 1.0, 0.0).astype(dtype)


def route(packed):
    t, d, y, z, x, core = coords()
    bf16, f32 = jnp.bfloat16, jnp.float32
    oi = lax.broadcasted_iota(jnp.int32, (128, 128), 0)
    oj = lax.broadcasted_iota(jnp.int32, (128, 128), 1)
    gi = lax.broadcasted_iota(jnp.int32, (16, 16), 0)
    gj = lax.broadcasted_iota(jnp.int32, (16, 16), 1)
    owner_groups = (lambda o: o >> 1, lambda o: o & 0x4E, lambda o: o & 0x0C, lambda o: o & 0)
    row_groups = (lambda g: g & 0, lambda g: g >> 3, lambda g: g & 14, lambda g: g)

    o = lax.broadcasted_iota(jnp.int32, (16, 128), 1)
    g = lax.broadcasted_iota(jnp.int32, (16, 128), 0)
    g_zlo = (g >> 1) & 1
    asked = [
        [jnp.max(flag((packed == s) & (g_zlo == b)), axis=0, keepdims=True) for s in range(8)] for b in range(2)
    ]
    by_slot = [jnp.maximum(p, q) for p, q in zip(*asked)]
    wants = (
        jnp.concatenate(by_slot + [jnp.zeros((8, 128), f32)], axis=0).astype(bf16),
        jnp.concatenate(asked[0] + asked[1], axis=0).astype(bf16),
        flag(packed >= 0, bf16),
        flag(packed >= 0, bf16),
    )

    ranks, counts = [], []
    for want, owner, row in zip(wants, owner_groups, row_groups):
        same = owner(oi) == owner(oj)
        before = jnp.dot(want, flag(same & (oi < oj), bf16), preferred_element_type=f32)
        total = jnp.dot(want, flag(same, bf16), preferred_element_type=f32)
        side = row(gi) == row(gj)
        rank = jnp.dot(flag(side, bf16), before.astype(bf16), preferred_element_type=f32)
        rank += jnp.dot(flag(side & (gj < gi), bf16), want, preferred_element_type=f32)
        ranks.append(rank.astype(jnp.int32))
        counts.append(jnp.dot(flag(side, bf16), total.astype(bf16), preferred_element_type=f32).astype(jnp.int32))

    rank_y = jnp.concatenate([ranks[0][0:8], ranks[0][0:8]], axis=0)
    rank_z = jnp.zeros((16, 128), jnp.int32)
    for s in range(8):
        row = jnp.where(g_zlo == 1, ranks[1][8 + s : 9 + s, :], ranks[1][s : s + 1, :])
        rank_z = jnp.where(packed == s, row, rank_z)

    o_x, o_y, o_z, o_c = (o >> 2) & 3, (o >> 4) & 3, ((o >> 6) << 1) | ((o >> 1) & 1), o & 1
    zlo = z % 2
    places = (
        (o_x == x) & (o_y == y) & (o_z == z),
        (o_x == x) & (o_z == z),
        (o_x == x) & (g_zlo == zlo),
        (g >> 1) == x * 2 + zlo,
    )
    mine = [(want.astype(f32) > 0) & place for want, place in zip(wants, places)]
    values = (
        o_c * 8 + g,
        o_y * CAP_Y + jnp.minimum(rank_y, CAP_Y - 1),
        o_z * CAP_Z + jnp.minimum(rank_z, CAP_Z - 1),
        o_x * CAP_X + jnp.minimum(ranks[2], CAP_X - 1),
    )
    lists = (
        (range(8),),
        (range(8), range(8, 16)),
        [[r for r in range(16) if r >> 2 == b] for b in range(4)],
        [[r for r in range(16) if r & 1 == b] for b in range(2)],
    )
    place = lax.broadcasted_iota(jnp.int32, (CTXP, 128), 0)
    lane = lax.broadcasted_iota(jnp.int32, (CTXP, 128), 1)
    table = jnp.zeros((CTXP, 128), jnp.int32)
    column = 0
    for stage in range(4):
        rank = jnp.where(mine[stage], ranks[stage], -1)
        for rows in lists[stage]:
            found = jnp.zeros((CTXP, 128), jnp.int32)
            for r in rows:
                found += jnp.where(rank[r : r + 1, :] == place, values[stage][r : r + 1, :], 0)
            found = jnp.sum(found.astype(f32), axis=1, keepdims=True).astype(jnp.int32)
            table = jnp.where(lane == column, found, table)
            column += 1
    live = packed >= 0
    held = jnp.sum(flag(live & (g == d))).astype(jnp.int32)
    over = jnp.maximum(
        jnp.maximum(jnp.max(counts[0]) - CAP_Y, jnp.max(counts[1]) - CAP_Z), jnp.max(counts[2]) - CAP_X
    )
    for c in range(2):
        size = jnp.sum(flag(live & (g == (d // 2) * 2 + c))).astype(jnp.int32)
        table = jnp.where((lane == 7 + c) & (place >= size), table[0:1, :], table)
    table = jnp.where(lane == 9, held, table)
    sizes = jnp.where(lane < 1, 16, jnp.where(lane < 3, 4 * CAP_Y, jnp.where(lane < 7, 4 * CAP_Z, 4 * CAP_X)))
    return jnp.minimum(jnp.maximum(table, 0), sizes - 1), over


QUARTERS = 4
NCH = 2 * QUARTERS
ROWS = 16
BLOCK = 2 * CTXP * ROWS


class Exchange:
    def __init__(self, tab, pool, span, pages, kv, refs, sems):
        self.tab, self.pool, self.span, self.pages, self.kv = tab, pool, span, pages, kv
        (self.pool16, self.send_y, self.recv_y, self.send_z, self.recv_z, self.send_x, self.recv_x, self.send_c,
         self.span_pad, self.send_n, self.recv_n, self.row, self.rows) = refs
        self.sems = sems
        self.t, self.d, self.y, self.z, self.x, self.core = coords()

    def barrier(self):
        t, d = self.t, self.d
        sem = pltpu.get_barrier_semaphore()
        for device in [self.peer("c", 1)] + [self.peer(a, k) for a in "yzx" for k in (1, 2, 3)]:
            pl.semaphore_signal(sem, inc=1, device_id=device, device_id_type=MESH)

        for k in range(1, 16):
            pl.semaphore_signal(sem, inc=1, device_id={"dec": (d + k) % 16}, device_id_type=MESH)
        zlo = self.z % 2

        @pl.loop(0, 16)
        def _(n):
            device = {"tp": n // 2, "dec": self.x * 4 + (t % 2) * 2 + n % 2}

            @pl.when((n // 2 != t) | (device["dec"] != d))
            def _():
                pl.semaphore_signal(sem, inc=1, device_id=device, device_id_type=MESH)

        pl.semaphore_wait(sem, 41 - jnp.where(t % 2 == zlo, 1, 0))

    def entry(self, place, column):
        return self.tab[place, column]

    def peer(self, axis, k):
        t, d, y, z, x, c = self.t, self.d, self.y, self.z, self.x, self.core
        if axis == "c":
            c = 1 - c
        elif axis == "y":
            y = (y + k) % 4
        elif axis == "z":
            z = (z + k) % 4
        else:
            x = (x + k) % 4
        return {"tp": (z // 2) * 4 + y, "dec": x * 4 + (z % 2) * 2 + c}

    def remote(self, src, dst, send_sem, recv_sem, device):
        return pltpu.make_async_remote_copy(
            src_ref=src, dst_ref=dst, send_sem=send_sem, recv_sem=recv_sem, device_id=device, device_id_type=MESH
        )

    def row_copy(self, k, slot):
        return self.remote(
            self.row,
            self.rows.at[slot],
            self.sems["row_send"].at[k],
            self.sems["row_recv"].at[slot],
            {"dec": (self.d + k) % 16},
        )

    def start_rows(self):
        for k in range(1, 16):
            self.row_copy(k, self.d).start()
        self.rows[self.d] = self.row[...]

    def wait_rows(self):
        for k in range(1, 16):
            self.row_copy(k, (self.d + 16 - k) % 16).wait_recv()
        return jnp.concatenate([self.rows[g] for g in range(16)], axis=0)

    def pool_own(self, half):
        rows = pl.ds(self.core * 64 + half * ROWS, ROWS)
        return pltpu.make_async_copy(
            self.pool.at[:, rows, :], self.pool16[half].at[pl.ds(self.core * 8, 8)], self.sems["own"].at[half]
        )

    def pool_pair(self, half, into):
        rows = pl.ds((1 - self.core) * 64 + half * ROWS, ROWS)
        return self.remote(
            self.pool.at[:, rows, :],
            self.pool16[half].at[pl.ds(into * 8, 8)],
            self.sems["pair_send"].at[half],
            self.sems["pair_recv"].at[half],
            self.peer("c", 1),
        )

    def start_pool(self):
        for half in range(QUARTERS):
            self.pool_pair(half, self.core).start()

    def wait_pool(self, half):
        self.pool_own(half).wait()
        self.pool_pair(half, 1 - self.core).wait_recv()

    def hop(self, axis, ch, k, source):
        send, recv, stage = {
            "y": (self.send_y, self.recv_y, 0), "z": (self.send_z, self.recv_z, 1), "x": (self.send_x, self.recv_x, 2),
        }[axis]
        units = send.shape[2]
        return self.remote(
            send.at[ch, k - 1],
            recv[ch].at[pl.ds(source * units, units)],
            self.sems["send"].at[stage, ch, k - 1],
            self.sems["recv"].at[stage, ch, k - 1],
            self.peer(axis, k),
        )

    def start_hop(self, axis, ch):
        for k in (1, 2, 3):
            self.hop(axis, ch, k, getattr(self, axis)).start()

    def wait_hop(self, axis, ch):
        me = getattr(self, axis)
        for k in (1, 2, 3):
            self.hop(axis, ch, k, (me + 4 - k) % 4).wait_recv()

    def pack_y(self, ch):
        half, kv = ch // 2, ch % 2

        @pl.loop(0, CAP_Y, unroll=True)
        def _(n):
            slot = self.entry(n, 0)
            for k in range(4):
                to = (self.y + k) % 4
                for zhi in range(2):
                    col = pl.multiple_of((zhi * 4 + to) * 256 + kv * HD, HD)
                    block = self.pool16[half][slot, :, pl.ds(col, HD)]
                    if k == 0:
                        self.recv_y[ch][self.y * (2 * CAP_Y) + n * 2 + zhi] = block
                    else:
                        self.send_y[ch, k - 1, n * 2 + zhi] = block

        self.start_hop("y", ch)

    def pack_z(self, ch):
        self.wait_hop("y", ch)

        @pl.loop(0, CAP_Z, unroll=True)
        def _(n):
            for k in range(4):
                to = (self.z + k) % 4
                block = self.recv_y[ch][self.entry(n, 1 + to % 2) * 2 + to // 2]
                if k == 0:
                    self.recv_z[ch][self.z * CAP_Z + n] = block
                else:
                    self.send_z[ch, k - 1, n] = block

        self.start_hop("z", ch)

    def pack_x(self, ch):
        self.wait_hop("z", ch)

        @pl.loop(0, CAP_X, unroll=True)
        def _(n):
            for k in range(4):
                to = (self.x + k) % 4
                block = self.recv_z[ch][self.entry(n, 3 + to)]
                if k == 0:
                    self.recv_x[ch][self.x * CAP_X + n] = block
                else:
                    self.send_x[ch, k - 1, n] = block

        self.start_hop("x", ch)

    def last(self, ch, lane):
        return self.remote(
            self.send_c.at[ch],
            self.kv.at[ch, pl.ds(lane * CTXP * ROWS, CTXP * ROWS)],
            self.sems["last_send"].at[ch],
            self.sems["last_recv"].at[ch],
            self.peer("c", 1),
        )

    def pack_c(self, ch):
        self.wait_hop("x", ch)

        @pl.loop(0, CTXP, unroll=True)
        def _(n):
            rows = pl.ds(pl.multiple_of(n * ROWS, ROWS), ROWS)
            own = pl.ds(pl.multiple_of((self.core * CTXP + n) * ROWS, ROWS), ROWS)
            self.kv[ch, own, :] = self.recv_x[ch][self.entry(n, 7 + self.core)]
            self.send_c[ch, rows, :] = self.recv_x[ch][self.entry(n, 8 - self.core)]

        self.last(ch, self.core).start()

    def wait_last(self, ch):
        self.last(ch, 1 - self.core).wait_recv()

    def new_hop(self, k, source):
        return self.remote(
            self.send_n.at[k - 1],
            self.recv_n.at[source],
            self.sems["new_send"].at[k - 1],
            self.sems["new_recv"].at[k - 1],
            self.peer("x", k),
        )

    def start_new(self, dest):
        self.span_pad[0:6] = self.span[...].reshape(6, PAGE, 256)
        self.span_pad[6] = jnp.zeros((PAGE, 256), jnp.bfloat16)
        for k in range(4):
            for j in range(4):
                column = ((self.x + k) % 4) * 4 + j
                page = jnp.int32(6)
                for p in range(6):
                    page = jnp.where(dest[p] == column, p, page)
                if k == 0:
                    self.recv_n[self.x, j] = self.span_pad[page]
                else:
                    self.send_n[k - 1, j] = self.span_pad[page]
        for k in (1, 2, 3):
            self.new_hop(k, self.x).start()

    def new_page(self, n, owner_t, owner_d, core, t):
        cols = pl.ds(pl.multiple_of(t * 256, 256), 256)
        return self.remote(
            self.recv_n.at[n // 4, n % 4],
            self.pages.at[core, :, cols],
            self.sems["page_send"].at[n],
            self.sems["page_recv"].at[core * 8 + t],
            {"tp": owner_t, "dec": owner_d},
        )

    def own_page(self, n):
        cols = pl.ds(pl.multiple_of(self.t * 256, 256), 256)
        return pltpu.make_async_copy(
            self.recv_n.at[n // 4, n % 4], self.pages.at[self.core, :, cols], self.sems["page_send"].at[n]
        )

    def each_page(self, mine, other):
        @pl.loop(0, 16)
        def _(n):
            owner_t, owner_d = (n // 4) * 2 + self.z % 2, self.x * 4 + n % 4
            own = (owner_t == self.t) & (owner_d == self.d)

            @pl.when(own)
            def _():
                mine(self.own_page(n))

            @pl.when(jnp.logical_not(own))
            def _():
                other(self.new_page(n, owner_t, owner_d, self.core, self.t))

    def forward_new(self):
        for k in (1, 2, 3):
            self.new_hop(k, (self.x + 4 - k) % 4).wait_recv()
        self.each_page(lambda copy: copy.start(), lambda copy: copy.start())

    def wait_new(self):
        self.each_page(lambda copy: copy.wait(), lambda copy: copy.wait_send())
        block = (self.t // 2) * 4 + self.d % 4

        @pl.loop(0, 16)
        def _(n):
            sender_t, core = n // 2, n % 2
            sender_d = self.x * 4 + (self.t % 2) * 2 + core

            @pl.when((sender_t != self.t) | (sender_d != self.d))
            def _():
                self.new_page(block, sender_t, sender_d, core, sender_t).wait_recv()

        for k in (1, 2, 3):
            self.new_hop(k, self.x).wait_send()

    def wait_sends(self):
        for k in range(1, 16):
            self.row_copy(k, self.d).wait_send()
        for half in range(QUARTERS):
            self.pool_pair(half, self.core).wait_send()
        for ch in range(NCH):
            for axis in "yzx":
                for k in (1, 2, 3):
                    self.hop(axis, ch, k, getattr(self, axis)).wait_send()
            self.last(ch, self.core).wait_send()


def exchange_scratch():
    bf16, vmem, dma = jnp.bfloat16, pltpu.VMEM, pltpu.SemaphoreType.DMA
    unit = (ROWS, HD)
    refs = [
        [vmem((16, ROWS, 2048), bf16) for _ in range(QUARTERS)],
        vmem((NCH, 3, 2 * CAP_Y) + unit, bf16),
        [vmem((8 * CAP_Y,) + unit, bf16) for _ in range(NCH)],
        vmem((NCH, 3, CAP_Z) + unit, bf16),
        [vmem((4 * CAP_Z,) + unit, bf16) for _ in range(NCH)],
        vmem((NCH, 3, CAP_X) + unit, bf16),
        [vmem((4 * CAP_X,) + unit, bf16) for _ in range(NCH)],
        vmem((NCH, CTXP * ROWS, HD), bf16),
        vmem((7, PAGE, 256), bf16),
        vmem((3, 4, PAGE, 256), bf16),
        vmem((4, 4, PAGE, 256), bf16),
        vmem((1, 128), jnp.int32),
        vmem((16, 1, 128), jnp.int32),
    ]
    sems = {
        "own": dma((QUARTERS,)), "pair_send": dma((QUARTERS,)), "pair_recv": dma((QUARTERS,)), "send": dma((3, NCH, 3)),
        "recv": dma((3, NCH, 3)), "last_send": dma((NCH,)), "last_recv": dma((NCH,)), "new_send": dma((3,)),
        "new_recv": dma((3,)), "page_send": dma((16,)), "page_recv": dma((16,)),
        "row_send": dma((16,)), "row_recv": dma((16,)), "table": dma((1,)),
    }
    return refs, sems


ONES = 16


class Attention:
    def __init__(self, q, s, mx, m, acc):
        self.q, self.s, self.mx, self.m, self.acc = q, s, mx, m, acc
        self.span = q.shape[0]
        self.heads = q.shape[1] // HD
        self.coef = LOG2E / math.sqrt(HD)

    def columns(self, n):
        return pl.ds(pl.multiple_of(n * HD, HD), HD)

    def product(self, k, q):
        return lax.dot_general(k, q, (((1,), (1,)), ((), ())), preferred_element_type=jnp.float32)

    def fold(self, part):
        return jnp.max(part.reshape(part.shape[0] // 8, 8, part.shape[1]), axis=0)

    def weights(self, part, top):
        return jnp.exp2((part - top) * self.coef).astype(jnp.bfloat16)

    def score(self, n, slot, k):
        q = self.q[:, self.columns(n)]
        top = None
        for start in range(0, BLOCK, KEYS):
            part = self.product(k[start : start + KEYS], q)
            self.s[slot][start : start + KEYS, :] = part
            piece = self.fold(part)
            top = piece if top is None else jnp.maximum(top, piece)
        self.mx[slot][...] = top

    def mix(self, n, slot, vt):
        top = jnp.max(self.mx[slot][...], axis=0, keepdims=True)
        old = self.m[n, 0:1, :]
        top = jnp.maximum(old, top)
        fade = jnp.exp2((old - top) * self.coef)
        self.m[n] = jnp.broadcast_to(top, (8, self.span))
        weights = [self.weights(self.s[slot][start : start + KEYS, :], top) for start in range(0, BLOCK, KEYS)]
        mixed = jnp.dot(vt[...], jnp.concatenate(weights, axis=0), preferred_element_type=jnp.float32)
        self.acc[n] = self.acc[n] * fade + mixed

    def score_span(self, n, slot, k):
        q = self.q[:, self.columns(n)]
        shape = (KEYS, KEYS)
        diagonal = lax.broadcasted_iota(jnp.int32, shape, 0) <= lax.broadcasted_iota(jnp.int32, shape, 1)
        top = None
        for start in range(0, self.span, KEYS):
            part = self.product(k[start : start + KEYS], q[start:])
            edge = jnp.where(diagonal, part[:, :KEYS], NEG)
            part = edge if start + KEYS == self.span else jnp.concatenate([edge, part[:, KEYS:]], axis=1)
            self.s[slot][start : start + KEYS, start:] = part
            piece = self.fold(part)
            if start:
                piece = jnp.concatenate([top[:, :start], jnp.maximum(top[:, start:], piece)], axis=1)
            top = piece
        self.mx[slot][...] = top

    def mix_span(self, n, slot, vt):
        top = jnp.max(self.mx[slot][...], axis=0, keepdims=True)
        self.m[n] = jnp.broadcast_to(top, (8, self.span))
        for start in range(0, self.span, KEYS):
            weights = self.weights(self.s[slot][start : start + KEYS, start:], top[:, start:])
            mixed = jnp.dot(vt[:, start : start + KEYS], weights, preferred_element_type=jnp.float32)
            if start:
                self.acc[n, :, start:] += mixed
            else:
                self.acc[n] = mixed

    def two_heads(self, pair, score, mix, k, v):
        n = pair * 2
        score(n + 1, 1, k)
        mix(n, 0, v)
        score(jnp.minimum(n + 2, self.heads - 1), 0, k)
        mix(n + 1, 1, v)

    def result(self, n):
        acc = self.acc[n]
        return jnp.transpose((acc[:HD] / acc[HD : HD + 1]).astype(jnp.bfloat16))


KEYS = 256


def attention_scratch(span, width):
    heads = width // HD
    f32 = jnp.float32
    return [
        [pltpu.VMEM((BLOCK, span), f32) for _ in range(2)],
        [pltpu.VMEM((8, span), f32) for _ in range(2)],
        pltpu.VMEM((heads, 8, span), f32),
        pltpu.VMEM((heads, HD + ONES, span), f32),
    ]


def span_values(span_ref, v_span):
    v_span[:HD, :] = jnp.transpose(span_ref[:, HD:])
    v_span[HD:, :] = jnp.ones((ONES, v_span.shape[1]), jnp.bfloat16)


def block_values(values, live, v_block):
    key = lax.broadcasted_iota(jnp.int32, (HD, BLOCK), 1) % (CTXP * ROWS)
    used = key < live * ROWS
    v_block[:HD, :] = jnp.where(used, jnp.transpose(values), 0).astype(jnp.bfloat16)
    v_block[HD:, :] = jnp.where(used[:ONES], 1.0, 0.0).astype(jnp.bfloat16)


FORWARD = 9


def fused_kernel(
    dest, slots, flags, q, span, pool, out, pages, over, kv, v_span, v_block, done, done_sem, tab, tab_made, attn, refs, sems
):
    ex = Exchange(tab, pool, span, pages, kv, refs, sems)
    at = Attention(q, *attn)
    pairs = at.heads // 2
    first_block = 10

    for quarter in range(QUARTERS):
        ex.pool_own(quarter).start()
    ex.row[...] = jnp.where(flags[...] == 1, slots[...], -1)
    ex.barrier()
    ex.start_rows()
    ex.start_pool()
    ex.start_new(dest)
    span_values(span, v_span)
    at.score_span(0, 0, span[:, :HD])
    table, most = route(ex.wait_rows())
    over[0] = jnp.maximum(most, 0)
    tab_made[...] = table
    to_scalars = pltpu.make_async_copy(tab_made, tab, sems["table"].at[0])
    to_scalars.start()
    to_scalars.wait()
    ex.wait_pool(0)
    ex.pack_y(0)
    ex.pack_y(1)

    def write_out(pair):
        cols = pl.ds(pl.multiple_of(pair * 2 * HD, 2 * HD), 2 * HD)
        return pltpu.make_async_copy(done.at[:, cols], out.at[:, cols], done_sem.at[pair])

    @pl.loop(0, first_block + QUARTERS * pairs)
    def _(step):
        for i in range(1, NCH + 3):

            @pl.when(step == 2 * i)
            def _(i=i):
                if i - 1 < NCH:
                    ex.pack_z(i - 1)
                if i + 1 < NCH:
                    if i % 2 == 1:
                        ex.wait_pool((i + 1) // 2)
                    ex.pack_y(i + 1)
                if i == FORWARD:
                    ex.forward_new()

            @pl.when(step == 2 * i + 1)
            def _(i=i):
                if 0 <= i - 2 < NCH:
                    ex.pack_x(i - 2)
                if 0 <= i - 3 < NCH:
                    ex.pack_c(i - 3)

        @pl.when(step < pairs)
        def _():
            at.two_heads(step, at.score_span, at.mix_span, span[:, :HD], v_span)

        for b in range(QUARTERS):

            @pl.when(step == first_block + b * pairs)
            def _(b=b):
                if b == QUARTERS - 1:
                    ex.wait_sends()
                ex.wait_last(2 * b)
                ex.wait_last(2 * b + 1)
                block_values(kv[2 * b + 1], tab[0, 9], v_block)
                at.score(0, 0, kv[2 * b])

        @pl.when(step >= first_block)
        def _():
            e = step - first_block
            at.two_heads(e % pairs, at.score, at.mix, kv[(e // pairs) * 2], v_block)

        @pl.when(step >= first_block + (QUARTERS - 1) * pairs)
        def _():
            pair = (step - first_block) % pairs
            for n in range(2):
                done[:, at.columns(pair * 2 + n)] = at.result(pair * 2 + n)
            write_out(pair).start()

    for pair in range(pairs):
        write_out(pair).wait()
    ex.wait_new()


VMEM_MIB = 56


def fused(dest, slots, flags, queries, span, pool):
    refs, sems = exchange_scratch()
    vmem = pl.BlockSpec(memory_space=pltpu.VMEM)
    smem = pl.BlockSpec(memory_space=pltpu.SMEM)
    hbm = pl.BlockSpec(memory_space=pl.ANY)
    bf16 = jnp.bfloat16
    rows, width = queries.shape
    return pl.pallas_call(
        fused_kernel,
        out_shape=[
            jax.ShapeDtypeStruct((rows, width), bf16),
            jax.ShapeDtypeStruct((2, PAGE, 2048), bf16),
            jax.ShapeDtypeStruct((1,), jnp.int32),
        ],
        in_specs=[smem, vmem, vmem, vmem, vmem, hbm],
        out_specs=[hbm, hbm, smem],
        scratch_shapes=[
            pltpu.VMEM((NCH, BLOCK, HD), bf16),
            pltpu.VMEM((HD + ONES, rows), bf16),
            pltpu.VMEM((HD + ONES, BLOCK), bf16),
            pltpu.VMEM((rows, width), bf16),
            pltpu.SemaphoreType.DMA((width // HD // 2,)),
            pltpu.SMEM((CTXP, 128), jnp.int32),
            pltpu.VMEM((CTXP, 128), jnp.int32),
            attention_scratch(rows, width),
            refs,
            sems,
        ],
        compiler_params=pltpu.CompilerParams(
            collective_id=1, has_side_effects=True, vmem_limit_bytes=VMEM_MIB * 1024 * 1024
        ),
    )(dest, slots, flags, queries, span, pool)


def attend_kernel(live, q, span, kv, out, v_span, v_block, attn):
    at = Attention(q, *attn)
    pairs = at.heads // 2
    span_values(span, v_span)
    at.score_span(0, 0, span[:, :HD])

    @pl.loop(0, pairs)
    def _(pair):
        at.two_heads(pair, at.score_span, at.mix_span, span[:, :HD], v_span)

    @pl.loop(0, QUARTERS)
    def _(b):
        block_values(kv[2 * b + 1], live[0], v_block)
        at.score(0, 0, kv[2 * b])

        @pl.loop(0, pairs)
        def _(pair):
            at.two_heads(pair, at.score, at.mix, kv[2 * b], v_block)

    @pl.loop(0, at.heads)
    def _(n):
        out[:, at.columns(n)] = at.result(n)


def attend(live, queries, span, kv):
    rows, width = queries.shape
    vmem = pl.BlockSpec(memory_space=pltpu.VMEM)
    smem = pl.BlockSpec(memory_space=pltpu.SMEM)
    return pl.pallas_call(
        attend_kernel,
        out_shape=jax.ShapeDtypeStruct((rows, width), jnp.bfloat16),
        in_specs=[smem, vmem, vmem, vmem],
        out_specs=vmem,
        scratch_shapes=[
            pltpu.VMEM((HD + ONES, rows), jnp.bfloat16),
            pltpu.VMEM((HD + ONES, BLOCK), jnp.bfloat16),
            attention_scratch(rows, width),
        ],
        compiler_params=pltpu.CompilerParams(vmem_limit_bytes=48 * 1024 * 1024),
    )(live, queries, span, kv)


def dense(dest, queries, span, pool, slots, flags):
    tp_size, dec_size = lax.axis_size("tp"), lax.axis_size("dec")
    devices = tp_size * dec_size
    width = span.shape[1]
    view = pool.reshape(pool.shape[0], PAGE, tp_size, width)
    source_rows = (jnp.arange(devices, dtype=jnp.int32) // dec_size)[:, None]
    axes = ("tp", "dec")
    asked = lax.all_to_all(slots, axes, split_axis=0, concat_axis=0, tiled=True)
    fetched = lax.all_to_all(view[asked, :, source_rows], axes, split_axis=0, concat_axis=0, tiled=True)
    live_index, live_count = compact_slots(flags)
    live_index = jnp.where(jnp.arange(CTXP) < live_count, live_index, live_index[0])
    cached = fetched.reshape(devices, PAGE, width)[live_index]
    cached = cached.reshape(CTXP, 2, QUARTERS, ROWS, 2, HD)
    cached = jnp.transpose(cached, (2, 4, 1, 0, 3, 5)).reshape(NCH, BLOCK, HD)
    new_pages = span.reshape(-1, PAGE, width)
    chosen = (dest[None, :] == jnp.arange(dec_size, dtype=jnp.int32)[:, None]).astype(jnp.bfloat16)
    outgoing = jnp.einsum("dp,pkc->dkc", chosen, new_pages, preferred_element_type=jnp.float32).astype(jnp.bfloat16)
    placed = lax.all_to_all(outgoing, "dec", split_axis=0, concat_axis=0, tiled=True)
    placed = lax.all_to_all(placed, "tp", split_axis=0, concat_axis=2, tiled=True)
    return (attend(live_count.reshape(1), queries, span, cached), placed)


def body(queries, span_kv, page_pool, cache_slot, cache_live, span_dest):
    dest, q, span = span_dest[0], queries[0], span_kv[0]
    attn_out, placed, over = fused(dest, cache_slot.reshape(1, -1), cache_live.reshape(1, -1), q, span, page_pool)
    attn_out, placed = lax.cond(
        over[0] > 0,
        lambda attn, pages, *a: dense(*a),
        lambda attn, pages, *a: (attn, pages),
        attn_out, placed, dest, q, span, page_pool, cache_slot[0], cache_live[0],
    )
    return (attn_out[None], placed)


def solution(mesh):
    in_specs = (
        P("dec", None, "tp"),
        P("dec", None, "tp"),
        P(("tp", "dec"), None, None),
        P("dec", None, None),
        P("dec", None, None),
        P("dec", None),
    )
    out_specs = (P("dec", None, "tp"), P(("tp", "dec"), None, None))
    return jax.shard_map(body, mesh=mesh, in_specs=in_specs, out_specs=out_specs, check_vma=False)
```
